32 devices in a mesh: ctx: 16 (over z, y, x), head: 2 (over core).
Axes of the slice: x: 2, y: 2, z: 4, core: 2. Of those that a mesh axis runs over, the one named last changes fastest.
Arguments:
- query_raw: bfloat16 [4096, 5120], P('ctx', 'head'), may hold values from -9 to 9
- key_raw: bfloat16 [4096, 5120], P('ctx', 'head'), may hold values from -9 to 9
- values: bfloat16 [4096, 5120], P('ctx', 'head'), may hold values from -6 to 6
- out_grad: bfloat16 [4096, 5120], P('ctx', 'head'), may hold values from -128 to 128
- query_gain: float32 [5120], P('head'), may hold values from 0.25 to 1.75
- key_gain: float32 [5120], P('head'), may hold values from 0.25 to 1.75
- key_tiles: int32 [32, 4], P('ctx'), may hold values from 0 to 31, as said below
- global_ids: int32 [32], P('ctx'), may hold values from 0 to 4095, as said below
- readers: int32 [16, 16], P('ctx'), may hold values from 0 to 1, as said below
Outputs:
- query_grad: bfloat16 [4096, 5120], P('ctx', 'head')
- key_grad: bfloat16 [4096, 5120], P('ctx', 'head')
- value_grad: bfloat16 [4096, 5120], P('ctx', 'head')
The draws below stay inside these ranges and needn't reach their ends.
Inputs may be any that keep to these rules, and one draw needn't show every extreme that they name: `key_tiles`: row t lists, ascending, the 4 tiles of 4 consecutive tile-frames of 1 tiles; every listed tile lies on an index of ctx at most 1 away from tile t's, and in every draw some tile reads a tile exactly 1 below and some tile one exactly 1 above. `global_ids`: entries c * 2 to (c + 1) * 2 - 1 are distinct ascending tokens of index c of ctx. `readers`: each row has either one 1 or all 16 entries 1; at least one row has all.
All inputs are finite; a program needn't handle non-finite values.
Results may differ from the reference program's by a relative error of at most 0.02.
Values may be sent and summed in bfloat16 or wider, within the bound.
No kernel may reach another device: no remote copies, remote signals or barrier semaphores. Data moves between devices by JAX's collectives and lax.ppermute only.
A program may use at most 128 MiB of HBM per device.

```python
import jax
import jax.numpy as jnp
from jax import lax

HEADS = 40
HEAD_DIM = 128
D = 5120
TILE = 128
FRAME_TILES = 1
WIN_FRAMES = 4
REACH = 1
KEYS = 4
TILES_DEV = 2
TOK_DEV = 256
TOKENS = 4096
NT = 32
G_DEV = 2
GLOBAL = 32


def draw_query_raw(key, part):
    position = jnp.arange(D, dtype=jnp.float32)[None, :] / D
    noise = jnp.clip(jax.random.normal(jax.random.fold_in(key, 13), (TOKENS, D)), -5.0, 5.0)
    return (noise * (0.6 + 1.2 * position)).astype(jnp.bfloat16)


def draw_key_raw(key, part):
    position = jnp.arange(D, dtype=jnp.float32)[None, :] / D
    noise = jnp.clip(jax.random.normal(jax.random.fold_in(key, 23), (TOKENS, D)), -5.0, 5.0)
    return (noise * (0.6 + 1.2 * position)).astype(jnp.bfloat16)


def draw_key_tiles(key, part):
    frames_here = TILES_DEV // FRAME_TILES
    frames_all = NT // FRAME_TILES
    devices_count = NT // TILES_DEV
    tile_ids = jnp.arange(NT, dtype=jnp.int32)
    frame_number = tile_ids // FRAME_TILES
    lowest = frame_number - REACH * frames_here
    start_count = 2 * REACH * frames_here - WIN_FRAMES + 2
    start = lowest + jax.random.randint(jax.random.fold_in(key, 31), (NT,), 0, start_count)
    low_device = jax.random.randint(jax.random.fold_in(key, 32), (), REACH, devices_count // 2)
    high_device = jax.random.randint(jax.random.fold_in(key, 33), (), devices_count // 2, devices_count - REACH)
    far_low = low_device * TILES_DEV
    far_high = high_device * TILES_DEV + TILES_DEV - 1
    start = jnp.where(tile_ids == far_low, lowest, start)
    start = jnp.where(tile_ids == far_high, lowest + start_count - 1, start)
    start = jnp.clip(start, 0, frames_all - WIN_FRAMES)
    return (start[:, None] * FRAME_TILES + jnp.arange(KEYS, dtype=jnp.int32)[None, :]).astype(jnp.int32)


def pick_rows(device_key, device_number):
    chosen_rows = jax.random.permutation(device_key, TOK_DEV)[:G_DEV]
    return jnp.sort(chosen_rows).astype(jnp.int32) + device_number * TOK_DEV


def draw_global_ids(key, part):
    devices_count = GLOBAL // G_DEV
    device_keys = jax.random.split(jax.random.fold_in(key, 41), devices_count)
    numbers = jnp.arange(devices_count, dtype=jnp.int32)
    return jax.vmap(pick_rows)(device_keys, numbers).reshape(-1).astype(jnp.int32)


def rank_tiles(device_key):
    return jax.random.permutation(device_key, GLOBAL // G_DEV).astype(jnp.int32)


def draw_readers(key, part):
    devices_count = GLOBAL // G_DEV
    tiles_count = GLOBAL // G_DEV
    ranks = jax.vmap(rank_tiles)(jax.random.split(jax.random.fold_in(key, 51), devices_count))
    heavy = jax.random.randint(jax.random.fold_in(key, 52), (devices_count,), 0, 4) == 0
    busiest = jax.random.randint(jax.random.fold_in(key, 53), (), 0, devices_count)
    heavy = heavy | (jnp.arange(devices_count, dtype=jnp.int32) == busiest)
    counts = jnp.where(heavy, tiles_count, 1)
    return (ranks < counts[:, None]).astype(jnp.int32)


def block_scale(stream_key, shape, cuts, least, high):
    factor_of = 1.0
    for dim, shards_of in cuts:
        draws = jax.random.uniform(jax.random.fold_in(jax.random.fold_in(stream_key, 6), dim), (shards_of,), jnp.float32, least / len(cuts), high / len(cuts))
        factor_of = factor_of * jnp.repeat(jnp.exp(draws), shape[dim] // shards_of).reshape((-1,) + (1,) * (len(shape) - 1 - dim))
    return factor_of


def normal_values(stream_key, dims, deviation, limit, cuts=(), kind=jnp.bfloat16):
    values = deviation * jax.random.normal(stream_key, dims, jnp.float32)
    if cuts:
        values = values * block_scale(stream_key, dims, cuts, -0.22, 0.18)
    return jnp.clip(values, -limit, limit).astype(kind)


def setup_inputs(seed: int = 0) -> dict:
    arg_keys = jax.random.split(jax.random.key(seed), 10)
    query_raw = draw_query_raw(jax.random.fold_in(arg_keys[9], 71), 0)
    key_raw = draw_key_raw(jax.random.fold_in(arg_keys[9], 71), 0)
    values = normal_values(arg_keys[2], (TOKENS, D), 1.0, 6.0, ((0, 16), (1, 2)))
    out_grad = normal_values(arg_keys[3], (TOKENS, D), 24.0, 128.0, ((0, 16), (1, 2)))
    query_gain = jnp.clip(1.0 + 0.15 * jax.random.normal(arg_keys[4], (D,), jnp.float32), 0.25, 1.75)
    key_gain = jnp.clip(1.0 + 0.15 * jax.random.normal(arg_keys[5], (D,), jnp.float32), 0.25, 1.75)
    key_tiles = draw_key_tiles(jax.random.fold_in(arg_keys[9], 71), 0)
    global_ids = draw_global_ids(jax.random.fold_in(arg_keys[9], 71), 0)
    readers = draw_readers(jax.random.fold_in(arg_keys[9], 71), 0)
    return dict(query_raw=query_raw, key_raw=key_raw, values=values, out_grad=out_grad, query_gain=query_gain, key_gain=key_gain, key_tiles=key_tiles, global_ids=global_ids, readers=readers)


EPSILON = 1e-06

def normalize(raw_rows, gain):
    as_float = raw_rows.astype(jnp.float32)
    inverse = lax.rsqrt(lax.optimization_barrier(jnp.mean(as_float * as_float, axis=1, keepdims=True)) + EPSILON)
    normed = lax.optimization_barrier((as_float * inverse * gain).astype(jnp.bfloat16))
    return (as_float, inverse, normed)

def norm_grad(as_float, inverse, scaled):
    coeffs = lax.optimization_barrier(jnp.mean(scaled * as_float, axis=1, keepdims=True))
    return (inverse * scaled - as_float * inverse ** 3 * coeffs).astype(jnp.bfloat16)

def reference(query_raw, key_raw, values, out_grad, query_gain, key_gain, key_tiles, global_ids, readers):
    query_float, query_inv, query_norm = normalize(query_raw, query_gain)
    key_float, key_inv, key_norm = normalize(key_raw, key_gain)
    factor = HEAD_DIM ** (-0.5)
    global_keys = key_norm[global_ids].astype(jnp.float32).reshape(GLOBAL, HEADS, HEAD_DIM)
    global_vals = values[global_ids].astype(jnp.float32).reshape(GLOBAL, HEADS, HEAD_DIM)
    offsets = jnp.arange(TILE, dtype=jnp.int32)

    def one_tile(carry, tile_index):
        key_acc, value_acc = carry
        start = tile_index * TILE
        query_block = lax.dynamic_slice_in_dim(query_norm, start, TILE, 0).astype(jnp.float32).reshape(TILE, HEADS, HEAD_DIM)
        grad_block = lax.dynamic_slice_in_dim(out_grad, start, TILE, 0).astype(jnp.float32).reshape(TILE, HEADS, HEAD_DIM)
        window_rows = (key_tiles[tile_index][:, None] * TILE + offsets[None, :]).reshape(-1).astype(jnp.int32)
        keys_all = jnp.concatenate([key_norm[window_rows].astype(jnp.float32).reshape(-1, HEADS, HEAD_DIM), global_keys], axis=0)
        vals_all = jnp.concatenate([values[window_rows].astype(jnp.float32).reshape(-1, HEADS, HEAD_DIM), global_vals], axis=0)
        live_mask = jnp.concatenate([jnp.ones((KEYS * TILE,), dtype=bool), jnp.repeat(readers[tile_index // TILES_DEV] > 0, G_DEV)])
        scores = jnp.einsum('qhd,khd->hqk', query_block, keys_all) * factor
        scores = jnp.where(live_mask[None, None, :], scores, -jnp.inf)
        largest = lax.optimization_barrier(jnp.max(scores, axis=2, keepdims=True))
        log_total = largest + jnp.log(lax.optimization_barrier(jnp.sum(jnp.exp(scores - largest), axis=2, keepdims=True)))
        probs = jnp.exp(scores - log_total)
        probs_low = lax.optimization_barrier(probs.astype(jnp.bfloat16)).astype(jnp.float32)
        attended = lax.optimization_barrier(jnp.einsum('hqk,khd->qhd', probs_low, vals_all).astype(jnp.bfloat16)).astype(jnp.float32)
        delta = lax.optimization_barrier(jnp.sum(grad_block * attended, axis=2))
        dprob = jnp.einsum('qhd,khd->hqk', grad_block, vals_all)
        dscore = probs * (dprob - jnp.transpose(delta)[:, :, None]) * factor
        dscore = lax.optimization_barrier(dscore.astype(jnp.bfloat16)).astype(jnp.float32)
        grad_query = jnp.einsum('hqk,khd->qhd', dscore, keys_all).reshape(TILE, D)
        key_part = jnp.einsum('hqk,qhd->khd', dscore, query_block).reshape(-1, D)
        value_part = jnp.einsum('hqk,qhd->khd', probs_low, grad_block).reshape(-1, D)
        all_rows = jnp.concatenate([window_rows, global_ids.astype(jnp.int32)])
        return ((key_acc.at[all_rows].add(key_part), value_acc.at[all_rows].add(value_part)), grad_query)
    zero_grads = jnp.zeros((TOKENS, D), jnp.float32)
    (key_acc, value_acc), grad_tiles = lax.scan(one_tile, (zero_grads, zero_grads), jnp.arange(NT, dtype=jnp.int32))
    grad_qnorm = grad_tiles.reshape(TOKENS, D)
    query_grad = norm_grad(query_float, query_inv, grad_qnorm * query_gain)
    key_grad = norm_grad(key_float, key_inv, key_acc * key_gain)
    return (query_grad, key_grad, value_acc.astype(jnp.bfloat16))
```

```python
import functools

import jax
import jax.numpy as jnp
from jax import lax
from jax.experimental import pallas as pl
from jax.experimental.pallas import tpu as pltpu
from jax.sharding import PartitionSpec as P

HEAD_DIM = 128
D = 5120
TILE = 128
REACH = 1
G_DEV = 2
GROUP = 4
CHUNKS = (2, 2, 1)


EPSILON = 1e-06
FACTOR = HEAD_DIM ** (-0.5)
F32 = jnp.float32
BF16 = jnp.bfloat16
VMEM_LIMIT = 48 * 1024 * 1024


def swapped(shard, bit):
    count = lax.axis_size("ctx")
    return lax.ppermute(shard, "ctx", [(i, i ^ bit) for i in range(count)])


def params():
    return pltpu.CompilerParams(vmem_limit_bytes=VMEM_LIMIT)


def cost(flops, read):
    return pl.CostEstimate(flops=int(flops), bytes_accessed=int(read), transcendentals=0)


def contract(a, b, dims, precision=None):
    return lax.dot_general(
        a, b, (dims, ((), ())), precision=precision, preferred_element_type=F32
    )


def lane_pair(first, second, rows):
    lane = lax.broadcasted_iota(jnp.int32, (rows, HEAD_DIM), 1)
    return jnp.where(lane < HEAD_DIM // 2, first, second)


def squares_kernel(query_ref, key_ref, out_ref):
    step = pl.program_id(0)
    query = query_ref[...].astype(F32)
    key = key_ref[...].astype(F32)
    part = lane_pair(
        jnp.sum(query * query, axis=1, keepdims=True),
        jnp.sum(key * key, axis=1, keepdims=True),
        query.shape[0],
    )

    @pl.when(step == 0)
    def _():
        out_ref[...] = part

    @pl.when(step > 0)
    def _():
        out_ref[...] += part


def squares(query_raw, key_raw):
    rows, width = query_raw.shape
    block = width // 4
    return pl.pallas_call(
        squares_kernel,
        out_shape=jax.ShapeDtypeStruct((rows, HEAD_DIM), F32),
        grid=(4,),
        in_specs=[pl.BlockSpec((rows, block), lambda i: (0, i))] * 2,
        out_specs=pl.BlockSpec((rows, HEAD_DIM), lambda i: (0, 0)),
        compiler_params=params(),
        cost_estimate=cost(4 * rows * width, 4 * rows * width),
        name="squares",
    )(query_raw, key_raw)


def inverses(own, other):
    both = lax.rsqrt((own + other) / D + EPSILON)
    return both[:, :1], both[:, HEAD_DIM // 2 : HEAD_DIM // 2 + 1]


def pack_kernel(place_ref, tiles_ref, ids_ref, readers_ref, own_ref, other_ref, *refs):
    per = 6
    me, plane = place_ref[0], place_ref[1]
    query_inv, key_inv = inverses(own_ref[...], other_ref[...])
    rows = own_ref.shape[0]
    row = lax.broadcasted_iota(jnp.int32, (16, HEAD_DIM), 0)
    lane = lax.broadcasted_iota(jnp.int32, (16, HEAD_DIM), 1)
    facts = jnp.full((16, HEAD_DIM), -1, jnp.int32)
    device = plane * GROUP + me
    for r in range(G_DEV):
        facts = jnp.where(row == me * G_DEV + r, ids_ref[r] - device * rows, facts)
    for tile in range(rows // TILE):
        start = tiles_ref[tile, 0] - (plane * GROUP - 1) * (rows // TILE)
        facts = jnp.where(row == 9 + tile, start, facts)
    for e in range(GROUP):
        for j in range(GROUP):
            live = readers_ref[0, (plane ^ e) * GROUP + j]
            chosen = (row == 8) & (lane // G_DEV == GROUP * e + j)
            facts = jnp.where(chosen, live, facts)
    facts = facts.astype(F32).astype(BF16)
    for d in range(GROUP):
        key, value, query, grad, key_gain, query_gain = refs[per * d : per * d + per]
        out = refs[per * GROUP + d]
        out[0:rows] = (key[...].astype(F32) * key_inv * key_gain[...]).astype(BF16)
        out[rows : 2 * rows] = value[...]
        out[2 * rows : 3 * rows] = (
            query[...].astype(F32) * query_inv * query_gain[...]
        ).astype(BF16)
        out[3 * rows : 4 * rows] = grad[...]
        out[4 * rows :] = facts


def pack(place, tiles, ids, readers, own, other, arrays, gains, first, count):
    query_raw, key_raw, values, out_grad = arrays
    query_gain, key_gain = gains
    rows, width = query_raw.shape
    each = width // HEAD_DIM // GROUP
    smem = pl.BlockSpec(memory_space=pltpu.SMEM)
    whole = pl.BlockSpec((rows, HEAD_DIM), lambda h, place: (0, 0))
    specs, operands = [], []
    for d in range(GROUP):
        at = lambda h, place, d=d: (0, (place[0] ^ d) * each + first + h)
        specs += [pl.BlockSpec((rows, HEAD_DIM), at)] * 4 + [pl.BlockSpec((1, HEAD_DIM), at)] * 2
        operands += [key_raw, values, query_raw, out_grad, key_gain, query_gain]
    out_rows = 4 * rows + 16
    return pl.pallas_call(
        pack_kernel,
        out_shape=[jax.ShapeDtypeStruct((out_rows, count * HEAD_DIM), BF16)] * GROUP,
        grid_spec=pltpu.PrefetchScalarGridSpec(
            num_scalar_prefetch=1,
            grid=(count,),
            in_specs=[smem, smem, smem, whole, whole] + specs,
            out_specs=[pl.BlockSpec((out_rows, HEAD_DIM), lambda h, place: (0, h))] * GROUP,
        ),
        compiler_params=params(),
        cost_estimate=cost(1, 4 * out_rows * count * HEAD_DIM * 4),
        name="pack",
    )(place, tiles, ids, readers, own, other, *operands)


def edges_kernel(place_ref, b0, b1, b2, b3, near_ref, far_ref, own_ref):
    me, plane = place_ref[0], place_ref[1]
    rows = (b0.shape[0] - 16) // 4
    total = jnp.zeros((16, HEAD_DIM), F32)
    lane = lax.broadcasted_iota(jnp.int32, (8, HEAD_DIM), 1)
    for block in (b0, b1, b2, b3):
        facts = block[4 * rows :].astype(F32)[:8].astype(jnp.int32)
        hot = jnp.concatenate([facts == lane, facts == lane + HEAD_DIM], axis=1)
        hot = hot.astype(F32).astype(BF16)
        total = total + jnp.concatenate(
            [
                contract(hot, block[0:rows], ((1,), (0,))),
                contract(hot, block[rows : 2 * rows], ((1,), (0,))),
            ],
            axis=0,
        )
    total = total.astype(BF16)
    own_ref[...] = total
    near_ref[2 * rows :] = total
    far_ref[2 * rows :] = total
    even = plane % 2 == 0
    last, first = me ^ (GROUP - 1), me
    for d, block in enumerate((b0, b1, b2, b3)):

        @pl.when(jnp.where(even, last, first) == d)
        def _(block=block):
            near_ref[: 2 * rows] = block[: 2 * rows]

        @pl.when(jnp.where(even, first, last) == d)
        def _(block=block):
            far_ref[: 2 * rows] = block[: 2 * rows]


def edges(place, blocks):
    out_rows, width = blocks[0].shape
    rows = (out_rows - 16) // 4
    at = lambda h, place: (0, h)
    return pl.pallas_call(
        edges_kernel,
        out_shape=[
            jax.ShapeDtypeStruct((2 * rows + 16, width), BF16),
            jax.ShapeDtypeStruct((2 * rows + 16, width), BF16),
            jax.ShapeDtypeStruct((16, width), BF16),
        ],
        grid_spec=pltpu.PrefetchScalarGridSpec(
            num_scalar_prefetch=1,
            grid=(width // HEAD_DIM,),
            in_specs=[pl.BlockSpec((out_rows, HEAD_DIM), at)] * GROUP,
            out_specs=[
                pl.BlockSpec((2 * rows + 16, HEAD_DIM), at),
                pl.BlockSpec((2 * rows + 16, HEAD_DIM), at),
                pl.BlockSpec((16, HEAD_DIM), at),
            ],
        ),
        compiler_params=params(),
        cost_estimate=cost(1, 4 * out_rows * width * 2),
        name="edges",
    )(place, *blocks)


def attend_kernel(
    place_ref, b0, b1, b2, b3, own_g, near, far, mid,
    q0, q1, q2, q3, a0, a1, a2, a3, near_out, far_out, mid_out, own_out,
    pair, weights, sums, pair_g, sums_g,
):
    me, plane = place_ref[0], place_ref[1]
    rows = (b0.shape[0] - 16) // 4
    keys = slice(0, HEAD_DIM)
    vals = slice(HEAD_DIM, 2 * HEAD_DIM)
    blocks = (b0, b1, b2, b3)
    for d, block in enumerate(blocks):
        at = pl.multiple_of(((me ^ d) + 1) * rows, TILE)
        pair[pl.ds(at, rows), keys] = block[0:rows]
        pair[pl.ds(at, rows), vals] = block[rows : 2 * rows]
    even = plane % 2 == 0
    top = (GROUP + 1) * rows
    near_at = pl.multiple_of(jnp.where(even, top, 0), TILE)
    far_at = pl.multiple_of(jnp.where(even, 0, top), TILE)
    for ref, at in ((near, near_at), (far, far_at)):
        pair[pl.ds(at, rows), keys] = ref[0:rows]
        pair[pl.ds(at, rows), vals] = ref[rows : 2 * rows]
    globals_in = [
        own_g[...].astype(F32),
        near[2 * rows :].astype(F32),
        mid[...].astype(F32),
        far[2 * rows :].astype(F32),
    ]
    pair_g[:, keys] = jnp.concatenate([x[:8] for x in globals_in], axis=0).astype(BF16)
    pair_g[:, vals] = jnp.concatenate([x[8:] for x in globals_in], axis=0).astype(BF16)
    sums[...] = jnp.zeros_like(sums)
    sums_g[...] = jnp.zeros_like(sums_g)
    weights[...] = jnp.zeros_like(weights)
    count_g = pair_g.shape[0]
    row = lax.broadcasted_iota(jnp.int32, (count_g, HEAD_DIM), 0)
    lane = lax.broadcasted_iota(jnp.int32, (count_g, HEAD_DIM), 1)
    span = 4 * TILE
    for d, (block, q_out) in enumerate(zip(blocks, (q0, q1, q2, q3))):
        facts = block[4 * rows :].astype(F32)
        live = jnp.sum(jnp.where(row == lane, facts[8:9], 0.0), axis=1, keepdims=True) > 0.0
        for tile in range(rows // TILE):
            start = jnp.max(facts[9 + tile : 10 + tile]).astype(jnp.int32)
            at = pl.multiple_of(start * TILE, TILE)
            here = slice(2 * rows + tile * TILE, 2 * rows + (tile + 1) * TILE)
            there = slice(3 * rows + tile * TILE, 3 * rows + (tile + 1) * TILE)
            weights[:TILE, keys] = block[here]
            weights[TILE:, vals] = block[there]
            w = weights[...]
            both = jnp.concatenate([pair[pl.ds(at, span)], pair_g[...]], axis=0)
            product = contract(both, w, ((1,), (1,)))
            score = product[:, :TILE] * FACTOR
            dprob = product[:, TILE:]
            score_g = jnp.where(live, score[span:], -jnp.inf)
            score = jnp.concatenate([score[:span], score_g], axis=0)
            largest = jnp.max(score, axis=0, keepdims=True)
            probs = jnp.exp(score - largest)
            probs = probs * (1.0 / jnp.sum(probs, axis=0, keepdims=True))
            delta = jnp.sum(probs * dprob, axis=0, keepdims=True)
            dscore = (probs * (dprob - delta) * FACTOR).astype(BF16)
            grads = contract(
                jnp.concatenate([dscore, probs.astype(BF16)], axis=1), w, ((1,), (0,))
            )
            sums[pl.ds(at, span)] += grads[:span]
            sums_g[...] += grads[span:]
            grad_query = contract(dscore, both[:, keys], ((0,), (0,)))
            q_out[tile * TILE : (tile + 1) * TILE] = grad_query.astype(BF16)
    for d, out in enumerate((a0, a1, a2, a3)):
        at = pl.multiple_of(((me ^ d) + 1) * rows, TILE)
        out[0] = sums[pl.ds(at, rows), keys]
        out[1] = sums[pl.ds(at, rows), vals]
    global_rows = [
        jnp.concatenate(
            [sums_g[8 * e : 8 * e + 8, keys], sums_g[8 * e : 8 * e + 8, vals]], axis=0
        )
        for e in range(GROUP)
    ]
    own_out[...] = global_rows[0]
    mid_out[...] = global_rows[2].astype(BF16)
    for out, at, part in (
        (near_out, near_at, global_rows[1]),
        (far_out, far_at, global_rows[3]),
    ):
        out[:rows] = sums[pl.ds(at, rows), keys].astype(BF16)
        out[rows : 2 * rows] = sums[pl.ds(at, rows), vals].astype(BF16)
        out[2 * rows :] = part.astype(BF16)


def attend(place, blocks, own_g, near, far, mid):
    out_rows, width = blocks[0].shape
    rows = (out_rows - 16) // 4
    count = width // HEAD_DIM
    at = lambda h, place: (0, h)
    deep = lambda h, place: (0, 0, h)
    tall = pl.BlockSpec((out_rows, HEAD_DIM), at)
    edge = pl.BlockSpec((2 * rows + 16, HEAD_DIM), at)
    few = pl.BlockSpec((16, HEAD_DIM), at)
    return pl.pallas_call(
        attend_kernel,
        out_shape=[jax.ShapeDtypeStruct((rows, width), BF16)] * GROUP
        + [jax.ShapeDtypeStruct((2, rows, width), F32)] * GROUP
        + [jax.ShapeDtypeStruct((2 * rows + 16, width), BF16)] * 2
        + [jax.ShapeDtypeStruct((16, width), BF16), jax.ShapeDtypeStruct((16, width), F32)],
        grid_spec=pltpu.PrefetchScalarGridSpec(
            num_scalar_prefetch=1,
            grid=(count,),
            in_specs=[tall] * GROUP + [few, edge, edge, few],
            out_specs=[pl.BlockSpec((rows, HEAD_DIM), at)] * GROUP
            + [pl.BlockSpec((2, rows, HEAD_DIM), deep)] * GROUP
            + [edge, edge, few, few],
            scratch_shapes=[
                pltpu.VMEM(((GROUP + 2) * rows, 2 * HEAD_DIM), BF16),
                pltpu.VMEM((2 * TILE, 2 * HEAD_DIM), BF16),
                pltpu.VMEM(((GROUP + 2) * rows, 2 * HEAD_DIM), F32),
                pltpu.VMEM((8 * GROUP, 2 * HEAD_DIM), BF16),
                pltpu.VMEM((8 * GROUP, 2 * HEAD_DIM), F32),
            ],
        ),
        compiler_params=params(),
        cost_estimate=cost(count * 5e9, 4 * out_rows * width * 4),
        name="attend",
    )(place, *blocks, own_g, near, far, mid)


def settle_kernel(
    place_ref, f0, f1, f2, f3, q0, q1, q2, q3, a0, a1, a2, a3, own_g, near, far, mid,
    o0, o1, o2, o3,
):
    me, plane = place_ref[0], place_ref[1]
    rows = q0.shape[0]
    even = plane % 2 == 0
    part = (
        own_g[...]
        + near[2 * rows :].astype(F32)
        + mid[...].astype(F32)
        + far[2 * rows :].astype(F32)
    )
    inner = (plane == 1) | (plane == 2)
    lane = lax.broadcasted_iota(jnp.int32, (8, HEAD_DIM), 1)
    for d, (fact, dq, acc, out) in enumerate(
        zip((f0, f1, f2, f3), (q0, q1, q2, q3), (a0, a1, a2, a3), (o0, o1, o2, o3))
    ):
        j = me ^ d
        facts = fact[...].astype(F32)[:8].astype(jnp.int32)
        hot = jnp.concatenate([facts == lane, facts == lane + HEAD_DIM], axis=1).astype(F32)
        near_here = j == jnp.where(even, GROUP - 1, 0)
        far_here = (j == jnp.where(even, 0, GROUP - 1)) & inner
        out[:rows] = dq[...]
        for i in range(2):
            total = acc[i] + contract(
                hot, part[8 * i : 8 * i + 8], ((0,), (0,)), lax.Precision.HIGHEST
            )
            rest = slice(i * rows, (i + 1) * rows)
            total = total + jnp.where(near_here, near[rest].astype(F32), 0.0)
            total = total + jnp.where(far_here, far[rest].astype(F32), 0.0)
            out[(i + 1) * rows : (i + 2) * rows] = total.astype(BF16)


def settle(place, blocks, dqs, accs, own_g, near, far, mid):
    rows, width = dqs[0].shape
    at = lambda h, place: (0, h)
    deep = lambda h, place: (0, 0, h)
    edge = pl.BlockSpec((2 * rows + 16, HEAD_DIM), at)
    few = pl.BlockSpec((16, HEAD_DIM), at)
    facts = pl.BlockSpec((16, HEAD_DIM), lambda h, place: (4 * rows // 16, h))
    return pl.pallas_call(
        settle_kernel,
        out_shape=[jax.ShapeDtypeStruct((3 * rows, width), BF16)] * GROUP,
        grid_spec=pltpu.PrefetchScalarGridSpec(
            num_scalar_prefetch=1,
            grid=(width // HEAD_DIM,),
            in_specs=[facts] * GROUP
            + [pl.BlockSpec((rows, HEAD_DIM), at)] * GROUP
            + [pl.BlockSpec((2, rows, HEAD_DIM), deep)] * GROUP
            + [few, edge, edge, few],
            out_specs=[pl.BlockSpec((3 * rows, HEAD_DIM), at)] * GROUP,
        ),
        compiler_params=params(),
        cost_estimate=cost(1, 16 * rows * width * 4),
        name="settle",
    )(place, *blocks, *dqs, *accs, own_g, near, far, mid)


def dots_kernel(place_ref, *refs):
    out_ref = refs[-1]
    rows = out_ref.shape[0]
    step = pl.program_id(0)
    totals = [jnp.zeros((rows, HEAD_DIM), F32), jnp.zeros((rows, HEAD_DIM), F32)]
    for d in range(GROUP):
        grads, query, key, query_gain, key_gain = refs[5 * d : 5 * d + 5]
        totals[0] += grads[:rows].astype(F32) * query_gain[...] * query[...].astype(F32)
        totals[1] += grads[rows:].astype(F32) * key_gain[...] * key[...].astype(F32)
    part = lane_pair(
        jnp.sum(totals[0], axis=1, keepdims=True), jnp.sum(totals[1], axis=1, keepdims=True), rows
    )

    @pl.when(step == 0)
    def _():
        out_ref[...] = part

    @pl.when(step > 0)
    def _():
        out_ref[...] += part


def dots(place, grads, query_raw, key_raw, gains, first):
    rows, full = query_raw.shape
    count = grads[0].shape[1] // HEAD_DIM
    each = full // HEAD_DIM // GROUP
    specs, operands = [], []
    for d in range(GROUP):
        at = lambda h, place, d=d: (0, (place[0] ^ d) * each + first + h)
        specs += (
            [pl.BlockSpec((2 * rows, HEAD_DIM), lambda h, place: (0, h))]
            + [pl.BlockSpec((rows, HEAD_DIM), at)] * 2
            + [pl.BlockSpec((1, HEAD_DIM), at)] * 2
        )
        operands += [grads[d], query_raw, key_raw, gains[0], gains[1]]
    return pl.pallas_call(
        dots_kernel,
        out_shape=jax.ShapeDtypeStruct((rows, HEAD_DIM), F32),
        grid_spec=pltpu.PrefetchScalarGridSpec(
            num_scalar_prefetch=1,
            grid=(count,),
            in_specs=specs,
            out_specs=pl.BlockSpec((rows, HEAD_DIM), lambda h, place: (0, 0)),
        ),
        compiler_params=params(),
        cost_estimate=cost(1, 16 * rows * count * HEAD_DIM * 2),
        name="dots",
    )(place, *operands)


def finish_kernel(chunks, place_ref, own_ref, other_ref, dot_ref, dot_other_ref, *refs):
    me = place_ref[0]
    grads = refs[: GROUP * len(chunks)]
    query_ref, key_ref, query_gain, key_gain = refs[GROUP * len(chunks) : GROUP * len(chunks) + 4]
    query_out, key_out, value_out = refs[GROUP * len(chunks) + 4 :]
    rows, full = query_ref.shape
    each = full // GROUP
    inv = inverses(own_ref[...], other_ref[...])
    total = dot_ref[...] + dot_other_ref[...]
    dot = (total[:, :1], total[:, HEAD_DIM // 2 : HEAD_DIM // 2 + 1])
    coeff = [inv[i] * inv[i] * inv[i] * (dot[i] / D) for i in range(2)]
    for d in range(GROUP):
        first = 0
        for c, count in enumerate(chunks):
            ref = grads[c * GROUP + d]
            for h in range(count):
                at = pl.multiple_of((me ^ d) * each + (first + h) * HEAD_DIM, HEAD_DIM)
                here = pl.ds(at, HEAD_DIM)
                col = slice(h * HEAD_DIM, (h + 1) * HEAD_DIM)
                for i, (raw, gain, out) in enumerate(
                    ((query_ref, query_gain, query_out), (key_ref, key_gain, key_out))
                ):
                    grad = ref[i * rows : (i + 1) * rows, col].astype(F32)
                    out[:, here] = (
                        inv[i] * (grad * gain[:, here]) - raw[:, here].astype(F32) * coeff[i]
                    ).astype(BF16)
                value_out[:, here] = ref[2 * rows :, col]
            first += count


def finish(place, own, other, dot, dot_other, grads, query_raw, key_raw, gains, chunks):
    vmem = pl.BlockSpec(memory_space=pltpu.VMEM)
    flat = [x for chunk in grads for x in chunk]
    return pl.pallas_call(
        functools.partial(finish_kernel, chunks),
        out_shape=[jax.ShapeDtypeStruct(query_raw.shape, BF16)] * 3,
        in_specs=[pl.BlockSpec(memory_space=pltpu.SMEM)] + [vmem] * (4 + len(flat) + 4),
        out_specs=[vmem] * 3,
        compiler_params=params(),
        cost_estimate=cost(1, 16 * query_raw.size),
        name="finish",
    )(place, own, other, dot, dot_other, *flat, query_raw, key_raw, *gains)


def swap_heads(x):
    return lax.ppermute(x, "head", [(0, 1), (1, 0)])


def plane_body(
    query_raw, key_raw, values, out_grad, query_gain, key_gain, key_tiles, global_ids, readers
):
    device = lax.axis_index("ctx")
    place = jnp.stack([device % GROUP, device // GROUP]).astype(jnp.int32)
    gains = (query_gain[None, :], key_gain[None, :])
    own = squares(query_raw, key_raw)
    other = swap_heads(own)
    arrays = (query_raw, key_raw, values, out_grad)
    packed, first = [], 0
    for count in CHUNKS:
        sent = pack(
            place, key_tiles, global_ids, readers, own, other, arrays, gains, first, count
        )
        packed.append([sent[0]] + [swapped(sent[d], d) for d in range(1, GROUP)])
        first += count
    homes, dot, first = [], None, 0
    for count, blocks in zip(CHUNKS, packed):
        near, far, own_g = edges(place, blocks)
        near, far, mid = swapped(near, 4), swapped(far, 12), swapped(own_g, 8)
        results = attend(place, blocks, own_g, near, far, mid)
        dqs, accs = results[:GROUP], results[GROUP : 2 * GROUP]
        near, far, mid, own_g = results[2 * GROUP :]
        near, far, mid = swapped(near, 4), swapped(far, 12), swapped(mid, 8)
        sent = settle(place, blocks, dqs, accs, own_g, near, far, mid)
        home = [sent[0]] + [swapped(sent[d], d) for d in range(1, GROUP)]
        part = dots(place, home, query_raw, key_raw, gains, first)
        dot = part if dot is None else dot + part
        homes.append(home)
        first += count
    dot_other = swap_heads(dot)
    return tuple(
        finish(place, own, other, dot, dot_other, homes, query_raw, key_raw, gains, CHUNKS)
    )


def passed_along(shard, axis, by):
    count = lax.axis_size(axis)
    return lax.ppermute(shard, axis, [(i, (i + by) % count) for i in range(count)])


def normalize(as_float, gain, squares):
    inverse = lax.rsqrt(squares[:, None] / D + EPSILON)
    return (inverse, (as_float * inverse * gain).astype(jnp.bfloat16))


def norm_grad(as_float, inverse, scaled, coeffs):
    return (inverse * scaled - as_float * inverse**3 * (coeffs[:, None] / D)).astype(jnp.bfloat16)


def body(
    query_raw, key_raw, values, out_grad, query_gain, key_gain, key_tiles, global_ids, readers
):
    tokens_here, width_here = query_raw.shape
    heads_here = width_here // HEAD_DIM
    tiles_here = tokens_here // TILE
    factor = HEAD_DIM ** (-0.5)
    device = lax.axis_index("ctx")
    query_rows = query_raw.astype(jnp.float32)
    key_rows = key_raw.astype(jnp.float32)
    query_sq, key_sq = lax.psum(
        (jnp.sum(query_rows * query_rows, axis=1), jnp.sum(key_rows * key_rows, axis=1)), "head"
    )
    query_inv, query_norm = normalize(query_rows, query_gain, query_sq)
    key_inv, key_norm = normalize(key_rows, key_gain, key_sq)
    own_rows = global_ids - device * tokens_here
    own_pair = jnp.stack([key_norm[own_rows], values[own_rows]])
    global_pair = lax.all_gather(own_pair, "ctx", axis=1, tiled=True)
    global_keys = global_pair[0].reshape(-1, heads_here, HEAD_DIM)
    global_vals = global_pair[1].reshape(-1, heads_here, HEAD_DIM)
    live_mask = jnp.repeat(readers[0] > 0, G_DEV)
    key_value = jnp.stack([key_norm, values])
    current = passed_along(key_value, "ctx", -REACH)
    pieces = [current]
    for hop_index in range(2 * REACH):
        current = passed_along(current, "ctx", 1)
        pieces.append(current)
    pieces = pieces[::-1]
    window_pair = jnp.concatenate(pieces, axis=1)
    first_tile = (device - REACH) * tiles_here
    local_tiles = key_tiles - first_tile
    window_rows = (
        local_tiles[:, :, None] * TILE + jnp.arange(TILE, dtype=jnp.int32)[None, None, :]
    ).reshape(tiles_here, -1)
    window_count = window_rows.shape[1]
    window_keys = window_pair[0][window_rows].reshape(
        tiles_here, window_count, heads_here, HEAD_DIM
    )
    window_vals = window_pair[1][window_rows].reshape(
        tiles_here, window_count, heads_here, HEAD_DIM
    )
    query_four = query_norm.reshape(tiles_here, TILE, heads_here, HEAD_DIM)
    grad_four = out_grad.reshape(tiles_here, TILE, heads_here, HEAD_DIM)

    def head_block(head_number):
        query_head = lax.dynamic_index_in_dim(query_four, head_number, 2, keepdims=False)
        grad_head = lax.dynamic_index_in_dim(grad_four, head_number, 2, keepdims=False)
        wkeys = lax.dynamic_index_in_dim(window_keys, head_number, 2, keepdims=False)
        wvals = lax.dynamic_index_in_dim(window_vals, head_number, 2, keepdims=False)
        gkeys = lax.dynamic_index_in_dim(global_keys, head_number, 1, keepdims=False)
        gvals = lax.dynamic_index_in_dim(global_vals, head_number, 1, keepdims=False)
        score_window = (
            jnp.einsum("tqd,tkd->tqk", query_head, wkeys, preferred_element_type=jnp.float32)
            * factor
        )
        score_global = (
            jnp.einsum("tqd,kd->tqk", query_head, gkeys, preferred_element_type=jnp.float32)
            * factor
        )
        score_global = jnp.where(live_mask, score_global, -jnp.inf)
        scores = jnp.concatenate([score_window, score_global], axis=2)
        largest = jnp.max(scores, axis=2, keepdims=True)
        log_total = largest + jnp.log(jnp.sum(jnp.exp(scores - largest), axis=2, keepdims=True))
        probs = jnp.exp(scores - log_total)
        probs_low = probs.astype(jnp.bfloat16)
        attended = jnp.einsum(
            "tqk,tkd->tqd", probs_low[..., :window_count], wvals, preferred_element_type=jnp.float32
        )
        attended = attended + jnp.einsum(
            "tqk,kd->tqd", probs_low[..., window_count:], gvals, preferred_element_type=jnp.float32
        )
        attended = lax.optimization_barrier(attended.astype(jnp.bfloat16))
        delta_rows = jnp.sum(grad_head.astype(jnp.float32) * attended.astype(jnp.float32), axis=2)
        dprob = jnp.concatenate(
            [
                jnp.einsum("tqd,tkd->tqk", grad_head, wvals, preferred_element_type=jnp.float32),
                jnp.einsum("tqd,kd->tqk", grad_head, gvals, preferred_element_type=jnp.float32),
            ],
            axis=2,
        )
        dscore = (probs * (dprob - delta_rows[..., None]) * factor).astype(jnp.bfloat16)
        grad_query = jnp.einsum(
            "tqk,tkd->tqd", dscore[..., :window_count], wkeys, preferred_element_type=jnp.float32
        )
        grad_query = grad_query + jnp.einsum(
            "tqk,kd->tqd", dscore[..., window_count:], gkeys, preferred_element_type=jnp.float32
        )
        window_dk = jnp.einsum(
            "tqk,tqd->tkd",
            dscore[..., :window_count],
            query_head,
            preferred_element_type=jnp.float32,
        )
        window_dv = jnp.einsum(
            "tqk,tqd->tkd",
            probs_low[..., :window_count],
            grad_head,
            preferred_element_type=jnp.float32,
        )
        global_dk = jnp.einsum(
            "tqk,tqd->kd",
            dscore[..., window_count:],
            query_head,
            preferred_element_type=jnp.float32,
        )
        global_dv = jnp.einsum(
            "tqk,tqd->kd",
            probs_low[..., window_count:],
            grad_head,
            preferred_element_type=jnp.float32,
        )
        return (grad_query, window_dk, window_dv, global_dk, global_dv)

    head_results = lax.map(head_block, jnp.arange(heads_here, dtype=jnp.int32))
    grad_query = jnp.moveaxis(head_results[0], 0, 2).reshape(tokens_here, width_here)
    window_dk = jnp.moveaxis(head_results[1], 0, 2).reshape(-1, width_here)
    window_dv = jnp.moveaxis(head_results[2], 0, 2).reshape(-1, width_here)
    global_dk = jnp.moveaxis(head_results[3], 0, 1).reshape(-1, width_here)
    global_dv = jnp.moveaxis(head_results[4], 0, 1).reshape(-1, width_here)
    window_grads = jnp.zeros((2, window_pair.shape[1], width_here), jnp.float32)
    window_grads = window_grads.at[:, window_rows.reshape(-1)].add(
        jnp.stack([window_dk, window_dv])
    )
    spread_grads = window_grads.reshape(2, 2 * REACH + 1, tokens_here, width_here)
    slots = [spread_grads[:, slot_index] for slot_index in range(2 * REACH + 1)]
    carried = slots[2 * REACH]
    for hop_index in range(2 * REACH):
        carried = (
            passed_along(carried.astype(jnp.bfloat16), "ctx", 1).astype(carried.dtype)
            + slots[2 * REACH - 1 - hop_index]
        )
    home_grads = passed_along(carried.astype(jnp.bfloat16), "ctx", -REACH).astype(carried.dtype)
    global_part = lax.psum_scatter(
        jnp.stack([global_dk, global_dv]), "ctx", scatter_dimension=1, tiled=True
    )
    home_grads = home_grads.at[:, own_rows].add(global_part)
    scaled_query = grad_query * query_gain
    scaled_key = home_grads[0] * key_gain
    query_dot, key_dot = lax.psum(
        (jnp.sum(scaled_query * query_rows, axis=1), jnp.sum(scaled_key * key_rows, axis=1)), "head"
    )
    query_grad = norm_grad(query_rows, query_inv, scaled_query, query_dot)
    key_grad = norm_grad(key_rows, key_inv, scaled_key, key_dot)
    return (query_grad, key_grad, home_grads[1].astype(jnp.bfloat16))


def solution(mesh):
    sizes = dict(mesh.shape)
    planes = sizes["ctx"] == GROUP * GROUP and sizes["head"] == 2
    return jax.shard_map(
        plane_body if planes else body,
        mesh=mesh,
        in_specs=(
            P("ctx", "head"),
            P("ctx", "head"),
            P("ctx", "head"),
            P("ctx", "head"),
            P("head"),
            P("head"),
            P("ctx", None),
            P("ctx"),
            P("ctx", None),
        ),
        out_specs=(P("ctx", "head"), P("ctx", "head"), P("ctx", "head")),
        check_vma=False,
    )
```

```python
import functools

import jax
import jax.numpy as jnp
from jax import lax
from jax.experimental import pallas as pl
from jax.experimental.pallas import tpu as pltpu
from jax.sharding import PartitionSpec as P

HEAD_DIM = 128
D = 5120
TILE = 128
REACH = 1
G_DEV = 2
GROUP = 4
CHUNKS = (2, 2, 1)
ORDER = ("b0 i0 g0 b1", "i1 e0 b2 g1", "i2 s0 e1 g2", "s1 e2 s2")


EPSILON = 1e-06
FACTOR = HEAD_DIM ** (-0.5)
LOG2_E = 1.4426950408889634
FACTS = 32
EXTRA = 16
F32 = jnp.float32
BF16 = jnp.bfloat16
ANY = pl.BlockSpec(memory_space=pl.ANY)
VMEM_LIMIT = 48 * 1024 * 1024


def swapped(shard, bit):
    count = lax.axis_size("ctx")
    return lax.ppermute(shard, "ctx", [(i, i ^ bit) for i in range(count)])


def swapped_edges(shard):
    count = lax.axis_size("ctx")
    pairs = [(i, i ^ 12) for i in range(count) if i // GROUP % GROUP in (1, 2)]
    return lax.ppermute(shard, "ctx", pairs)


def params():
    return pltpu.CompilerParams(vmem_limit_bytes=VMEM_LIMIT)


def cost(flops, read):
    return pl.CostEstimate(flops=1, bytes_accessed=1, transcendentals=0)


def behind(kernel, inputs, tokens):
    def run(*refs):
        kernel(*refs[:inputs], *refs[inputs + tokens :])

    return run


def contract(a, b, dims, precision=None):
    return lax.dot_general(
        a, b, (dims, ((), ())), precision=precision, preferred_element_type=F32
    )


def lane_pair(first, second, rows):
    lane = lax.broadcasted_iota(jnp.int32, (rows, HEAD_DIM), 1)
    return jnp.where(lane < HEAD_DIM // 2, first, second)


def squares_kernel(query_ref, key_ref, out_ref):
    step = pl.program_id(0)
    query = query_ref[...].astype(F32)
    key = key_ref[...].astype(F32)
    part = lane_pair(
        jnp.sum(query * query, axis=1, keepdims=True),
        jnp.sum(key * key, axis=1, keepdims=True),
        query.shape[0],
    )

    @pl.when(step == 0)
    def _():
        out_ref[...] = part

    @pl.when(step > 0)
    def _():
        out_ref[...] += part


def squares(query_raw, key_raw):
    rows, width = query_raw.shape
    block = width // 4
    return pl.pallas_call(
        squares_kernel,
        out_shape=jax.ShapeDtypeStruct((rows, HEAD_DIM), F32),
        grid=(4,),
        in_specs=[pl.BlockSpec((rows, block), lambda i: (0, i))] * 2,
        out_specs=pl.BlockSpec((rows, HEAD_DIM), lambda i: (0, 0)),
        compiler_params=params(),
        cost_estimate=cost(4 * rows * width, 4 * rows * width),
        name="squares",
    )(query_raw, key_raw)


def inverses(own, other):
    both = lax.rsqrt((own + other) / D + EPSILON)
    return both[:, :1], both[:, HEAD_DIM // 2 : HEAD_DIM // 2 + 1]


def rows_kernel(place_ref, ids_ref, own_ref, other_ref, key_ref, value_ref, gain_ref, *outs):
    rows = key_ref.shape[0]
    _, key_inv = inverses(own_ref[...], other_ref[...])
    device = place_ref[1] * GROUP + place_ref[0]
    row = lax.broadcasted_iota(jnp.int32, (16 * GROUP, rows), 0)
    col = lax.broadcasted_iota(jnp.int32, (16 * GROUP, rows), 1)
    is_key = jnp.zeros((16 * GROUP, rows), jnp.bool_)
    is_value = is_key
    for r in range(G_DEV):
        here = col == ids_ref[r] - device * rows
        for e in range(GROUP):
            is_key = is_key | (here & (row == 16 * e + 2 * e + r))
            is_value = is_value | (here & (row == 16 * e + 8 + 2 * e + r))
    is_key = is_key.astype(F32).astype(BF16)
    is_value = is_value.astype(F32).astype(BF16)
    key = key_ref[...]
    normed = (key.astype(F32) * key_inv * gain_ref[...]).astype(BF16)
    total = contract(is_key, normed, ((1,), (0,))) + contract(
        is_value, value_ref[...], ((1,), (0,))
    )
    for e in range(GROUP):
        outs[e][...] = total[16 * e : 16 * e + 16].astype(BF16)
    outs[GROUP][...] = contract(is_key[:16], key, ((1,), (0,))).astype(BF16)


def global_rows(place, ids, own, other, key_raw, values, key_gain):
    rows, width = key_raw.shape
    block = width // 4
    smem = pl.BlockSpec(memory_space=pltpu.SMEM)
    whole = pl.BlockSpec((rows, HEAD_DIM), lambda i: (0, 0))
    return pl.pallas_call(
        rows_kernel,
        out_shape=[jax.ShapeDtypeStruct((16, width), BF16)] * (GROUP + 1),
        grid=(4,),
        in_specs=[smem, smem, whole, whole]
        + [pl.BlockSpec((rows, block), lambda i: (0, i))] * 2
        + [pl.BlockSpec((1, block), lambda i: (0, i))],
        out_specs=[pl.BlockSpec((16, block), lambda i: (0, i))] * (GROUP + 1),
        compiler_params=params(),
        cost_estimate=cost(1, 1),
        name="global_rows",
    )(place, ids, own, other, key_raw, values, key_gain)


def pack_kernel(place_ref, tiles_ref, readers_ref, own_ref, other_ref, *refs):
    per = 6 + GROUP
    me, plane = place_ref[0], place_ref[1]
    query_inv, key_inv = inverses(own_ref[...], other_ref[...])
    rows = own_ref.shape[0]
    row = lax.broadcasted_iota(jnp.int32, (16, HEAD_DIM), 0)
    lane = lax.broadcasted_iota(jnp.int32, (16, HEAD_DIM), 1)
    facts = jnp.zeros((16, HEAD_DIM), jnp.int32)
    for tile in range(rows // TILE):
        start = tiles_ref[tile, 0] - (plane * GROUP - 1) * (rows // TILE)
        facts = jnp.where(row == 1 + tile, start, facts)
    for e in range(GROUP):
        for j in range(GROUP):
            live = readers_ref[0, (plane ^ e) * GROUP + j]
            chosen = (row == 0) & (lane // G_DEV == GROUP * j + e)
            facts = jnp.where(chosen, live, facts)
    facts = facts.astype(F32).astype(BF16)
    refs[-1][...] = jnp.zeros((8, HEAD_DIM), F32)
    for d in range(GROUP):
        key, value, query, grad, key_gain, query_gain, *parts = refs[per * d : per * d + per]
        out = refs[per * GROUP + d]
        out[0:rows] = (key[...].astype(F32) * key_inv * key_gain[...]).astype(BF16)
        out[rows : 2 * rows] = value[...]
        out[2 * rows : 3 * rows] = (
            query[...].astype(F32) * query_inv * query_gain[...]
        ).astype(BF16)
        out[3 * rows : 4 * rows] = grad[...]
        out[4 * rows : 4 * rows + 16] = facts
        out[4 * rows + 16 :] = sum(part[...].astype(F32) for part in parts).astype(BF16)


def pack(place, tiles, readers, own, other, arrays, gains, parts, first, count, after):
    query_raw, key_raw, values, out_grad = arrays
    query_gain, key_gain = gains
    rows, width = query_raw.shape
    each = width // HEAD_DIM // GROUP
    smem = pl.BlockSpec(memory_space=pltpu.SMEM)
    whole = pl.BlockSpec((rows, HEAD_DIM), lambda h, place: (0, 0))
    specs, operands = [], []
    for d in range(GROUP):
        at = lambda h, place, d=d: (0, (place[0] ^ d) * each + first + h)
        specs += [pl.BlockSpec((rows, HEAD_DIM), at)] * 4
        specs += [pl.BlockSpec((1, HEAD_DIM), at)] * 2
        specs += [pl.BlockSpec((16, HEAD_DIM), at)] * GROUP
        operands += [key_raw, values, query_raw, out_grad, key_gain, query_gain, *parts]
    out_rows = 4 * rows + FACTS
    return pl.pallas_call(
        behind(pack_kernel, 5 + len(specs), len(after)),
        out_shape=[jax.ShapeDtypeStruct((out_rows, count * HEAD_DIM), BF16)] * GROUP
        + [jax.ShapeDtypeStruct((8, HEAD_DIM), F32)],
        grid_spec=pltpu.PrefetchScalarGridSpec(
            num_scalar_prefetch=1,
            grid=(count,),
            in_specs=[smem, smem, whole, whole] + specs + [ANY] * len(after),
            out_specs=[pl.BlockSpec((out_rows, HEAD_DIM), lambda h, place: (0, h))] * GROUP
            + [pl.BlockSpec((8, HEAD_DIM), lambda h, place: (0, 0))],
        ),
        compiler_params=params(),
        cost_estimate=cost(1, 1),
        name="pack",
    )(place, tiles, readers, own, other, *operands, *after)


def edges_kernel(place_ref, b0, b1, b2, b3, near_ref, far_ref, token):
    me, plane = place_ref[0], place_ref[1]
    token[...] = jnp.zeros((8, HEAD_DIM), F32)
    even = plane % 2 == 0
    last, first = me ^ (GROUP - 1), me
    for d, block in enumerate((b0, b1, b2, b3)):

        @pl.when(jnp.where(even, last, first) == d)
        def _(block=block):
            near_ref[...] = block[...]

        @pl.when(jnp.where(even, first, last) == d)
        def _(block=block):
            far_ref[...] = block[...]


def edges(place, blocks, after):
    out_rows, width = blocks[0].shape
    rows = (out_rows - FACTS) // 4
    whole = pl.BlockSpec((2 * rows, width), lambda i, place: (0, 0))
    return pl.pallas_call(
        behind(edges_kernel, 1 + GROUP, len(after)),
        out_shape=[jax.ShapeDtypeStruct((2 * rows, width), BF16)] * 2
        + [jax.ShapeDtypeStruct((8, HEAD_DIM), F32)],
        grid_spec=pltpu.PrefetchScalarGridSpec(
            num_scalar_prefetch=1,
            grid=(1,),
            in_specs=[whole] * GROUP + [ANY] * len(after),
            out_specs=[whole] * 2 + [pl.BlockSpec((8, HEAD_DIM), lambda i, place: (0, 0))],
        ),
        compiler_params=params(),
        cost_estimate=cost(1, 1),
        name="edges",
    )(place, *blocks, *after)


def attend_kernel(outer, place_ref, b0, b1, b2, b3, *refs):
    if outer:
        near, far, dq_out, acc_out, g_out, near_out, far_out = refs[:7]
    else:
        dq_out, acc_out, g_out = refs[:3]
    pair, weights, sums, raw_g, pair_g, sums_g, facts_at = refs[-7:]
    me, plane = place_ref[0], place_ref[1]
    rows = (b0.shape[0] - FACTS) // 4
    tiles = rows // TILE
    keys = slice(0, HEAD_DIM)
    vals = slice(HEAD_DIM, 2 * HEAD_DIM)

    @pl.when(pl.program_id(0) == 0)
    def _():
        weights[...] = jnp.zeros_like(weights)

    for d, block in enumerate((b0, b1, b2, b3)):
        j = me ^ d
        at = pl.multiple_of((j + 1) * rows, TILE)
        pair[pl.ds(at, rows), keys] = block[0:rows]
        pair[pl.ds(at, rows), vals] = block[rows : 2 * rows]
        for tile in range(tiles):
            here = 2 * rows + tile * TILE
            weights[j * tiles + tile, :TILE, keys] = block[here : here + TILE]
            weights[j * tiles + tile, TILE:, vals] = block[here + rows : here + rows + TILE]
        facts_at[j] = block[4 * rows : 4 * rows + 16].astype(F32)
        extra = block[4 * rows + 16 :].astype(F32)
        eight = pl.ds(pl.multiple_of(8 * j, 8), 8)
        raw_g[eight, keys] = extra[:8]
        raw_g[eight, vals] = extra[8:]
    pair_g[...] = raw_g[...].astype(BF16)
    if outer:
        even = plane % 2 == 0
        top = (GROUP + 1) * rows
        near_at = pl.multiple_of(jnp.where(even, top, 0), TILE)
        far_at = pl.multiple_of(jnp.where(even, 0, top), TILE)
        for ref, at in ((near, near_at), (far, far_at)):
            pair[pl.ds(at, rows), keys] = ref[0:rows]
            pair[pl.ds(at, rows), vals] = ref[rows : 2 * rows]
    sums[...] = jnp.zeros_like(sums)
    sums_g[...] = jnp.zeros_like(sums_g)
    count_g = pair_g.shape[0]
    row = lax.broadcasted_iota(jnp.int32, (count_g, HEAD_DIM), 0)
    lane = lax.broadcasted_iota(jnp.int32, (count_g, HEAD_DIM), 1)
    span = 4 * TILE
    units = []
    for j in (0, GROUP - 1) if outer else range(1, GROUP - 1):
        facts = facts_at[j]
        live = jnp.sum(jnp.where(row == lane, facts[0:1], 0.0), axis=1, keepdims=True) > 0.0
        for tile in range(tiles):
            start = jnp.max(facts[1 + tile : 2 + tile]).astype(jnp.int32)
            units.append((j * tiles + tile, pl.multiple_of(start * TILE, TILE), live))

    def products(unit):
        weight, at, _ = units[unit]
        both = jnp.concatenate([pair[pl.ds(at, span)], pair_g[...]], axis=0)
        return contract(both, weights[weight], ((1,), (1,)))

    ahead = products(0)
    for unit, (weight, at, live) in enumerate(units):
        product = ahead
        if unit + 1 < len(units):
            ahead = products(unit + 1)
        score = product[:, :TILE] * (FACTOR * LOG2_E)
        dprob = product[:, TILE:]
        score_g = jnp.where(live, score[span:], -jnp.inf)
        score = jnp.concatenate([score[:span], score_g], axis=0)
        largest = jnp.max(score, axis=0, keepdims=True)
        probs = jnp.exp2(score - largest)
        probs = probs * (1.0 / jnp.sum(probs, axis=0, keepdims=True))
        delta = jnp.sum(probs * dprob, axis=0, keepdims=True)
        dscore = (probs * ((dprob - delta) * FACTOR)).astype(BF16)
        grads = contract(
            jnp.concatenate([dscore, probs.astype(BF16)], axis=1), weights[weight], ((1,), (0,))
        )
        sums[pl.ds(at, span)] += grads[:span]
        sums_g[...] += grads[span:]
        both = jnp.concatenate([pair[pl.ds(at, span), keys], pair_g[:, keys]], axis=0)
        grad_query = contract(dscore, both, ((0,), (0,)))
        dq_out[unit * TILE : (unit + 1) * TILE] = grad_query.astype(BF16)
    acc_out[...] = sums[rows : (GROUP + 1) * rows].astype(BF16)
    g_out[...] = sums_g[...]
    if outer:
        for out, at in ((near_out, near_at), (far_out, far_at)):
            out[:rows] = sums[pl.ds(at, rows), keys].astype(BF16)
            out[rows : 2 * rows] = sums[pl.ds(at, rows), vals].astype(BF16)


def attend(place, blocks, halo, after):
    out_rows, width = blocks[0].shape
    rows = (out_rows - FACTS) // 4
    at = lambda h, place: (0, h)
    tall = pl.BlockSpec((out_rows, HEAD_DIM), at)
    edge = pl.BlockSpec((2 * rows, HEAD_DIM), at)
    wide = 2 * HEAD_DIM
    edge_shape = jax.ShapeDtypeStruct((2 * rows, width), BF16)
    return pl.pallas_call(
        behind(
            functools.partial(attend_kernel, len(halo) > 0), 1 + GROUP + len(halo), len(after)
        ),
        out_shape=[
            edge_shape,
            jax.ShapeDtypeStruct((GROUP * rows, 2 * width), BF16),
            jax.ShapeDtypeStruct((8 * GROUP, 2 * width), F32),
        ]
        + [edge_shape] * len(halo),
        grid_spec=pltpu.PrefetchScalarGridSpec(
            num_scalar_prefetch=1,
            grid=(width // HEAD_DIM,),
            in_specs=[tall] * GROUP + [edge] * len(halo) + [ANY] * len(after),
            out_specs=[
                edge,
                pl.BlockSpec((GROUP * rows, wide), at),
                pl.BlockSpec((8 * GROUP, wide), at),
            ]
            + [edge] * len(halo),
            scratch_shapes=[
                pltpu.VMEM(((GROUP + 2) * rows, wide), BF16),
                pltpu.VMEM((GROUP * rows // TILE, 2 * TILE, wide), BF16),
                pltpu.VMEM(((GROUP + 2) * rows, wide), F32),
                pltpu.VMEM((8 * GROUP, wide), F32),
                pltpu.VMEM((8 * GROUP, wide), BF16),
                pltpu.VMEM((8 * GROUP, wide), F32),
                pltpu.VMEM((GROUP, 16, HEAD_DIM), F32),
            ],
        ),
        compiler_params=params(),
        cost_estimate=cost(1, 1),
        name="outer" if halo else "inner",
    )(place, *blocks, *halo, *after)


def settle_kernel(
    place_ref, dq_in, acc_in, g_in, dq_out, acc_out, g_out, near, far, o0, o1, o2, o3, token,
    total_g,
):
    me, plane = place_ref[0], place_ref[1]
    token[...] = jnp.zeros((8, HEAD_DIM), F32)
    rows = dq_in.shape[0] // 2
    even = plane % 2 == 0
    inner = (plane == 1) | (plane == 2)
    total_g[...] = g_in[...] + g_out[...]
    for d, out in enumerate((o0, o1, o2, o3)):
        j = me ^ d
        near_here = j == jnp.where(even, GROUP - 1, 0)
        far_here = (j == jnp.where(even, 0, GROUP - 1)) & inner
        outside = (j == 0) | (j == GROUP - 1)

        @pl.when(outside)
        def _(out=out, j=j):
            out[:rows] = dq_out[pl.ds(pl.multiple_of(jnp.where(j == 0, 0, rows), TILE), rows)]

        @pl.when(~outside)
        def _(out=out, j=j):
            out[:rows] = dq_in[pl.ds(pl.multiple_of(jnp.where(j == 1, 0, rows), TILE), rows)]

        here = pl.ds(pl.multiple_of(j * rows, TILE), rows)
        for i in range(2):
            lanes = slice(i * HEAD_DIM, (i + 1) * HEAD_DIM)
            rest = slice(i * rows, (i + 1) * rows)
            total = acc_in[here, lanes].astype(F32) + acc_out[here, lanes].astype(F32)
            total = total + jnp.where(near_here, near[rest].astype(F32), 0.0)
            total = total + jnp.where(far_here, far[rest].astype(F32), 0.0)
            out[(i + 1) * rows : (i + 2) * rows] = total.astype(BF16)
        eight = pl.ds(pl.multiple_of(8 * j, 8), 8)
        both = total_g[eight]
        out[3 * rows :] = jnp.concatenate(
            [both[:, :HEAD_DIM], both[:, HEAD_DIM:]], axis=0
        ).astype(BF16)


def settle(place, inner, outer, near, far, after):
    rows, width = inner[0].shape
    rows = rows // 2
    at = lambda h, place: (0, h)
    wide = 2 * HEAD_DIM
    edge = pl.BlockSpec((2 * rows, HEAD_DIM), at)
    part = [edge, pl.BlockSpec((GROUP * rows, wide), at), pl.BlockSpec((8 * GROUP, wide), at)]
    return pl.pallas_call(
        behind(settle_kernel, 9, len(after)),
        out_shape=[jax.ShapeDtypeStruct((3 * rows + EXTRA, width), BF16)] * GROUP
        + [jax.ShapeDtypeStruct((8, HEAD_DIM), F32)],
        grid_spec=pltpu.PrefetchScalarGridSpec(
            num_scalar_prefetch=1,
            grid=(width // HEAD_DIM,),
            in_specs=part * 2 + [edge] * 2 + [ANY] * len(after),
            out_specs=[pl.BlockSpec((3 * rows + EXTRA, HEAD_DIM), at)] * GROUP
            + [pl.BlockSpec((8, HEAD_DIM), lambda h, place: (0, 0))],
            scratch_shapes=[pltpu.VMEM((8 * GROUP, wide), F32)],
        ),
        compiler_params=params(),
        cost_estimate=cost(1, 1),
        name="settle",
    )(place, *inner, *outer, near, far, *after)


def collect_kernel(chunks, place_ref, *refs):
    me = place_ref[0]
    out = refs[-1]
    each = out.shape[1] // GROUP
    for d in range(GROUP):
        first = 0
        for c, count in enumerate(chunks):
            at = pl.multiple_of((me ^ d) * each + first * HEAD_DIM, HEAD_DIM)
            out[:, pl.ds(at, count * HEAD_DIM)] = refs[c * GROUP + d][...]
            first += count


def collect(place, grads, width, chunks):
    flat = [x for chunk in grads for x in chunk]
    return pl.pallas_call(
        functools.partial(collect_kernel, chunks),
        out_shape=jax.ShapeDtypeStruct((EXTRA, width), BF16),
        grid_spec=pltpu.PrefetchScalarGridSpec(
            num_scalar_prefetch=1,
            grid=(1,),
            in_specs=[
                pl.BlockSpec(
                    (EXTRA, x.shape[1]),
                    lambda i, place, n=x.shape[0] // EXTRA - 1: (n, 0),
                )
                for x in flat
            ],
            out_specs=pl.BlockSpec((EXTRA, width), lambda i, place: (0, 0)),
        ),
        compiler_params=params(),
        cost_estimate=cost(1, 1),
        name="collect",
    )(place, *flat)


def global_sum(parts, row):
    return sum(
        part[row + 2 * e : row + 2 * e + 1].astype(F32) for e, part in enumerate(parts)
    )


def total_kernel(place_ref, ids_ref, raw_ref, gain_ref, p0, p1, p2, p3, *refs):
    out = refs[-1]
    rows = out.shape[0]
    device = place_ref[1] * GROUP + place_ref[0]
    total = refs[0][...]
    for ref in refs[1:-1]:
        total = total + ref[...]
    row = lax.broadcasted_iota(jnp.int32, (rows, HEAD_DIM), 0)
    lane = lax.broadcasted_iota(jnp.int32, (rows, HEAD_DIM), 1)
    parts = [p[...] for p in (p0, p1, p2, p3)]
    for r in range(G_DEV):
        raw = raw_ref[...].astype(F32)[r : r + 1]
        dot = jnp.sum(global_sum(parts, r) * gain_ref[...] * raw, axis=1, keepdims=True)
        here = (row == ids_ref[r] - device * rows) & (lane >= HEAD_DIM // 2)
        total = total + jnp.where(here, dot, 0.0)
    out[...] = total


def total_dots(place, ids, raw, gain, parts, dots):
    smem = pl.BlockSpec(memory_space=pltpu.SMEM)
    vmem = pl.BlockSpec(memory_space=pltpu.VMEM)
    return pl.pallas_call(
        total_kernel,
        out_shape=jax.ShapeDtypeStruct(dots[0].shape, F32),
        in_specs=[smem, smem] + [vmem] * (2 + GROUP + len(dots)),
        out_specs=vmem,
        compiler_params=params(),
        cost_estimate=cost(1, 1),
        name="total_dots",
    )(place, ids, raw, gain, *parts, *dots)


def dots_kernel(place_ref, *refs):
    out_ref = refs[-1]
    rows = out_ref.shape[0]
    step = pl.program_id(0)
    totals = [jnp.zeros((rows, HEAD_DIM), F32), jnp.zeros((rows, HEAD_DIM), F32)]
    for d in range(GROUP):
        grads, query, key, query_gain, key_gain = refs[5 * d : 5 * d + 5]
        totals[0] += grads[:rows].astype(F32) * query_gain[...] * query[...].astype(F32)
        totals[1] += grads[rows:].astype(F32) * key_gain[...] * key[...].astype(F32)
    part = lane_pair(
        jnp.sum(totals[0], axis=1, keepdims=True), jnp.sum(totals[1], axis=1, keepdims=True), rows
    )

    @pl.when(step == 0)
    def _():
        out_ref[...] = part

    @pl.when(step > 0)
    def _():
        out_ref[...] += part


def dots(place, grads, query_raw, key_raw, gains, first, after):
    rows, full = query_raw.shape
    count = grads[0].shape[1] // HEAD_DIM
    each = full // HEAD_DIM // GROUP
    specs, operands = [], []
    for d in range(GROUP):
        at = lambda h, place, d=d: (0, (place[0] ^ d) * each + first + h)
        specs += (
            [pl.BlockSpec((2 * rows, HEAD_DIM), lambda h, place: (0, h))]
            + [pl.BlockSpec((rows, HEAD_DIM), at)] * 2
            + [pl.BlockSpec((1, HEAD_DIM), at)] * 2
        )
        operands += [grads[d], query_raw, key_raw, gains[0], gains[1]]
    return pl.pallas_call(
        behind(dots_kernel, 1 + 5 * GROUP, len(after)),
        out_shape=jax.ShapeDtypeStruct((rows, HEAD_DIM), F32),
        grid_spec=pltpu.PrefetchScalarGridSpec(
            num_scalar_prefetch=1,
            grid=(count,),
            in_specs=specs + [ANY] * len(after),
            out_specs=pl.BlockSpec((rows, HEAD_DIM), lambda h, place: (0, 0)),
        ),
        compiler_params=params(),
        cost_estimate=cost(1, 16 * rows * count * HEAD_DIM * 2),
        name="dots",
    )(place, *operands, *after)


def finish_kernel(chunks, place_ref, ids_ref, own_ref, other_ref, dot_ref, dot_other_ref, *refs):
    me = place_ref[0]
    device = place_ref[1] * GROUP + me
    p0, p1, p2, p3, *refs = refs
    grads = refs[: GROUP * len(chunks)]
    query_ref, key_ref, query_gain, key_gain = refs[GROUP * len(chunks) : GROUP * len(chunks) + 4]
    query_out, key_out, value_out = refs[GROUP * len(chunks) + 4 :]
    rows, full = query_ref.shape
    each = full // GROUP
    inv = inverses(own_ref[...], other_ref[...])
    total = dot_ref[...] + dot_other_ref[...]
    dot = (total[:, :1], total[:, HEAD_DIM // 2 : HEAD_DIM // 2 + 1])
    coeff = [inv[i] * inv[i] * inv[i] * (dot[i] / D) for i in range(2)]
    row = lax.broadcasted_iota(jnp.int32, (rows, HEAD_DIM), 0)
    hot = [row == ids_ref[r] - device * rows for r in range(G_DEV)]
    for d in range(GROUP):
        first = 0
        for c, count in enumerate(chunks):
            ref = grads[c * GROUP + d]
            for h in range(count):
                at = pl.multiple_of((me ^ d) * each + (first + h) * HEAD_DIM, HEAD_DIM)
                here = pl.ds(at, HEAD_DIM)
                col = slice(h * HEAD_DIM, (h + 1) * HEAD_DIM)
                parts = [p[:, here] for p in (p0, p1, p2, p3)]
                grad = [ref[i * rows : (i + 1) * rows, col].astype(F32) for i in range(3)]
                for i in (1, 2):
                    for r in range(G_DEV):
                        more = global_sum(parts, 8 * (i - 1) + r)
                        grad[i] = grad[i] + jnp.where(hot[r], more, 0.0)
                for i, (raw, gain, out) in enumerate(
                    ((query_ref, query_gain, query_out), (key_ref, key_gain, key_out))
                ):
                    out[:, here] = (
                        inv[i] * (grad[i] * gain[:, here]) - raw[:, here].astype(F32) * coeff[i]
                    ).astype(BF16)
                value_out[:, here] = grad[2].astype(BF16)
            first += count


def finish(place, ids, own, other, dot, dot_other, parts, grads, query_raw, key_raw, gains, chunks):
    vmem = pl.BlockSpec(memory_space=pltpu.VMEM)
    smem = pl.BlockSpec(memory_space=pltpu.SMEM)
    flat = [x for chunk in grads for x in chunk]
    return pl.pallas_call(
        functools.partial(finish_kernel, chunks),
        out_shape=[jax.ShapeDtypeStruct(query_raw.shape, BF16)] * 3,
        in_specs=[smem, smem] + [vmem] * (4 + GROUP + len(flat) + 4),
        out_specs=[vmem] * 3,
        compiler_params=params(),
        cost_estimate=cost(1, 1),
        name="finish",
    )(place, ids, own, other, dot, dot_other, *parts, *flat, query_raw, key_raw, *gains)


def swap_heads(x):
    return lax.ppermute(x, "head", [(0, 1), (1, 0)])


def plane_body(
    query_raw, key_raw, values, out_grad, query_gain, key_gain, key_tiles, global_ids, readers
):
    device = lax.axis_index("ctx")
    place = jnp.stack([device % GROUP, device // GROUP]).astype(jnp.int32)
    gains = (query_gain[None, :], key_gain[None, :])
    own = squares(query_raw, key_raw)
    other = swap_heads(own)
    arrays = (query_raw, key_raw, values, out_grad)
    *sent, raw_rows = global_rows(place, global_ids, own, other, key_raw, values, gains[1])
    parts = [sent[0]] + [swapped(sent[e], 4 * e) for e in range(1, GROUP)]
    chunks = len(CHUNKS)
    firsts = [sum(CHUNKS[:c]) for c in range(chunks)]
    packed, token = [], ()
    for first, count in zip(firsts, CHUNKS):
        *sent, last = pack(
            place, key_tiles, readers, own, other, arrays, gains, parts, first, count, token
        )
        token = (last,)
        packed.append([sent[0]] + [swapped(sent[d], d) for d in range(1, GROUP)])
    edge, inner, outer, back, home, dot = ({} for _ in range(6))

    def begin(c, token):
        near, far, last = edges(place, packed[c], token)
        edge[c] = (swapped(near, 4), swapped_edges(far))
        return (last,)

    def inside(c, token):
        inner[c] = attend(place, packed[c], (), token)
        return (inner[c][2],)

    def outside(c, token):
        *outer[c], near, far = attend(place, packed[c], edge[c], token)
        back[c] = (swapped(near, 4), swapped_edges(far))
        return (outer[c][2],)

    def end(c, token):
        *sent, last = settle(place, inner[c], outer[c], *back[c], token)
        home[c] = [sent[0]] + [swapped(sent[d], d) for d in range(1, GROUP)]
        return (last,)

    def score(c, token):
        dot[c] = dots(place, home[c], query_raw, key_raw, gains, firsts[c], token)
        return (dot[c],)

    stages = {"b": begin, "i": inside, "g": outside, "e": end, "s": score}
    for step in " ".join(ORDER).split():
        name, *extra = step.split(":")
        held = tuple((packed if e[0] == "i" else home)[int(e[1])]["oxyd".index(e[2])] for e in extra)
        token = stages[name[0]](int(name[1]), token + held)
    homes = [home[c] for c in range(chunks)]
    mine = collect(place, homes, query_raw.shape[1], CHUNKS)
    parts = [mine] + [swapped(mine, 4 * e) for e in range(1, GROUP)]
    total = total_dots(
        place, global_ids, raw_rows, gains[1], parts, [dot[c] for c in range(chunks)]
    )
    return tuple(
        finish(
            place, global_ids, own, other, total, swap_heads(total), parts, homes,
            query_raw, key_raw, gains, CHUNKS,
        )
    )


def passed_along(shard, axis, by):
    count = lax.axis_size(axis)
    return lax.ppermute(shard, axis, [(i, (i + by) % count) for i in range(count)])


def normalize(as_float, gain, squares):
    inverse = lax.rsqrt(squares[:, None] / D + EPSILON)
    return (inverse, (as_float * inverse * gain).astype(jnp.bfloat16))


def norm_grad(as_float, inverse, scaled, coeffs):
    return (inverse * scaled - as_float * inverse**3 * (coeffs[:, None] / D)).astype(jnp.bfloat16)


def body(
    query_raw, key_raw, values, out_grad, query_gain, key_gain, key_tiles, global_ids, readers
):
    tokens_here, width_here = query_raw.shape
    heads_here = width_here // HEAD_DIM
    tiles_here = tokens_here // TILE
    factor = HEAD_DIM ** (-0.5)
    device = lax.axis_index("ctx")
    query_rows = query_raw.astype(jnp.float32)
    key_rows = key_raw.astype(jnp.float32)
    query_sq, key_sq = lax.psum(
        (jnp.sum(query_rows * query_rows, axis=1), jnp.sum(key_rows * key_rows, axis=1)), "head"
    )
    query_inv, query_norm = normalize(query_rows, query_gain, query_sq)
    key_inv, key_norm = normalize(key_rows, key_gain, key_sq)
    own_rows = global_ids - device * tokens_here
    own_pair = jnp.stack([key_norm[own_rows], values[own_rows]])
    global_pair = lax.all_gather(own_pair, "ctx", axis=1, tiled=True)
    global_keys = global_pair[0].reshape(-1, heads_here, HEAD_DIM)
    global_vals = global_pair[1].reshape(-1, heads_here, HEAD_DIM)
    live_mask = jnp.repeat(readers[0] > 0, G_DEV)
    key_value = jnp.stack([key_norm, values])
    current = passed_along(key_value, "ctx", -REACH)
    pieces = [current]
    for hop_index in range(2 * REACH):
        current = passed_along(current, "ctx", 1)
        pieces.append(current)
    pieces = pieces[::-1]
    window_pair = jnp.concatenate(pieces, axis=1)
    first_tile = (device - REACH) * tiles_here
    local_tiles = key_tiles - first_tile
    window_rows = (
        local_tiles[:, :, None] * TILE + jnp.arange(TILE, dtype=jnp.int32)[None, None, :]
    ).reshape(tiles_here, -1)
    window_count = window_rows.shape[1]
    window_keys = window_pair[0][window_rows].reshape(
        tiles_here, window_count, heads_here, HEAD_DIM
    )
    window_vals = window_pair[1][window_rows].reshape(
        tiles_here, window_count, heads_here, HEAD_DIM
    )
    query_four = query_norm.reshape(tiles_here, TILE, heads_here, HEAD_DIM)
    grad_four = out_grad.reshape(tiles_here, TILE, heads_here, HEAD_DIM)

    def head_block(head_number):
        query_head = lax.dynamic_index_in_dim(query_four, head_number, 2, keepdims=False)
        grad_head = lax.dynamic_index_in_dim(grad_four, head_number, 2, keepdims=False)
        wkeys = lax.dynamic_index_in_dim(window_keys, head_number, 2, keepdims=False)
        wvals = lax.dynamic_index_in_dim(window_vals, head_number, 2, keepdims=False)
        gkeys = lax.dynamic_index_in_dim(global_keys, head_number, 1, keepdims=False)
        gvals = lax.dynamic_index_in_dim(global_vals, head_number, 1, keepdims=False)
        score_window = (
            jnp.einsum("tqd,tkd->tqk", query_head, wkeys, preferred_element_type=jnp.float32)
            * factor
        )
        score_global = (
            jnp.einsum("tqd,kd->tqk", query_head, gkeys, preferred_element_type=jnp.float32)
            * factor
        )
        score_global = jnp.where(live_mask, score_global, -jnp.inf)
        scores = jnp.concatenate([score_window, score_global], axis=2)
        largest = jnp.max(scores, axis=2, keepdims=True)
        log_total = largest + jnp.log(jnp.sum(jnp.exp(scores - largest), axis=2, keepdims=True))
        probs = jnp.exp(scores - log_total)
        probs_low = probs.astype(jnp.bfloat16)
        attended = jnp.einsum(
            "tqk,tkd->tqd", probs_low[..., :window_count], wvals, preferred_element_type=jnp.float32
        )
        attended = attended + jnp.einsum(
            "tqk,kd->tqd", probs_low[..., window_count:], gvals, preferred_element_type=jnp.float32
        )
        attended = lax.optimization_barrier(attended.astype(jnp.bfloat16))
        delta_rows = jnp.sum(grad_head.astype(jnp.float32) * attended.astype(jnp.float32), axis=2)
        dprob = jnp.concatenate(
            [
                jnp.einsum("tqd,tkd->tqk", grad_head, wvals, preferred_element_type=jnp.float32),
                jnp.einsum("tqd,kd->tqk", grad_head, gvals, preferred_element_type=jnp.float32),
            ],
            axis=2,
        )
        dscore = (probs * (dprob - delta_rows[..., None]) * factor).astype(jnp.bfloat16)
        grad_query = jnp.einsum(
            "tqk,tkd->tqd", dscore[..., :window_count], wkeys, preferred_element_type=jnp.float32
        )
        grad_query = grad_query + jnp.einsum(
            "tqk,kd->tqd", dscore[..., window_count:], gkeys, preferred_element_type=jnp.float32
        )
        window_dk = jnp.einsum(
            "tqk,tqd->tkd",
            dscore[..., :window_count],
            query_head,
            preferred_element_type=jnp.float32,
        )
        window_dv = jnp.einsum(
            "tqk,tqd->tkd",
            probs_low[..., :window_count],
            grad_head,
            preferred_element_type=jnp.float32,
        )
        global_dk = jnp.einsum(
            "tqk,tqd->kd",
            dscore[..., window_count:],
            query_head,
            preferred_element_type=jnp.float32,
        )
        global_dv = jnp.einsum(
            "tqk,tqd->kd",
            probs_low[..., window_count:],
            grad_head,
            preferred_element_type=jnp.float32,
        )
        return (grad_query, window_dk, window_dv, global_dk, global_dv)

    head_results = lax.map(head_block, jnp.arange(heads_here, dtype=jnp.int32))
    grad_query = jnp.moveaxis(head_results[0], 0, 2).reshape(tokens_here, width_here)
    window_dk = jnp.moveaxis(head_results[1], 0, 2).reshape(-1, width_here)
    window_dv = jnp.moveaxis(head_results[2], 0, 2).reshape(-1, width_here)
    global_dk = jnp.moveaxis(head_results[3], 0, 1).reshape(-1, width_here)
    global_dv = jnp.moveaxis(head_results[4], 0, 1).reshape(-1, width_here)
    window_grads = jnp.zeros((2, window_pair.shape[1], width_here), jnp.float32)
    window_grads = window_grads.at[:, window_rows.reshape(-1)].add(
        jnp.stack([window_dk, window_dv])
    )
    spread_grads = window_grads.reshape(2, 2 * REACH + 1, tokens_here, width_here)
    slots = [spread_grads[:, slot_index] for slot_index in range(2 * REACH + 1)]
    carried = slots[2 * REACH]
    for hop_index in range(2 * REACH):
        carried = (
            passed_along(carried.astype(jnp.bfloat16), "ctx", 1).astype(carried.dtype)
            + slots[2 * REACH - 1 - hop_index]
        )
    home_grads = passed_along(carried.astype(jnp.bfloat16), "ctx", -REACH).astype(carried.dtype)
    global_part = lax.psum_scatter(
        jnp.stack([global_dk, global_dv]), "ctx", scatter_dimension=1, tiled=True
    )
    home_grads = home_grads.at[:, own_rows].add(global_part)
    scaled_query = grad_query * query_gain
    scaled_key = home_grads[0] * key_gain
    query_dot, key_dot = lax.psum(
        (jnp.sum(scaled_query * query_rows, axis=1), jnp.sum(scaled_key * key_rows, axis=1)), "head"
    )
    query_grad = norm_grad(query_rows, query_inv, scaled_query, query_dot)
    key_grad = norm_grad(key_rows, key_inv, scaled_key, key_dot)
    return (query_grad, key_grad, home_grads[1].astype(jnp.bfloat16))


def solution(mesh):
    sizes = dict(mesh.shape)
    planes = sizes["ctx"] == GROUP * GROUP and sizes["head"] == 2
    return jax.shard_map(
        plane_body if planes else body,
        mesh=mesh,
        in_specs=(
            P("ctx", "head"),
            P("ctx", "head"),
            P("ctx", "head"),
            P("ctx", "head"),
            P("head"),
            P("head"),
            P("ctx", None),
            P("ctx"),
            P("ctx", None),
        ),
        out_specs=(P("ctx", "head"), P("ctx", "head"), P("ctx", "head")),
        check_vma=False,
    )
```

```python
import functools

import jax
import jax.numpy as jnp
from jax import lax
from jax.experimental import pallas as pl
from jax.experimental.pallas import tpu as pltpu
from jax.sharding import PartitionSpec as P

HEAD_DIM = 128
D = 5120
TILE = 128
REACH = 1
G_DEV = 2
GROUP = 4
CHUNKS = (2, 2, 1)
ORDER = ("b0 i0 g0 b1", "i1 e0 b2 g1", "i2 s0 e1 g2", "s1 e2 s2")


EPSILON = 1e-06
FACTOR = HEAD_DIM ** (-0.5)
LOG2_E = 1.4426950408889634
FACTS = 32
F32 = jnp.float32
BF16 = jnp.bfloat16
ANY = pl.BlockSpec(memory_space=pl.ANY)
VMEM_LIMIT = 48 * 1024 * 1024


def swapped(shard, bit):
    count = lax.axis_size("ctx")
    return lax.ppermute(shard, "ctx", [(i, i ^ bit) for i in range(count)])


def swapped_edges(shard):
    count = lax.axis_size("ctx")
    pairs = [(i, i ^ 12) for i in range(count) if i // GROUP % GROUP in (1, 2)]
    return lax.ppermute(shard, "ctx", pairs)


def params():
    return pltpu.CompilerParams(vmem_limit_bytes=VMEM_LIMIT)


def cost(flops, read):
    return pl.CostEstimate(flops=1, bytes_accessed=1, transcendentals=0)


def behind(kernel, inputs, tokens):
    def run(*refs):
        kernel(*refs[:inputs], *refs[inputs + tokens :])

    return run


def heads_call(kernel, count, place, inputs, outputs, after=(), scratch=(), name=None):
    widths = [w for _, w in inputs] + [w for _, w in outputs]

    def run(place_ref, *refs):
        refs = refs[: len(inputs)] + refs[len(inputs) + len(after) :]
        for h in range(count):
            views = [
                ref.at[:, h * w : (h + 1) * w] if w else ref for ref, w in zip(refs, widths)
            ]
            kernel(h, place_ref, *views, *refs[len(widths) :])

    vmem = pl.BlockSpec(memory_space=pltpu.VMEM)
    return pl.pallas_call(
        run,
        out_shape=[shape for shape, _ in outputs],
        in_specs=[pl.BlockSpec(memory_space=pltpu.SMEM)]
        + [vmem] * len(inputs)
        + [ANY] * len(after),
        out_specs=[vmem] * len(outputs),
        scratch_shapes=scratch,
        compiler_params=params(),
        cost_estimate=cost(1, 1),
        name=name,
    )(place, *[x for x, _ in inputs], *after)


def contract(a, b, dims, precision=None):
    return lax.dot_general(
        a, b, (dims, ((), ())), precision=precision, preferred_element_type=F32
    )


def lane_pair(first, second, rows):
    lane = lax.broadcasted_iota(jnp.int32, (rows, HEAD_DIM), 1)
    return jnp.where(lane < HEAD_DIM // 2, first, second)


def squares_kernel(query_ref, key_ref, out_ref):
    rows, width = query_ref.shape
    step = rows // 4
    for at in range(0, rows, step):
        part = []
        for ref in (query_ref, key_ref):
            x = ref[at : at + step].astype(F32)
            part.append(jnp.sum(x * x, axis=1, keepdims=True))
        out_ref[at : at + step] = lane_pair(*part, step)


def squares(query_raw, key_raw):
    rows, width = query_raw.shape
    vmem = pl.BlockSpec(memory_space=pltpu.VMEM)
    return pl.pallas_call(
        squares_kernel,
        out_shape=jax.ShapeDtypeStruct((rows, HEAD_DIM), F32),
        in_specs=[vmem] * 2,
        out_specs=vmem,
        compiler_params=params(),
        cost_estimate=cost(1, 1),
        name="squares",
    )(query_raw, key_raw)


def inverses(own, other):
    both = lax.rsqrt((own + other) / D + EPSILON)
    return both[:, :1], both[:, HEAD_DIM // 2 : HEAD_DIM // 2 + 1]


def rows_kernel(place_ref, ids_ref, own_ref, other_ref, key_ref, value_ref, gain_ref, out, raw):
    rows, width = key_ref.shape
    block = width // GROUP
    device = place_ref[1] * GROUP + place_ref[0]
    row = lax.broadcasted_iota(jnp.int32, (16, width), 0)
    keys, found, vals = [], [], []
    for r in range(G_DEV):
        at = ids_ref[r] - device * rows
        base = pl.multiple_of(at // 16 * 16, 16)
        here = pl.ds(base, 16)
        _, inv = inverses(own_ref[here], other_ref[here])
        hot = row == at - base

        def only(x):
            return jnp.sum(jnp.where(hot, x, 0.0), axis=0, keepdims=True)

        key = key_ref[here].astype(F32)
        keys.append(only(key))
        found.append(only((key * inv * gain_ref[...]).astype(BF16).astype(F32)))
        vals.append(only(value_ref[here].astype(F32)))
    raw[...] = jnp.where(row == 0, keys[0], keys[1]).astype(BF16)
    total = jnp.zeros((16, block), F32)
    row = lax.broadcasted_iota(jnp.int32, (16, block), 0)
    for g in range(GROUP):
        for i, x in enumerate(found + vals):
            total = jnp.where(row == 4 * g + i, x[:, g * block : (g + 1) * block], total)
    out[...] = total.astype(BF16)


def global_rows(place, ids, own, other, key_raw, values, key_gain):
    rows, width = key_raw.shape
    smem = pl.BlockSpec(memory_space=pltpu.SMEM)
    vmem = pl.BlockSpec(memory_space=pltpu.VMEM)
    return pl.pallas_call(
        rows_kernel,
        out_shape=[
            jax.ShapeDtypeStruct((16, width // GROUP), BF16),
            jax.ShapeDtypeStruct((16, width), BF16),
        ],
        in_specs=[smem, smem] + [vmem] * 5,
        out_specs=[vmem] * 2,
        compiler_params=params(),
        cost_estimate=cost(1, 1),
        name="global_rows",
    )(place, ids, own, other, key_raw, values, key_gain)


def pack_kernel(first, place_ref, tiles_ref, readers_ref, own_ref, other_ref, *refs):
    me, plane = place_ref[0], place_ref[1]
    query_inv, key_inv = inverses(own_ref[...], other_ref[...])
    rows = own_ref.shape[0]
    row = lax.broadcasted_iota(jnp.int32, (16, HEAD_DIM), 0)
    lane = lax.broadcasted_iota(jnp.int32, (16, HEAD_DIM), 1)
    facts = jnp.zeros((16, HEAD_DIM), jnp.int32)
    for tile in range(rows // TILE):
        start = tiles_ref[tile, 0] - (plane * GROUP - 1) * (rows // TILE)
        facts = jnp.where(row == 1 + tile, start, facts)
    for e in range(GROUP):
        for j in range(GROUP):
            live = readers_ref[0, (plane ^ e) * GROUP + j]
            chosen = (row == 0) & (lane // G_DEV == GROUP * j + e)
            facts = jnp.where(chosen, live, facts)
    facts = facts.astype(F32).astype(BF16)
    key_ref, value_ref, query_ref, grad_ref, key_gain, query_gain = refs[:6]
    *outs, token = refs[6 + GROUP :]
    token[...] = jnp.zeros((8, HEAD_DIM), F32)
    parts = jnp.concatenate([ref[...] for ref in refs[6 : 6 + GROUP]], axis=0)
    row = lax.broadcasted_iota(jnp.int32, (16, 16 * GROUP), 0)
    col = lax.broadcasted_iota(jnp.int32, (16, 16 * GROUP), 1)
    each = key_ref.shape[1] // HEAD_DIM // GROUP
    for d, out in enumerate(outs):
        spot = col % 16 - 4 * (me ^ d)
        hot = (spot >= 0) & (spot < 4)
        hot = hot & (row == 2 * (col // 16) + spot % 2 + 8 * (spot // 2))
        hot = hot.astype(F32).astype(BF16)
        chosen = parts[:, first * HEAD_DIM : first * HEAD_DIM + out.shape[1]]
        out[4 * rows + 16 :] = contract(hot, chosen, ((1,), (0,))).astype(BF16)
        for h in range(out.shape[1] // HEAD_DIM):
            at = pl.multiple_of(((me ^ d) * each + first + h) * HEAD_DIM, HEAD_DIM)
            here = pl.ds(at, HEAD_DIM)
            lanes = slice(h * HEAD_DIM, (h + 1) * HEAD_DIM)
            key = key_ref[:, here].astype(F32)
            query = query_ref[:, here].astype(F32)
            out[0:rows, lanes] = (key * key_inv * key_gain[:, here]).astype(BF16)
            out[rows : 2 * rows, lanes] = value_ref[:, here]
            out[2 * rows : 3 * rows, lanes] = (query * query_inv * query_gain[:, here]).astype(BF16)
            out[3 * rows : 4 * rows, lanes] = grad_ref[:, here]
            out[4 * rows : 4 * rows + 16, lanes] = facts


def pack(place, tiles, readers, own, other, arrays, gains, parts, first, count, after):
    query_raw, key_raw, values, out_grad = arrays
    query_gain, key_gain = gains
    rows, width = query_raw.shape
    smem = pl.BlockSpec(memory_space=pltpu.SMEM)
    vmem = pl.BlockSpec(memory_space=pltpu.VMEM)
    out_rows = 4 * rows + FACTS
    kernel = functools.partial(pack_kernel, first)
    return pl.pallas_call(
        behind(kernel, 11 + GROUP, len(after)),
        out_shape=[jax.ShapeDtypeStruct((out_rows, count * HEAD_DIM), BF16)] * GROUP
        + [jax.ShapeDtypeStruct((8, HEAD_DIM), F32)],
        in_specs=[smem] * 3 + [vmem] * (8 + GROUP) + [ANY] * len(after),
        out_specs=[vmem] * (GROUP + 1),
        compiler_params=params(),
        cost_estimate=cost(1, 1),
        name="pack",
    )(
        place, tiles, readers, own, other, key_raw, values, query_raw, out_grad,
        key_gain, query_gain, *parts, *after,
    )


def edges_kernel(head, place_ref, b0, b1, b2, b3, near_ref, far_ref, token):
    me, plane = place_ref[0], place_ref[1]
    token[...] = jnp.zeros((8, HEAD_DIM), F32)
    even = plane % 2 == 0
    last, first = me ^ (GROUP - 1), me
    for d, block in enumerate((b0, b1, b2, b3)):

        @pl.when(jnp.where(even, last, first) == d)
        def _(block=block):
            near_ref[...] = block[: near_ref.shape[0]]

        @pl.when(jnp.where(even, first, last) == d)
        def _(block=block):
            far_ref[...] = block[: far_ref.shape[0]]


def edges(place, blocks, after):
    out_rows, width = blocks[0].shape
    rows = (out_rows - FACTS) // 4
    half = jax.ShapeDtypeStruct((2 * rows, width), BF16)
    return heads_call(
        edges_kernel,
        1,
        place,
        [(block, 0) for block in blocks],
        [(half, 0), (half, 0), (jax.ShapeDtypeStruct((8, HEAD_DIM), F32), 0)],
        after,
        name="edges",
    )


def attend_kernel(outer, head, place_ref, b0, b1, b2, b3, *refs):
    if outer:
        near, far, g_in, dq_out, acc_out, g_out, near_out, far_out, mid_out, end_out = refs[:10]
    else:
        dq_out, acc_out, g_out = refs[:3]
    pair, weights, sums, raw_g, pair_g, sums_g, facts_at = refs[-7:]
    me, plane = place_ref[0], place_ref[1]
    rows = (b0.shape[0] - FACTS) // 4
    tiles = rows // TILE
    keys = slice(0, HEAD_DIM)
    vals = slice(HEAD_DIM, 2 * HEAD_DIM)

    if head == 0:
        weights[...] = jnp.zeros_like(weights)

    for d, block in enumerate((b0, b1, b2, b3)):
        j = me ^ d
        at = pl.multiple_of((j + 1) * rows, TILE)
        pair[pl.ds(at, rows), keys] = block[0:rows]
        pair[pl.ds(at, rows), vals] = block[rows : 2 * rows]
        for tile in range(tiles):
            here = 2 * rows + tile * TILE
            weights[j * tiles + tile, :TILE, keys] = block[here : here + TILE]
            weights[j * tiles + tile, TILE:, vals] = block[here + rows : here + rows + TILE]
        facts_at[j] = block[4 * rows : 4 * rows + 16].astype(F32)
        extra = block[4 * rows + 16 :].astype(F32)
        eight = pl.ds(pl.multiple_of(8 * j, 8), 8)
        raw_g[eight, keys] = extra[:8]
        raw_g[eight, vals] = extra[8:]
    pair_g[...] = raw_g[...].astype(BF16)
    if outer:
        even = plane % 2 == 0
        top = (GROUP + 1) * rows
        near_at = pl.multiple_of(jnp.where(even, top, 0), TILE)
        far_at = pl.multiple_of(jnp.where(even, 0, top), TILE)
        for ref, at in ((near, near_at), (far, far_at)):
            pair[pl.ds(at, rows), keys] = ref[0:rows]
            pair[pl.ds(at, rows), vals] = ref[rows : 2 * rows]
    sums[...] = jnp.zeros_like(sums)
    sums_g[...] = jnp.zeros_like(sums_g)
    count_g = pair_g.shape[0]
    row = lax.broadcasted_iota(jnp.int32, (count_g, HEAD_DIM), 0)
    lane = lax.broadcasted_iota(jnp.int32, (count_g, HEAD_DIM), 1)
    span = 4 * TILE
    units = []
    for j in (0, GROUP - 1) if outer else range(1, GROUP - 1):
        facts = facts_at[j]
        live = jnp.sum(jnp.where(row == lane, facts[0:1], 0.0), axis=1, keepdims=True) > 0.0
        for tile in range(tiles):
            start = jnp.max(facts[1 + tile : 2 + tile]).astype(jnp.int32)
            units.append((j * tiles + tile, pl.multiple_of(start * TILE, TILE), live))

    def products(unit):
        weight, at, _ = units[unit]
        both = jnp.concatenate([pair[pl.ds(at, span)], pair_g[...]], axis=0)
        return contract(both, weights[weight], ((1,), (1,)))

    ahead = products(0)
    for unit, (weight, at, live) in enumerate(units):
        product = ahead
        if unit + 1 < len(units):
            ahead = products(unit + 1)
        score = product[:, :TILE] * (FACTOR * LOG2_E)
        dprob = product[:, TILE:]
        score_g = jnp.where(live, score[span:], -jnp.inf)
        score = jnp.concatenate([score[:span], score_g], axis=0)
        largest = jnp.max(score, axis=0, keepdims=True)
        probs = jnp.exp2(score - largest)
        probs = probs * (1.0 / jnp.sum(probs, axis=0, keepdims=True))
        delta = jnp.sum(probs * dprob, axis=0, keepdims=True)
        dscore = (probs * ((dprob - delta) * FACTOR)).astype(BF16)
        grads = contract(
            jnp.concatenate([dscore, probs.astype(BF16)], axis=1), weights[weight], ((1,), (0,))
        )
        sums[pl.ds(at, span)] += grads[:span]
        sums_g[...] += grads[span:]
        both = jnp.concatenate([pair[pl.ds(at, span), keys], pair_g[:, keys]], axis=0)
        grad_query = contract(dscore, both, ((0,), (0,)))
        dq_out[unit * TILE : (unit + 1) * TILE] = grad_query.astype(BF16)
    acc_out[...] = sums[rows : (GROUP + 1) * rows].astype(BF16)
    if not outer:
        g_out[...] = sums_g[...]
    else:
        total_g = (g_in[...] + sums_g[...]).astype(BF16)
        row = lax.broadcasted_iota(jnp.int32, (8, 8 * GROUP), 0)
        col = lax.broadcasted_iota(jnp.int32, (8, 8 * GROUP), 1)
        for e, out in enumerate((g_out, near_out, mid_out, end_out)):
            hot = (col // 8 == row // G_DEV) & (col % 8 == G_DEV * e + row % G_DEV)
            part = contract(hot.astype(F32).astype(BF16), total_g, ((1,), (0,)))
            out[out.shape[0] - 16 :] = jnp.concatenate([part[:, keys], part[:, vals]], axis=0).astype(
                BF16
            )
        for out, at in ((near_out, near_at), (far_out, far_at)):
            out[:rows] = sums[pl.ds(at, rows), keys].astype(BF16)
            out[rows : 2 * rows] = sums[pl.ds(at, rows), vals].astype(BF16)


def attend(place, blocks, halo, inner_g, after):
    out_rows, width = blocks[0].shape
    rows = (out_rows - FACTS) // 4
    wide = 2 * HEAD_DIM
    half = jax.ShapeDtypeStruct((2 * rows, width), BF16)
    few = jax.ShapeDtypeStruct((16, width), BF16)
    near = jax.ShapeDtypeStruct((2 * rows + 16, width), BF16)
    outs = [(half, HEAD_DIM), (jax.ShapeDtypeStruct((GROUP * rows, 2 * width), BF16), wide)]
    if halo:
        outs += [(x, HEAD_DIM) for x in (few, near, half, few, few)]
    else:
        outs += [(jax.ShapeDtypeStruct((8 * GROUP, 2 * width), F32), wide)]
    return heads_call(
        functools.partial(attend_kernel, len(halo) > 0),
        width // HEAD_DIM,
        place,
        [(x, HEAD_DIM) for x in (*blocks, *halo)] + [(x, wide) for x in inner_g],
        outs,
        after,
        [
            pltpu.VMEM(((GROUP + 2) * rows, wide), BF16),
            pltpu.VMEM((GROUP * rows // TILE, 2 * TILE, wide), BF16),
            pltpu.VMEM(((GROUP + 2) * rows, wide), F32),
            pltpu.VMEM((8 * GROUP, wide), F32),
            pltpu.VMEM((8 * GROUP, wide), BF16),
            pltpu.VMEM((8 * GROUP, wide), F32),
            pltpu.VMEM((GROUP, 16, HEAD_DIM), F32),
        ],
        name="outer" if halo else "inner",
    )


def settle_kernel(
    head, place_ref, dq_in, acc_in, dq_out, acc_out, own_g, near, far, *refs
):
    *more, o0, o1, o2, o3, token = refs
    me, plane = place_ref[0], place_ref[1]
    token[...] = jnp.zeros((8, HEAD_DIM), F32)
    rows = dq_in.shape[0] // 2
    even = plane % 2 == 0
    inner = (plane == 1) | (plane == 2)
    part = (own_g[...].astype(F32) + near[2 * rows :].astype(F32)).astype(BF16)
    if more and head == 0:
        rest_g = (more[0][...].astype(F32) + more[1][...].astype(F32)).astype(BF16)
    for d, out in enumerate((o0, o1, o2, o3)):
        j = me ^ d
        near_here = j == jnp.where(even, GROUP - 1, 0)
        far_here = (j == jnp.where(even, 0, GROUP - 1)) & inner
        outside = (j == 0) | (j == GROUP - 1)

        @pl.when(outside)
        def _(out=out, j=j):
            out[:rows] = dq_out[pl.ds(pl.multiple_of(jnp.where(j == 0, 0, rows), TILE), rows)]

        @pl.when(~outside)
        def _(out=out, j=j):
            out[:rows] = dq_in[pl.ds(pl.multiple_of(jnp.where(j == 1, 0, rows), TILE), rows)]

        here = pl.ds(pl.multiple_of(j * rows, TILE), rows)
        for i in range(2):
            lanes = slice(i * HEAD_DIM, (i + 1) * HEAD_DIM)
            rest = slice(i * rows, (i + 1) * rows)
            total = acc_in[here, lanes].astype(F32) + acc_out[here, lanes].astype(F32)
            total = total + jnp.where(near_here, near[rest].astype(F32), 0.0)
            total = total + jnp.where(far_here, far[rest].astype(F32), 0.0)
            out[(i + 1) * rows : (i + 2) * rows] = total.astype(BF16)
        out[3 * rows : 3 * rows + 16] = part
        if more and head == 0:
            for h in range(rest_g.shape[1] // HEAD_DIM):
                at = 3 * rows + 16 * (h + 1)
                out[at : at + 16] = rest_g[:, h * HEAD_DIM : (h + 1) * HEAD_DIM]


def settle(place, inner, outer, own_g, near, far, more, after):
    rows, width = inner[0].shape
    rows = rows // 2
    part = (HEAD_DIM, 2 * HEAD_DIM)
    extra = 16 + 16 * (more[0].shape[1] // HEAD_DIM if more else 0)
    home = jax.ShapeDtypeStruct((3 * rows + extra, width), BF16)
    return heads_call(
        settle_kernel,
        width // HEAD_DIM,
        place,
        [*zip(inner, part), *zip(outer, part)]
        + [(x, HEAD_DIM) for x in (own_g, near, far)]
        + [(x, 0) for x in more],
        [(home, HEAD_DIM)] * GROUP + [(jax.ShapeDtypeStruct((8, HEAD_DIM), F32), 0)],
        after,
        name="settle",
    )


def join_kernel(head, place_ref, *refs):
    *parts, mid, end = refs
    half = len(parts) // 2
    for out, some in ((mid, parts[:half]), (end, parts[half:])):
        first = 0
        for part in some:
            out[:, first : first + part.shape[1]] = part[...]
            first += part.shape[1]


def join(place, mids, ends):
    shape = jax.ShapeDtypeStruct((16, sum(x.shape[1] for x in mids)), BF16)
    return heads_call(
        join_kernel,
        1,
        place,
        [(x, 0) for x in (*mids, *ends)],
        [(shape, 0), (shape, 0)],
        name="join",
    )


def total_kernel(chunks, place_ref, ids_ref, raw_ref, gain_ref, *refs):
    *refs, out, sums = refs
    homes, dot_refs = refs[: GROUP * len(chunks)], refs[GROUP * len(chunks) :]
    rows, width = out.shape[0], sums.shape[1]
    me = place_ref[0]
    device = place_ref[1] * GROUP + me
    total = dot_refs[0][...]
    for ref in dot_refs[1:]:
        total = total + ref[...]
    few = lax.broadcasted_iota(jnp.int32, (16, HEAD_DIM), 0)
    eight = lax.broadcasted_iota(jnp.int32, (8, HEAD_DIM), 0)
    hot = [few == 8 * i + G_DEV * me + r for i in range(2) for r in range(G_DEV)]
    dot = [jnp.zeros((1, HEAD_DIM), F32) for _ in range(G_DEV)]
    for d in range(GROUP):
        first = 0
        for c, count in enumerate(chunks):
            for h in range(count):
                home = homes[c * GROUP + d]
                last = homes[(len(chunks) - 1) * GROUP + d]
                at = 3 * rows + 16 * (first + h + 1)
                part = home[3 * rows : 3 * rows + 16, h * HEAD_DIM : (h + 1) * HEAD_DIM].astype(F32)
                part = part + last[at : at + 16, :HEAD_DIM].astype(F32)
                found = [jnp.sum(jnp.where(x, part, 0.0), axis=0, keepdims=True) for x in hot]
                at = pl.multiple_of(
                    (me ^ d) * (width // GROUP) + (first + h) * HEAD_DIM, HEAD_DIM
                )
                here = pl.ds(at, HEAD_DIM)
                block = jnp.zeros((8, HEAD_DIM), F32)
                for i, x in enumerate(found):
                    block = jnp.where(eight == i, x, block)
                sums[:, here] = block
                raw = raw_ref[:, here].astype(F32)
                for r in range(G_DEV):
                    dot[r] = dot[r] + found[r] * gain_ref[:, here] * raw[r : r + 1]
            first += count
    row = lax.broadcasted_iota(jnp.int32, (rows, HEAD_DIM), 0)
    lane = lax.broadcasted_iota(jnp.int32, (rows, HEAD_DIM), 1)
    for r in range(G_DEV):
        here = (row == ids_ref[r] - device * rows) & (lane >= HEAD_DIM // 2)
        total = total + jnp.where(here, jnp.sum(dot[r], axis=1, keepdims=True), 0.0)
    out[...] = total


def total_dots(place, ids, raw, gain, homes, dots, chunks):
    smem = pl.BlockSpec(memory_space=pltpu.SMEM)
    vmem = pl.BlockSpec(memory_space=pltpu.VMEM)
    flat = [x for home in homes for x in home]
    return pl.pallas_call(
        functools.partial(total_kernel, chunks),
        out_shape=[
            jax.ShapeDtypeStruct(dots[0].shape, F32),
            jax.ShapeDtypeStruct((8, raw.shape[1]), F32),
        ],
        in_specs=[smem, smem] + [vmem] * (2 + len(flat) + len(dots)),
        out_specs=[vmem, vmem],
        compiler_params=params(),
        cost_estimate=cost(1, 1),
        name="total_dots",
    )(place, ids, raw, gain, *flat, *dots)


def dots_kernel(first, head, place_ref, g0, g1, g2, g3, query, key, query_gain, key_gain, out_ref):
    rows = out_ref.shape[0]
    each = query.shape[1] // HEAD_DIM // GROUP
    totals = [jnp.zeros((rows, HEAD_DIM), F32), jnp.zeros((rows, HEAD_DIM), F32)]
    for d, grads in enumerate((g0, g1, g2, g3)):
        for h in range(grads.shape[1] // HEAD_DIM):
            at = ((place_ref[0] ^ d) * each + first + h) * HEAD_DIM
            here = pl.ds(pl.multiple_of(at, HEAD_DIM), HEAD_DIM)
            lanes = slice(h * HEAD_DIM, (h + 1) * HEAD_DIM)
            for i, (raw, gain) in enumerate(((query, query_gain), (key, key_gain))):
                grad = grads[i * rows : (i + 1) * rows, lanes].astype(F32)
                totals[i] += grad * gain[:, here] * raw[:, here].astype(F32)
    out_ref[...] = lane_pair(
        jnp.sum(totals[0], axis=1, keepdims=True), jnp.sum(totals[1], axis=1, keepdims=True), rows
    )


def dots(place, grads, query_raw, key_raw, gains, first, after):
    return heads_call(
        functools.partial(dots_kernel, first),
        1,
        place,
        [(x, 0) for x in (*grads, query_raw, key_raw, *gains)],
        [(jax.ShapeDtypeStruct((query_raw.shape[0], HEAD_DIM), F32), 0)],
        after,
        name="dots",
    )[0]


def finish_kernel(chunks, place_ref, ids_ref, own_ref, other_ref, dot_ref, dot_other_ref, *refs):
    device = place_ref[1] * GROUP + place_ref[0]
    grads = refs[: GROUP * len(chunks)]
    sum_ref, query_ref, key_ref, query_gain, key_gain = refs[GROUP * len(chunks) : -3]
    query_out, key_out, value_out = refs[-3:]
    rows = query_ref.shape[0]
    each = query_ref.shape[1] // GROUP
    inv = inverses(own_ref[...], other_ref[...])
    total = dot_ref[...] + dot_other_ref[...]
    dot = (total[:, :1], total[:, HEAD_DIM // 2 : HEAD_DIM // 2 + 1])
    coeff = [inv[i] * inv[i] * inv[i] * (dot[i] / D) for i in range(2)]
    row = lax.broadcasted_iota(jnp.int32, (rows, HEAD_DIM), 0)
    hot = [row == ids_ref[r] - device * rows for r in range(G_DEV)]

    def whole(d):
        first = 0
        for c, count in enumerate(chunks):
            ref = grads[c * GROUP + d]
            for h in range(count):
                at = (first + h) * HEAD_DIM
                there = slice(at, at + HEAD_DIM)
                at = pl.multiple_of((place_ref[0] ^ d) * each + at, HEAD_DIM)
                here = pl.ds(at, HEAD_DIM)
                col = slice(h * HEAD_DIM, (h + 1) * HEAD_DIM)
                grad = [ref[i * rows : (i + 1) * rows, col].astype(F32) for i in range(3)]
                for i in (1, 2):
                    for r in range(G_DEV):
                        more = sum_ref[2 * (i - 1) + r : 2 * (i - 1) + r + 1, here]
                        grad[i] = grad[i] + jnp.where(hot[r], more, 0.0)
                for i, (raw, gain, out) in enumerate(
                    ((query_ref, query_gain, query_out), (key_ref, key_gain, key_out))
                ):
                    out[:, there] = (
                        inv[i] * (grad[i] * gain[:, here]) - raw[:, here].astype(F32) * coeff[i]
                    ).astype(BF16)
                value_out[:, there] = grad[2].astype(BF16)
            first += count

    for d in range(GROUP):
        pl.when(pl.program_id(0) == d)(functools.partial(whole, d))


def finish(place, ids, own, other, dot, dot_other, sums, grads, query_raw, key_raw, gains, chunks):
    rows, width = query_raw.shape
    block = width // GROUP
    smem = pl.BlockSpec(memory_space=pltpu.SMEM)
    at = lambda i, place: (0, place[0] ^ i)
    vmem = pl.BlockSpec(memory_space=pltpu.VMEM)
    flat = [x for chunk in grads for x in chunk]
    column = pl.BlockSpec((rows, block), at)
    return pl.pallas_call(
        functools.partial(finish_kernel, chunks),
        out_shape=[jax.ShapeDtypeStruct(query_raw.shape, BF16)] * 3,
        grid_spec=pltpu.PrefetchScalarGridSpec(
            num_scalar_prefetch=1,
            grid=(GROUP,),
            in_specs=[smem] + [vmem] * (4 + len(flat) + 5),
            out_specs=[column] * 3,
        ),
        compiler_params=params(),
        cost_estimate=cost(1, 1),
        name="finish",
    )(place, ids, own, other, dot, dot_other, *flat, sums, query_raw, key_raw, *gains)


def swap_heads(x):
    return lax.ppermute(x, "head", [(0, 1), (1, 0)])


def plane_body(
    query_raw, key_raw, values, out_grad, query_gain, key_gain, key_tiles, global_ids, readers
):
    device = lax.axis_index("ctx")
    place = jnp.stack([device % GROUP, device // GROUP]).astype(jnp.int32)
    gains = (query_gain[None, :], key_gain[None, :])
    own = squares(query_raw, key_raw)
    other = swap_heads(own)
    arrays = (query_raw, key_raw, values, out_grad)
    mine, raw_rows = global_rows(place, global_ids, own, other, key_raw, values, gains[1])
    parts = [mine] + [swapped(mine, 4 * e) for e in range(1, GROUP)]
    chunks = len(CHUNKS)
    firsts = [sum(CHUNKS[:c]) for c in range(chunks)]
    packed, token = [], ()
    for first, count in zip(firsts, CHUNKS):
        *sent, last = pack(
            place, key_tiles, readers, own, other, arrays, gains, parts, first, count, token
        )
        token = (last,)
        packed.append([sent[0]] + [swapped(sent[d], d) for d in range(1, GROUP)])
    edge, inner, outer, back, home, dot = ({} for _ in range(6))
    fars = []

    def begin(c, token):
        near, far, last = edges(place, packed[c], token)
        edge[c] = (swapped(near, 4), swapped_edges(far))
        return (last,)

    def inside(c, token):
        inner[c] = attend(place, packed[c], (), (), token)
        return (inner[c][2],)

    def outside(c, token):
        results = attend(place, packed[c], edge[c], (inner[c][2],), token)
        outer[c], own_g, near, far, mid, last = results[:2], *results[2:]
        fars.append((mid, last))
        more = ()
        if c == chunks - 1:
            mids, lasts = zip(*fars)
            mid, last = join(place, mids, lasts)
            more = (swapped(mid, 8), swapped(last, 12))
        back[c] = (own_g, swapped(near, 4), swapped_edges(far), more)
        return (own_g,)

    def end(c, token):
        *sent, last = settle(place, inner[c][:2], outer[c], *back[c], token)
        home[c] = [sent[0]] + [swapped(sent[d], d) for d in range(1, GROUP)]
        return (last,)

    def score(c, token):
        dot[c] = dots(place, home[c], query_raw, key_raw, gains, firsts[c], token)
        return (dot[c],)

    stages = {"b": begin, "i": inside, "g": outside, "e": end, "s": score}
    for step in " ".join(ORDER).split():
        name, *extra = step.split(":")
        held = tuple((packed if e[0] == "i" else home)[int(e[1])]["oxyd".index(e[2])] for e in extra)
        token = stages[name[0]](int(name[1]), token + held)
    homes = [home[c] for c in range(chunks)]
    total, sums = total_dots(
        place, global_ids, raw_rows, gains[1], homes, [dot[c] for c in range(chunks)], CHUNKS
    )
    return tuple(
        finish(
            place, global_ids, own, other, total, swap_heads(total), sums, homes,
            query_raw, key_raw, gains, CHUNKS,
        )
    )


def passed_along(shard, axis, by):
    count = lax.axis_size(axis)
    return lax.ppermute(shard, axis, [(i, (i + by) % count) for i in range(count)])


def normalize(as_float, gain, squares):
    inverse = lax.rsqrt(squares[:, None] / D + EPSILON)
    return (inverse, (as_float * inverse * gain).astype(jnp.bfloat16))


def norm_grad(as_float, inverse, scaled, coeffs):
    return (inverse * scaled - as_float * inverse**3 * (coeffs[:, None] / D)).astype(jnp.bfloat16)


def body(
    query_raw, key_raw, values, out_grad, query_gain, key_gain, key_tiles, global_ids, readers
):
    tokens_here, width_here = query_raw.shape
    heads_here = width_here // HEAD_DIM
    tiles_here = tokens_here // TILE
    factor = HEAD_DIM ** (-0.5)
    device = lax.axis_index("ctx")
    query_rows = query_raw.astype(jnp.float32)
    key_rows = key_raw.astype(jnp.float32)
    query_sq, key_sq = lax.psum(
        (jnp.sum(query_rows * query_rows, axis=1), jnp.sum(key_rows * key_rows, axis=1)), "head"
    )
    query_inv, query_norm = normalize(query_rows, query_gain, query_sq)
    key_inv, key_norm = normalize(key_rows, key_gain, key_sq)
    own_rows = global_ids - device * tokens_here
    own_pair = jnp.stack([key_norm[own_rows], values[own_rows]])
    global_pair = lax.all_gather(own_pair, "ctx", axis=1, tiled=True)
    global_keys = global_pair[0].reshape(-1, heads_here, HEAD_DIM)
    global_vals = global_pair[1].reshape(-1, heads_here, HEAD_DIM)
    live_mask = jnp.repeat(readers[0] > 0, G_DEV)
    key_value = jnp.stack([key_norm, values])
    current = passed_along(key_value, "ctx", -REACH)
    pieces = [current]
    for hop_index in range(2 * REACH):
        current = passed_along(current, "ctx", 1)
        pieces.append(current)
    pieces = pieces[::-1]
    window_pair = jnp.concatenate(pieces, axis=1)
    first_tile = (device - REACH) * tiles_here
    local_tiles = key_tiles - first_tile
    window_rows = (
        local_tiles[:, :, None] * TILE + jnp.arange(TILE, dtype=jnp.int32)[None, None, :]
    ).reshape(tiles_here, -1)
    window_count = window_rows.shape[1]
    window_keys = window_pair[0][window_rows].reshape(
        tiles_here, window_count, heads_here, HEAD_DIM
    )
    window_vals = window_pair[1][window_rows].reshape(
        tiles_here, window_count, heads_here, HEAD_DIM
    )
    query_four = query_norm.reshape(tiles_here, TILE, heads_here, HEAD_DIM)
    grad_four = out_grad.reshape(tiles_here, TILE, heads_here, HEAD_DIM)

    def head_block(head_number):
        query_head = lax.dynamic_index_in_dim(query_four, head_number, 2, keepdims=False)
        grad_head = lax.dynamic_index_in_dim(grad_four, head_number, 2, keepdims=False)
        wkeys = lax.dynamic_index_in_dim(window_keys, head_number, 2, keepdims=False)
        wvals = lax.dynamic_index_in_dim(window_vals, head_number, 2, keepdims=False)
        gkeys = lax.dynamic_index_in_dim(global_keys, head_number, 1, keepdims=False)
        gvals = lax.dynamic_index_in_dim(global_vals, head_number, 1, keepdims=False)
        score_window = (
            jnp.einsum("tqd,tkd->tqk", query_head, wkeys, preferred_element_type=jnp.float32)
            * factor
        )
        score_global = (
            jnp.einsum("tqd,kd->tqk", query_head, gkeys, preferred_element_type=jnp.float32)
            * factor
        )
        score_global = jnp.where(live_mask, score_global, -jnp.inf)
        scores = jnp.concatenate([score_window, score_global], axis=2)
        largest = jnp.max(scores, axis=2, keepdims=True)
        log_total = largest + jnp.log(jnp.sum(jnp.exp(scores - largest), axis=2, keepdims=True))
        probs = jnp.exp(scores - log_total)
        probs_low = probs.astype(jnp.bfloat16)
        attended = jnp.einsum(
            "tqk,tkd->tqd", probs_low[..., :window_count], wvals, preferred_element_type=jnp.float32
        )
        attended = attended + jnp.einsum(
            "tqk,kd->tqd", probs_low[..., window_count:], gvals, preferred_element_type=jnp.float32
        )
        attended = lax.optimization_barrier(attended.astype(jnp.bfloat16))
        delta_rows = jnp.sum(grad_head.astype(jnp.float32) * attended.astype(jnp.float32), axis=2)
        dprob = jnp.concatenate(
            [
                jnp.einsum("tqd,tkd->tqk", grad_head, wvals, preferred_element_type=jnp.float32),
                jnp.einsum("tqd,kd->tqk", grad_head, gvals, preferred_element_type=jnp.float32),
            ],
            axis=2,
        )
        dscore = (probs * (dprob - delta_rows[..., None]) * factor).astype(jnp.bfloat16)
        grad_query = jnp.einsum(
            "tqk,tkd->tqd", dscore[..., :window_count], wkeys, preferred_element_type=jnp.float32
        )
        grad_query = grad_query + jnp.einsum(
            "tqk,kd->tqd", dscore[..., window_count:], gkeys, preferred_element_type=jnp.float32
        )
        window_dk = jnp.einsum(
            "tqk,tqd->tkd",
            dscore[..., :window_count],
            query_head,
            preferred_element_type=jnp.float32,
        )
        window_dv = jnp.einsum(
            "tqk,tqd->tkd",
            probs_low[..., :window_count],
            grad_head,
            preferred_element_type=jnp.float32,
        )
        global_dk = jnp.einsum(
            "tqk,tqd->kd",
            dscore[..., window_count:],
            query_head,
            preferred_element_type=jnp.float32,
        )
        global_dv = jnp.einsum(
            "tqk,tqd->kd",
            probs_low[..., window_count:],
            grad_head,
            preferred_element_type=jnp.float32,
        )
        return (grad_query, window_dk, window_dv, global_dk, global_dv)

    head_results = lax.map(head_block, jnp.arange(heads_here, dtype=jnp.int32))
    grad_query = jnp.moveaxis(head_results[0], 0, 2).reshape(tokens_here, width_here)
    window_dk = jnp.moveaxis(head_results[1], 0, 2).reshape(-1, width_here)
    window_dv = jnp.moveaxis(head_results[2], 0, 2).reshape(-1, width_here)
    global_dk = jnp.moveaxis(head_results[3], 0, 1).reshape(-1, width_here)
    global_dv = jnp.moveaxis(head_results[4], 0, 1).reshape(-1, width_here)
    window_grads = jnp.zeros((2, window_pair.shape[1], width_here), jnp.float32)
    window_grads = window_grads.at[:, window_rows.reshape(-1)].add(
        jnp.stack([window_dk, window_dv])
    )
    spread_grads = window_grads.reshape(2, 2 * REACH + 1, tokens_here, width_here)
    slots = [spread_grads[:, slot_index] for slot_index in range(2 * REACH + 1)]
    carried = slots[2 * REACH]
    for hop_index in range(2 * REACH):
        carried = (
            passed_along(carried.astype(jnp.bfloat16), "ctx", 1).astype(carried.dtype)
            + slots[2 * REACH - 1 - hop_index]
        )
    home_grads = passed_along(carried.astype(jnp.bfloat16), "ctx", -REACH).astype(carried.dtype)
    global_part = lax.psum_scatter(
        jnp.stack([global_dk, global_dv]), "ctx", scatter_dimension=1, tiled=True
    )
    home_grads = home_grads.at[:, own_rows].add(global_part)
    scaled_query = grad_query * query_gain
    scaled_key = home_grads[0] * key_gain
    query_dot, key_dot = lax.psum(
        (jnp.sum(scaled_query * query_rows, axis=1), jnp.sum(scaled_key * key_rows, axis=1)), "head"
    )
    query_grad = norm_grad(query_rows, query_inv, scaled_query, query_dot)
    key_grad = norm_grad(key_rows, key_inv, scaled_key, key_dot)
    return (query_grad, key_grad, home_grads[1].astype(jnp.bfloat16))


def solution(mesh):
    sizes = dict(mesh.shape)
    planes = sizes["ctx"] == GROUP * GROUP and sizes["head"] == 2
    return jax.shard_map(
        plane_body if planes else body,
        mesh=mesh,
        in_specs=(
            P("ctx", "head"),
            P("ctx", "head"),
            P("ctx", "head"),
            P("ctx", "head"),
            P("head"),
            P("head"),
            P("ctx", None),
            P("ctx"),
            P("ctx", None),
        ),
        out_specs=(P("ctx", "head"), P("ctx", "head"), P("ctx", "head")),
        check_vma=False,
    )
```

```python
import functools

import jax
import jax.numpy as jnp
from jax import lax
from jax.experimental import pallas as pl
from jax.experimental.pallas import tpu as pltpu
from jax.sharding import PartitionSpec as P

HEAD_DIM = 128
D = 5120
TILE = 128
REACH = 1
G_DEV = 2
GROUP = 4
CHUNKS = (2, 2, 1)
ORDER = ("b0 i0 g0 b1", "i1 e0 b2 g1", "i2:z2 s0 e1 g2", "e2 s1",)


EPSILON = 1e-06
FACTOR = HEAD_DIM ** (-0.5)
LOG2_E = 1.4426950408889634
FACTS = 32
FINISH_STEPS = 4
F32 = jnp.float32
BF16 = jnp.bfloat16
ANY = pl.BlockSpec(memory_space=pl.ANY)
VMEM_LIMIT = 48 * 1024 * 1024


def swapped(shard, bit):
    count = lax.axis_size("ctx")
    return lax.ppermute(shard, "ctx", [(i, i ^ bit) for i in range(count)])


def swapped_edges(shard):
    count = lax.axis_size("ctx")
    pairs = [(i, i ^ 12) for i in range(count) if i // GROUP % GROUP in (1, 2)]
    return lax.ppermute(shard, "ctx", pairs)


def params():
    return pltpu.CompilerParams(vmem_limit_bytes=VMEM_LIMIT)


def cost(flops, read):
    return pl.CostEstimate(flops=1, bytes_accessed=1, transcendentals=0)


def behind(kernel, inputs, tokens):
    def run(*refs):
        kernel(*refs[:inputs], *refs[inputs + tokens :])

    return run


def heads_call(kernel, count, place, inputs, outputs, after=(), scratch=(), name=None):
    widths = [w for _, w in inputs] + [w for _, w in outputs]

    def run(place_ref, *refs):
        refs = refs[: len(inputs)] + refs[len(inputs) + len(after) :]
        for h in range(count):
            views = [
                ref.at[:, h * w : (h + 1) * w] if w else ref for ref, w in zip(refs, widths)
            ]
            kernel(h, place_ref, *views, *refs[len(widths) :])

    vmem = pl.BlockSpec(memory_space=pltpu.VMEM)
    return pl.pallas_call(
        run,
        out_shape=[shape for shape, _ in outputs],
        in_specs=[pl.BlockSpec(memory_space=pltpu.SMEM)]
        + [vmem] * len(inputs)
        + [ANY] * len(after),
        out_specs=[vmem] * len(outputs),
        scratch_shapes=scratch,
        compiler_params=params(),
        cost_estimate=cost(1, 1),
        name=name,
    )(place, *[x for x, _ in inputs], *after)


def contract(a, b, dims, precision=None):
    return lax.dot_general(
        a, b, (dims, ((), ())), precision=precision, preferred_element_type=F32
    )


def lane_pair(first, second, rows):
    lane = lax.broadcasted_iota(jnp.int32, (rows, HEAD_DIM), 1)
    return jnp.where(lane < HEAD_DIM // 2, first, second)


def squares_kernel(query_ref, key_ref, out_ref):
    rows, width = query_ref.shape
    step = rows // 4
    for at in range(0, rows, step):
        part = []
        for ref in (query_ref, key_ref):
            x = ref[at : at + step].astype(F32)
            part.append(jnp.sum(x * x, axis=1, keepdims=True))
        out_ref[at : at + step] = lane_pair(*part, step)


def squares(query_raw, key_raw):
    rows, width = query_raw.shape
    vmem = pl.BlockSpec(memory_space=pltpu.VMEM)
    return pl.pallas_call(
        squares_kernel,
        out_shape=jax.ShapeDtypeStruct((rows, HEAD_DIM), F32),
        in_specs=[vmem] * 2,
        out_specs=vmem,
        compiler_params=params(),
        cost_estimate=cost(1, 1),
        name="squares",
    )(query_raw, key_raw)


def inverses(own, other):
    both = lax.rsqrt((own + other) / D + EPSILON)
    return both[:, :1], both[:, HEAD_DIM // 2 : HEAD_DIM // 2 + 1]


def rows_kernel(place_ref, ids_ref, own_ref, other_ref, key_ref, value_ref, gain_ref, out, raw):
    rows, width = key_ref.shape
    block = width // GROUP
    device = place_ref[1] * GROUP + place_ref[0]
    row = lax.broadcasted_iota(jnp.int32, (16, width), 0)
    keys, found, vals = [], [], []
    for r in range(G_DEV):
        at = ids_ref[r] - device * rows
        base = pl.multiple_of(at // 16 * 16, 16)
        here = pl.ds(base, 16)
        _, inv = inverses(own_ref[here], other_ref[here])
        hot = row == at - base

        def only(x):
            return jnp.sum(jnp.where(hot, x, 0.0), axis=0, keepdims=True)

        key = key_ref[here].astype(F32)
        keys.append(only(key))
        found.append(only((key * inv * gain_ref[...]).astype(BF16).astype(F32)))
        vals.append(only(value_ref[here].astype(F32)))
    raw[...] = jnp.where(row == 0, keys[0], keys[1]).astype(BF16)
    total = jnp.zeros((16, block), F32)
    row = lax.broadcasted_iota(jnp.int32, (16, block), 0)
    for g in range(GROUP):
        for i, x in enumerate(found + vals):
            total = jnp.where(row == 4 * g + i, x[:, g * block : (g + 1) * block], total)
    out[...] = total.astype(BF16)


def global_rows(place, ids, own, other, key_raw, values, key_gain):
    rows, width = key_raw.shape
    smem = pl.BlockSpec(memory_space=pltpu.SMEM)
    vmem = pl.BlockSpec(memory_space=pltpu.VMEM)
    return pl.pallas_call(
        rows_kernel,
        out_shape=[
            jax.ShapeDtypeStruct((16, width // GROUP), BF16),
            jax.ShapeDtypeStruct((16, width), BF16),
        ],
        in_specs=[smem, smem] + [vmem] * 5,
        out_specs=[vmem] * 2,
        compiler_params=params(),
        cost_estimate=cost(1, 1),
        name="global_rows",
    )(place, ids, own, other, key_raw, values, key_gain)


def pack_kernel(first, place_ref, tiles_ref, readers_ref, own_ref, other_ref, *refs):
    me, plane = place_ref[0], place_ref[1]
    query_inv, key_inv = inverses(own_ref[...], other_ref[...])
    rows = own_ref.shape[0]
    row = lax.broadcasted_iota(jnp.int32, (16, HEAD_DIM), 0)
    lane = lax.broadcasted_iota(jnp.int32, (16, HEAD_DIM), 1)
    facts = jnp.zeros((16, HEAD_DIM), jnp.int32)
    for tile in range(rows // TILE):
        start = tiles_ref[tile, 0] - (plane * GROUP - 1) * (rows // TILE)
        facts = jnp.where(row == 1 + tile, start, facts)
    for e in range(GROUP):
        for j in range(GROUP):
            live = readers_ref[0, (plane ^ e) * GROUP + j]
            chosen = (row == 0) & (lane // G_DEV == GROUP * j + e)
            facts = jnp.where(chosen, live, facts)
    facts = facts.astype(F32).astype(BF16)
    key_ref, value_ref, query_ref, grad_ref, key_gain, query_gain = refs[:6]
    *outs, token = refs[6 + GROUP :]
    token[...] = jnp.zeros((8, HEAD_DIM), F32)
    parts = jnp.concatenate([ref[...] for ref in refs[6 : 6 + GROUP]], axis=0)
    row = lax.broadcasted_iota(jnp.int32, (16, 16 * GROUP), 0)
    col = lax.broadcasted_iota(jnp.int32, (16, 16 * GROUP), 1)
    each = key_ref.shape[1] // HEAD_DIM // GROUP
    for d, out in enumerate(outs):
        spot = col % 16 - 4 * (me ^ d)
        hot = (spot >= 0) & (spot < 4)
        hot = hot & (row == 2 * (col // 16) + spot % 2 + 8 * (spot // 2))
        hot = hot.astype(F32).astype(BF16)
        chosen = parts[:, first * HEAD_DIM : first * HEAD_DIM + out.shape[1]]
        out[4 * rows + 16 :] = contract(hot, chosen, ((1,), (0,))).astype(BF16)
        for h in range(out.shape[1] // HEAD_DIM):
            at = pl.multiple_of(((me ^ d) * each + first + h) * HEAD_DIM, HEAD_DIM)
            here = pl.ds(at, HEAD_DIM)
            lanes = slice(h * HEAD_DIM, (h + 1) * HEAD_DIM)
            key = key_ref[:, here].astype(F32)
            query = query_ref[:, here].astype(F32)
            out[0:rows, lanes] = (key * key_inv * key_gain[:, here]).astype(BF16)
            out[rows : 2 * rows, lanes] = value_ref[:, here]
            out[2 * rows : 3 * rows, lanes] = (query * query_inv * query_gain[:, here]).astype(BF16)
            out[3 * rows : 4 * rows, lanes] = grad_ref[:, here]
            out[4 * rows : 4 * rows + 16, lanes] = facts


def pack(place, tiles, readers, own, other, arrays, gains, parts, first, count, after):
    query_raw, key_raw, values, out_grad = arrays
    query_gain, key_gain = gains
    rows, width = query_raw.shape
    smem = pl.BlockSpec(memory_space=pltpu.SMEM)
    vmem = pl.BlockSpec(memory_space=pltpu.VMEM)
    out_rows = 4 * rows + FACTS
    kernel = functools.partial(pack_kernel, first)
    return pl.pallas_call(
        behind(kernel, 11 + GROUP, len(after)),
        out_shape=[jax.ShapeDtypeStruct((out_rows, count * HEAD_DIM), BF16)] * GROUP
        + [jax.ShapeDtypeStruct((8, HEAD_DIM), F32)],
        in_specs=[smem] * 3 + [vmem] * (8 + GROUP) + [ANY] * len(after),
        out_specs=[vmem] * (GROUP + 1),
        compiler_params=params(),
        cost_estimate=cost(1, 1),
        name="pack",
    )(
        place, tiles, readers, own, other, key_raw, values, query_raw, out_grad,
        key_gain, query_gain, *parts, *after,
    )


def edges_kernel(head, place_ref, b0, b1, b2, b3, near_ref, far_ref, token):
    me, plane = place_ref[0], place_ref[1]
    token[...] = jnp.zeros((8, HEAD_DIM), F32)
    even = plane % 2 == 0
    last, first = me ^ (GROUP - 1), me
    for d, block in enumerate((b0, b1, b2, b3)):

        @pl.when(jnp.where(even, last, first) == d)
        def _(block=block):
            near_ref[...] = block[: near_ref.shape[0]]

        @pl.when(jnp.where(even, first, last) == d)
        def _(block=block):
            far_ref[...] = block[: far_ref.shape[0]]


def edges(place, blocks, after):
    out_rows, width = blocks[0].shape
    rows = (out_rows - FACTS) // 4
    half = jax.ShapeDtypeStruct((2 * rows, width), BF16)
    return heads_call(
        edges_kernel,
        1,
        place,
        [(block, 0) for block in blocks],
        [(half, 0), (half, 0), (jax.ShapeDtypeStruct((8, HEAD_DIM), F32), 0)],
        after,
        name="edges",
    )


def attend_kernel(outer, head, place_ref, b0, b1, b2, b3, *refs):
    if outer:
        near, far, g_in, dq_out, acc_out, g_out, near_out, far_out, mid_out, end_out = refs[:10]
    else:
        dq_out, acc_out, g_out = refs[:3]
    pair, weights, sums, raw_g, pair_g, sums_g, facts_at = refs[-7:]
    me, plane = place_ref[0], place_ref[1]
    rows = (b0.shape[0] - FACTS) // 4
    tiles = rows // TILE
    keys = slice(0, HEAD_DIM)
    vals = slice(HEAD_DIM, 2 * HEAD_DIM)

    if head == 0:
        weights[...] = jnp.zeros_like(weights)

    for d, block in enumerate((b0, b1, b2, b3)):
        j = me ^ d
        at = pl.multiple_of((j + 1) * rows, TILE)
        pair[pl.ds(at, rows), keys] = block[0:rows]
        pair[pl.ds(at, rows), vals] = block[rows : 2 * rows]
        for tile in range(tiles):
            here = 2 * rows + tile * TILE
            weights[j * tiles + tile, :TILE, keys] = block[here : here + TILE]
            weights[j * tiles + tile, TILE:, vals] = block[here + rows : here + rows + TILE]
        facts_at[j] = block[4 * rows : 4 * rows + 16].astype(F32)
        extra = block[4 * rows + 16 :].astype(F32)
        eight = pl.ds(pl.multiple_of(8 * j, 8), 8)
        raw_g[eight, keys] = extra[:8]
        raw_g[eight, vals] = extra[8:]
    pair_g[...] = raw_g[...].astype(BF16)
    if outer:
        even = plane % 2 == 0
        top = (GROUP + 1) * rows
        near_at = pl.multiple_of(jnp.where(even, top, 0), TILE)
        far_at = pl.multiple_of(jnp.where(even, 0, top), TILE)
        for ref, at in ((near, near_at), (far, far_at)):
            pair[pl.ds(at, rows), keys] = ref[0:rows]
            pair[pl.ds(at, rows), vals] = ref[rows : 2 * rows]
    sums[...] = jnp.zeros_like(sums)
    sums_g[...] = jnp.zeros_like(sums_g)
    count_g = pair_g.shape[0]
    row = lax.broadcasted_iota(jnp.int32, (count_g, HEAD_DIM), 0)
    lane = lax.broadcasted_iota(jnp.int32, (count_g, HEAD_DIM), 1)
    span = 4 * TILE
    units = []
    for j in (0, GROUP - 1) if outer else range(1, GROUP - 1):
        facts = facts_at[j]
        live = jnp.sum(jnp.where(row == lane, facts[0:1], 0.0), axis=1, keepdims=True) > 0.0
        for tile in range(tiles):
            start = jnp.max(facts[1 + tile : 2 + tile]).astype(jnp.int32)
            units.append((j * tiles + tile, pl.multiple_of(start * TILE, TILE), live))

    def products(unit):
        weight, at, _ = units[unit]
        both = jnp.concatenate([pair[pl.ds(at, span)], pair_g[...]], axis=0)
        return contract(both, weights[weight], ((1,), (1,)))

    ahead = products(0)
    for unit, (weight, at, live) in enumerate(units):
        product = ahead
        if unit + 1 < len(units):
            ahead = products(unit + 1)
        score = product[:, :TILE] * (FACTOR * LOG2_E)
        dprob = product[:, TILE:]
        score_g = jnp.where(live, score[span:], -jnp.inf)
        score = jnp.concatenate([score[:span], score_g], axis=0)
        largest = jnp.max(score, axis=0, keepdims=True)
        probs = jnp.exp2(score - largest)
        probs = probs * (1.0 / jnp.sum(probs, axis=0, keepdims=True))
        delta = jnp.sum(probs * dprob, axis=0, keepdims=True)
        dscore = (probs * ((dprob - delta) * FACTOR)).astype(BF16)
        grads = contract(
            jnp.concatenate([dscore, probs.astype(BF16)], axis=1), weights[weight], ((1,), (0,))
        )
        sums[pl.ds(at, span)] += grads[:span]
        sums_g[...] += grads[span:]
        both = jnp.concatenate([pair[pl.ds(at, span), keys], pair_g[:, keys]], axis=0)
        grad_query = contract(dscore, both, ((0,), (0,)))
        dq_out[unit * TILE : (unit + 1) * TILE] = grad_query.astype(BF16)
    acc_out[...] = sums[rows : (GROUP + 1) * rows].astype(BF16)
    if not outer:
        g_out[...] = sums_g[...]
    else:
        total_g = (g_in[...] + sums_g[...]).astype(BF16)
        row = lax.broadcasted_iota(jnp.int32, (8, 8 * GROUP), 0)
        col = lax.broadcasted_iota(jnp.int32, (8, 8 * GROUP), 1)
        for e, out in enumerate((g_out, near_out, mid_out, end_out)):
            hot = (col // 8 == row // G_DEV) & (col % 8 == G_DEV * e + row % G_DEV)
            part = contract(hot.astype(F32).astype(BF16), total_g, ((1,), (0,)))
            out[out.shape[0] - 16 :] = jnp.concatenate([part[:, keys], part[:, vals]], axis=0).astype(
                BF16
            )
        for out, at in ((near_out, near_at), (far_out, far_at)):
            out[:rows] = sums[pl.ds(at, rows), keys].astype(BF16)
            out[rows : 2 * rows] = sums[pl.ds(at, rows), vals].astype(BF16)


def attend(place, blocks, halo, inner_g, after):
    out_rows, width = blocks[0].shape
    rows = (out_rows - FACTS) // 4
    wide = 2 * HEAD_DIM
    half = jax.ShapeDtypeStruct((2 * rows, width), BF16)
    few = jax.ShapeDtypeStruct((16, width), BF16)
    near = jax.ShapeDtypeStruct((2 * rows + 16, width), BF16)
    outs = [(half, HEAD_DIM), (jax.ShapeDtypeStruct((GROUP * rows, 2 * width), BF16), wide)]
    if halo:
        outs += [(x, HEAD_DIM) for x in (few, near, half, few, few)]
    else:
        outs += [(jax.ShapeDtypeStruct((8 * GROUP, 2 * width), F32), wide)]
    return heads_call(
        functools.partial(attend_kernel, len(halo) > 0),
        width // HEAD_DIM,
        place,
        [(x, HEAD_DIM) for x in (*blocks, *halo)] + [(x, wide) for x in inner_g],
        outs,
        after,
        [
            pltpu.VMEM(((GROUP + 2) * rows, wide), BF16),
            pltpu.VMEM((GROUP * rows // TILE, 2 * TILE, wide), BF16),
            pltpu.VMEM(((GROUP + 2) * rows, wide), F32),
            pltpu.VMEM((8 * GROUP, wide), F32),
            pltpu.VMEM((8 * GROUP, wide), BF16),
            pltpu.VMEM((8 * GROUP, wide), F32),
            pltpu.VMEM((GROUP, 16, HEAD_DIM), F32),
        ],
        name="outer" if halo else "inner",
    )


def settle_kernel(
    head, place_ref, dq_in, acc_in, dq_out, acc_out, own_g, near, far, *refs
):
    *more, o0, o1, o2, o3, token = refs
    me, plane = place_ref[0], place_ref[1]
    token[...] = jnp.zeros((8, HEAD_DIM), F32)
    rows = dq_in.shape[0] // 2
    even = plane % 2 == 0
    inner = (plane == 1) | (plane == 2)
    part = (own_g[...].astype(F32) + near[2 * rows :].astype(F32)).astype(BF16)
    if more and head == 0:
        rest_g = (more[0][...].astype(F32) + more[1][...].astype(F32)).astype(BF16)
    for d, out in enumerate((o0, o1, o2, o3)):
        j = me ^ d
        near_here = j == jnp.where(even, GROUP - 1, 0)
        far_here = (j == jnp.where(even, 0, GROUP - 1)) & inner
        outside = (j == 0) | (j == GROUP - 1)

        @pl.when(outside)
        def _(out=out, j=j):
            out[:rows] = dq_out[pl.ds(pl.multiple_of(jnp.where(j == 0, 0, rows), TILE), rows)]

        @pl.when(~outside)
        def _(out=out, j=j):
            out[:rows] = dq_in[pl.ds(pl.multiple_of(jnp.where(j == 1, 0, rows), TILE), rows)]

        here = pl.ds(pl.multiple_of(j * rows, TILE), rows)
        for i in range(2):
            lanes = slice(i * HEAD_DIM, (i + 1) * HEAD_DIM)
            rest = slice(i * rows, (i + 1) * rows)
            total = acc_in[here, lanes].astype(F32) + acc_out[here, lanes].astype(F32)
            total = total + jnp.where(near_here, near[rest].astype(F32), 0.0)
            total = total + jnp.where(far_here, far[rest].astype(F32), 0.0)
            out[(i + 1) * rows : (i + 2) * rows] = total.astype(BF16)
        out[3 * rows : 3 * rows + 16] = part
        if more and head == 0:
            for h in range(rest_g.shape[1] // HEAD_DIM):
                at = 3 * rows + 16 * (h + 1)
                out[at : at + 16] = rest_g[:, h * HEAD_DIM : (h + 1) * HEAD_DIM]


def settle(place, inner, outer, own_g, near, far, more, after):
    rows, width = inner[0].shape
    rows = rows // 2
    part = (HEAD_DIM, 2 * HEAD_DIM)
    extra = 16 + 16 * (more[0].shape[1] // HEAD_DIM if more else 0)
    home = jax.ShapeDtypeStruct((3 * rows + extra, width), BF16)
    return heads_call(
        settle_kernel,
        width // HEAD_DIM,
        place,
        [*zip(inner, part), *zip(outer, part)]
        + [(x, HEAD_DIM) for x in (own_g, near, far)]
        + [(x, 0) for x in more],
        [(home, HEAD_DIM)] * GROUP + [(jax.ShapeDtypeStruct((8, HEAD_DIM), F32), 0)],
        after,
        name="settle",
    )


def join_kernel(head, place_ref, *refs):
    *parts, mid, end = refs
    half = len(parts) // 2
    for out, some in ((mid, parts[:half]), (end, parts[half:])):
        first = 0
        for part in some:
            out[:, first : first + part.shape[1]] = part[...]
            first += part.shape[1]


def join(place, mids, ends):
    shape = jax.ShapeDtypeStruct((16, sum(x.shape[1] for x in mids)), BF16)
    return heads_call(
        join_kernel,
        1,
        place,
        [(x, 0) for x in (*mids, *ends)],
        [(shape, 0), (shape, 0)],
        name="join",
    )


def total_kernel(chunks, place_ref, ids_ref, raw_ref, query, key, query_gain, gain_ref, *refs):
    *refs, out, sums = refs
    homes, dot_refs = refs[: GROUP * len(chunks)], refs[GROUP * len(chunks) :]
    rows, width = out.shape[0], sums.shape[1]
    me = place_ref[0]
    device = place_ref[1] * GROUP + me
    total = part_dots(
        sum(chunks[:-1]), me, homes[-GROUP:], query, key, query_gain, gain_ref
    )
    for ref in dot_refs:
        total = total + ref[...]
    few = lax.broadcasted_iota(jnp.int32, (16, HEAD_DIM), 0)
    eight = lax.broadcasted_iota(jnp.int32, (8, HEAD_DIM), 0)
    hot = [few == 8 * i + G_DEV * me + r for i in range(2) for r in range(G_DEV)]
    dot = [jnp.zeros((1, HEAD_DIM), F32) for _ in range(G_DEV)]
    for d in range(GROUP):
        first = 0
        for c, count in enumerate(chunks):
            for h in range(count):
                home = homes[c * GROUP + d]
                last = homes[(len(chunks) - 1) * GROUP + d]
                at = 3 * rows + 16 * (first + h + 1)
                part = home[3 * rows : 3 * rows + 16, h * HEAD_DIM : (h + 1) * HEAD_DIM].astype(F32)
                part = part + last[at : at + 16, :HEAD_DIM].astype(F32)
                found = [jnp.sum(jnp.where(x, part, 0.0), axis=0, keepdims=True) for x in hot]
                at = pl.multiple_of(
                    (me ^ d) * (width // GROUP) + (first + h) * HEAD_DIM, HEAD_DIM
                )
                here = pl.ds(at, HEAD_DIM)
                block = jnp.zeros((8, HEAD_DIM), F32)
                for i, x in enumerate(found):
                    block = jnp.where(eight == i, x, block)
                sums[:, here] = block
                raw = raw_ref[:, here].astype(F32)
                for r in range(G_DEV):
                    dot[r] = dot[r] + found[r] * gain_ref[:, here] * raw[r : r + 1]
            first += count
    row = lax.broadcasted_iota(jnp.int32, (rows, HEAD_DIM), 0)
    lane = lax.broadcasted_iota(jnp.int32, (rows, HEAD_DIM), 1)
    for r in range(G_DEV):
        here = (row == ids_ref[r] - device * rows) & (lane >= HEAD_DIM // 2)
        total = total + jnp.where(here, jnp.sum(dot[r], axis=1, keepdims=True), 0.0)
    out[...] = total


def total_dots(place, ids, raw, query_raw, key_raw, gains, homes, dots, chunks):
    smem = pl.BlockSpec(memory_space=pltpu.SMEM)
    vmem = pl.BlockSpec(memory_space=pltpu.VMEM)
    flat = [x for home in homes for x in home]
    raw_rows = query_raw.shape[0]
    return pl.pallas_call(
        functools.partial(total_kernel, chunks),
        out_shape=[
            jax.ShapeDtypeStruct((raw_rows, HEAD_DIM), F32),
            jax.ShapeDtypeStruct((8, raw.shape[1]), F32),
        ],
        in_specs=[smem, smem] + [vmem] * (5 + len(flat) + len(dots)),
        out_specs=[vmem, vmem],
        compiler_params=params(),
        cost_estimate=cost(1, 1),
        name="total_dots",
    )(place, ids, raw, query_raw, key_raw, *gains, *flat, *dots)


def part_dots(first, me, homes, query, key, query_gain, key_gain):
    rows, width = query.shape
    each = width // HEAD_DIM // GROUP
    totals = [jnp.zeros((rows, HEAD_DIM), F32), jnp.zeros((rows, HEAD_DIM), F32)]
    for d, grads in enumerate(homes):
        for h in range(grads.shape[1] // HEAD_DIM):
            at = ((me ^ d) * each + first + h) * HEAD_DIM
            here = pl.ds(pl.multiple_of(at, HEAD_DIM), HEAD_DIM)
            lanes = slice(h * HEAD_DIM, (h + 1) * HEAD_DIM)
            for i, (raw, gain) in enumerate(((query, query_gain), (key, key_gain))):
                grad = grads[i * rows : (i + 1) * rows, lanes].astype(F32)
                totals[i] += grad * gain[:, here] * raw[:, here].astype(F32)
    sums = [jnp.sum(x, axis=1, keepdims=True) for x in totals]
    return lane_pair(*sums, rows)


def dots_kernel(first, head, place_ref, *refs):
    refs[-1][...] = part_dots(first, place_ref[0], refs[:GROUP], *refs[GROUP:-1])


def dots(place, grads, query_raw, key_raw, gains, first, after):
    return heads_call(
        functools.partial(dots_kernel, first),
        1,
        place,
        [(x, 0) for x in (*grads, query_raw, key_raw, *gains)],
        [(jax.ShapeDtypeStruct((query_raw.shape[0], HEAD_DIM), F32), 0)],
        after,
        name="dots",
    )[0]


def finish_kernel(chunks, place_ref, ids_ref, own_ref, other_ref, dot_ref, dot_other_ref, *refs):
    me = place_ref[0]
    device = place_ref[1] * GROUP + me
    grads = refs[: GROUP * len(chunks)]
    sum_ref, query_ref, key_ref, query_gain, key_gain = refs[GROUP * len(chunks) : -3]
    query_out, key_out, value_out = refs[-3:]
    rows, width = query_ref.shape
    block = query_out.shape[0]
    each = width // GROUP
    start = pl.program_id(0) * block
    now = pl.ds(pl.multiple_of(start, block), block)
    inv = inverses(own_ref[now], other_ref[now])
    total = dot_ref[now] + dot_other_ref[now]
    dot = (total[:, :1], total[:, HEAD_DIM // 2 : HEAD_DIM // 2 + 1])
    coeff = [inv[i] * inv[i] * inv[i] * (dot[i] / D) for i in range(2)]
    row = lax.broadcasted_iota(jnp.int32, (block, HEAD_DIM), 0) + start
    hot = [row == ids_ref[r] - device * rows for r in range(G_DEV)]
    for d in range(GROUP):
        first = 0
        for c, count in enumerate(chunks):
            ref = grads[c * GROUP + d]
            for h in range(count):
                at = pl.multiple_of((me ^ d) * each + (first + h) * HEAD_DIM, HEAD_DIM)
                here = pl.ds(at, HEAD_DIM)
                col = slice(h * HEAD_DIM, (h + 1) * HEAD_DIM)
                grad = [
                    ref[pl.ds(pl.multiple_of(start + i * rows, block), block), col].astype(F32)
                    for i in range(3)
                ]
                for i in (1, 2):
                    for r in range(G_DEV):
                        more = sum_ref[2 * (i - 1) + r : 2 * (i - 1) + r + 1, here]
                        grad[i] = grad[i] + jnp.where(hot[r], more, 0.0)
                for i, (raw, gain, out) in enumerate(
                    ((query_ref, query_gain, query_out), (key_ref, key_gain, key_out))
                ):
                    out[:, here] = (
                        inv[i] * (grad[i] * gain[:, here]) - raw[now, here].astype(F32) * coeff[i]
                    ).astype(BF16)
                value_out[:, here] = grad[2].astype(BF16)
            first += count


def finish(place, ids, own, other, dot, dot_other, sums, grads, query_raw, key_raw, gains, chunks):
    rows, width = query_raw.shape
    smem = pl.BlockSpec(memory_space=pltpu.SMEM)
    vmem = pl.BlockSpec(memory_space=pltpu.VMEM)
    flat = [x for chunk in grads for x in chunk]
    block = pl.BlockSpec((rows // FINISH_STEPS, width), lambda i: (i, 0))
    return pl.pallas_call(
        functools.partial(finish_kernel, chunks),
        out_shape=[jax.ShapeDtypeStruct(query_raw.shape, BF16)] * 3,
        grid=(FINISH_STEPS,),
        in_specs=[smem, smem] + [vmem] * (4 + len(flat) + 5),
        out_specs=[block] * 3,
        compiler_params=params(),
        cost_estimate=cost(1, 1),
        name="finish",
    )(place, ids, own, other, dot, dot_other, *flat, sums, query_raw, key_raw, *gains)


def swap_heads(x):
    return lax.ppermute(x, "head", [(0, 1), (1, 0)])


def plane_body(
    query_raw, key_raw, values, out_grad, query_gain, key_gain, key_tiles, global_ids, readers
):
    device = lax.axis_index("ctx")
    place = jnp.stack([device % GROUP, device // GROUP]).astype(jnp.int32)
    gains = (query_gain[None, :], key_gain[None, :])
    own = squares(query_raw, key_raw)
    other = swap_heads(own)
    arrays = (query_raw, key_raw, values, out_grad)
    mine, raw_rows = global_rows(place, global_ids, own, other, key_raw, values, gains[1])
    parts = [mine] + [swapped(mine, 4 * e) for e in range(1, GROUP)]
    chunks = len(CHUNKS)
    firsts = [sum(CHUNKS[:c]) for c in range(chunks)]
    packed, token = [], ()
    for first, count in zip(firsts, CHUNKS):
        *sent, last = pack(
            place, key_tiles, readers, own, other, arrays, gains, parts, first, count, token
        )
        token = (last,)
        packed.append([sent[0]] + [swapped(sent[d], d) for d in range(1, GROUP)])
    edge, inner, outer, back, home, dot = ({} for _ in range(6))
    fars = []

    def begin(c, token):
        near, far, last = edges(place, packed[c], token)
        edge[c] = (swapped(near, 4), swapped_edges(far))
        return (last,)

    def inside(c, token):
        inner[c] = attend(place, packed[c], (), (), token)
        return (inner[c][2],)

    def outside(c, token):
        results = attend(place, packed[c], edge[c], (inner[c][2],), token)
        outer[c], own_g, near, far, mid, last = results[:2], *results[2:]
        fars.append((mid, last))
        more = ()
        if c == chunks - 1:
            mids, lasts = zip(*fars)
            mid, last = join(place, mids, lasts)
            more = (swapped(mid, 8), swapped(last, 12))
        back[c] = (own_g, swapped(near, 4), swapped_edges(far), more)
        return (own_g,)

    def end(c, token):
        *sent, last = settle(place, inner[c][:2], outer[c], *back[c], token)
        home[c] = [sent[0]] + [swapped(sent[d], d) for d in range(1, GROUP)]
        return (last,)

    def score(c, token):
        dot[c] = dots(place, home[c], query_raw, key_raw, gains, firsts[c], token)
        return (dot[c],)

    stages = {"b": begin, "i": inside, "g": outside, "e": end, "s": score}
    for step in " ".join(ORDER).split():
        name, *extra = step.split(":")
        held = tuple(x for e in extra for x in edge[int(e[1])])
        token = stages[name[0]](int(name[1]), token + held)
    homes = [home[c] for c in range(chunks)]
    total, sums = total_dots(
        place, global_ids, raw_rows, query_raw, key_raw, gains, homes, list(dot.values()), CHUNKS
    )
    return tuple(
        finish(
            place, global_ids, own, other, total, swap_heads(total), sums, homes,
            query_raw, key_raw, gains, CHUNKS,
        )
    )


def passed_along(shard, axis, by):
    count = lax.axis_size(axis)
    return lax.ppermute(shard, axis, [(i, (i + by) % count) for i in range(count)])


def normalize(as_float, gain, squares):
    inverse = lax.rsqrt(squares[:, None] / D + EPSILON)
    return (inverse, (as_float * inverse * gain).astype(jnp.bfloat16))


def norm_grad(as_float, inverse, scaled, coeffs):
    return (inverse * scaled - as_float * inverse**3 * (coeffs[:, None] / D)).astype(jnp.bfloat16)


def body(
    query_raw, key_raw, values, out_grad, query_gain, key_gain, key_tiles, global_ids, readers
):
    tokens_here, width_here = query_raw.shape
    heads_here = width_here // HEAD_DIM
    tiles_here = tokens_here // TILE
    factor = HEAD_DIM ** (-0.5)
    device = lax.axis_index("ctx")
    query_rows = query_raw.astype(jnp.float32)
    key_rows = key_raw.astype(jnp.float32)
    query_sq, key_sq = lax.psum(
        (jnp.sum(query_rows * query_rows, axis=1), jnp.sum(key_rows * key_rows, axis=1)), "head"
    )
    query_inv, query_norm = normalize(query_rows, query_gain, query_sq)
    key_inv, key_norm = normalize(key_rows, key_gain, key_sq)
    own_rows = global_ids - device * tokens_here
    own_pair = jnp.stack([key_norm[own_rows], values[own_rows]])
    global_pair = lax.all_gather(own_pair, "ctx", axis=1, tiled=True)
    global_keys = global_pair[0].reshape(-1, heads_here, HEAD_DIM)
    global_vals = global_pair[1].reshape(-1, heads_here, HEAD_DIM)
    live_mask = jnp.repeat(readers[0] > 0, G_DEV)
    key_value = jnp.stack([key_norm, values])
    current = passed_along(key_value, "ctx", -REACH)
    pieces = [current]
    for hop_index in range(2 * REACH):
        current = passed_along(current, "ctx", 1)
        pieces.append(current)
    pieces = pieces[::-1]
    window_pair = jnp.concatenate(pieces, axis=1)
    first_tile = (device - REACH) * tiles_here
    local_tiles = key_tiles - first_tile
    window_rows = (
        local_tiles[:, :, None] * TILE + jnp.arange(TILE, dtype=jnp.int32)[None, None, :]
    ).reshape(tiles_here, -1)
    window_count = window_rows.shape[1]
    window_keys = window_pair[0][window_rows].reshape(
        tiles_here, window_count, heads_here, HEAD_DIM
    )
    window_vals = window_pair[1][window_rows].reshape(
        tiles_here, window_count, heads_here, HEAD_DIM
    )
    query_four = query_norm.reshape(tiles_here, TILE, heads_here, HEAD_DIM)
    grad_four = out_grad.reshape(tiles_here, TILE, heads_here, HEAD_DIM)

    def head_block(head_number):
        query_head = lax.dynamic_index_in_dim(query_four, head_number, 2, keepdims=False)
        grad_head = lax.dynamic_index_in_dim(grad_four, head_number, 2, keepdims=False)
        wkeys = lax.dynamic_index_in_dim(window_keys, head_number, 2, keepdims=False)
        wvals = lax.dynamic_index_in_dim(window_vals, head_number, 2, keepdims=False)
        gkeys = lax.dynamic_index_in_dim(global_keys, head_number, 1, keepdims=False)
        gvals = lax.dynamic_index_in_dim(global_vals, head_number, 1, keepdims=False)
        score_window = (
            jnp.einsum("tqd,tkd->tqk", query_head, wkeys, preferred_element_type=jnp.float32)
            * factor
        )
        score_global = (
            jnp.einsum("tqd,kd->tqk", query_head, gkeys, preferred_element_type=jnp.float32)
            * factor
        )
        score_global = jnp.where(live_mask, score_global, -jnp.inf)
        scores = jnp.concatenate([score_window, score_global], axis=2)
        largest = jnp.max(scores, axis=2, keepdims=True)
        log_total = largest + jnp.log(jnp.sum(jnp.exp(scores - largest), axis=2, keepdims=True))
        probs = jnp.exp(scores - log_total)
        probs_low = probs.astype(jnp.bfloat16)
        attended = jnp.einsum(
            "tqk,tkd->tqd", probs_low[..., :window_count], wvals, preferred_element_type=jnp.float32
        )
        attended = attended + jnp.einsum(
            "tqk,kd->tqd", probs_low[..., window_count:], gvals, preferred_element_type=jnp.float32
        )
        attended = lax.optimization_barrier(attended.astype(jnp.bfloat16))
        delta_rows = jnp.sum(grad_head.astype(jnp.float32) * attended.astype(jnp.float32), axis=2)
        dprob = jnp.concatenate(
            [
                jnp.einsum("tqd,tkd->tqk", grad_head, wvals, preferred_element_type=jnp.float32),
                jnp.einsum("tqd,kd->tqk", grad_head, gvals, preferred_element_type=jnp.float32),
            ],
            axis=2,
        )
        dscore = (probs * (dprob - delta_rows[..., None]) * factor).astype(jnp.bfloat16)
        grad_query = jnp.einsum(
            "tqk,tkd->tqd", dscore[..., :window_count], wkeys, preferred_element_type=jnp.float32
        )
        grad_query = grad_query + jnp.einsum(
            "tqk,kd->tqd", dscore[..., window_count:], gkeys, preferred_element_type=jnp.float32
        )
        window_dk = jnp.einsum(
            "tqk,tqd->tkd",
            dscore[..., :window_count],
            query_head,
            preferred_element_type=jnp.float32,
        )
        window_dv = jnp.einsum(
            "tqk,tqd->tkd",
            probs_low[..., :window_count],
            grad_head,
            preferred_element_type=jnp.float32,
        )
        global_dk = jnp.einsum(
            "tqk,tqd->kd",
            dscore[..., window_count:],
            query_head,
            preferred_element_type=jnp.float32,
        )
        global_dv = jnp.einsum(
            "tqk,tqd->kd",
            probs_low[..., window_count:],
            grad_head,
            preferred_element_type=jnp.float32,
        )
        return (grad_query, window_dk, window_dv, global_dk, global_dv)

    head_results = lax.map(head_block, jnp.arange(heads_here, dtype=jnp.int32))
    grad_query = jnp.moveaxis(head_results[0], 0, 2).reshape(tokens_here, width_here)
    window_dk = jnp.moveaxis(head_results[1], 0, 2).reshape(-1, width_here)
    window_dv = jnp.moveaxis(head_results[2], 0, 2).reshape(-1, width_here)
    global_dk = jnp.moveaxis(head_results[3], 0, 1).reshape(-1, width_here)
    global_dv = jnp.moveaxis(head_results[4], 0, 1).reshape(-1, width_here)
    window_grads = jnp.zeros((2, window_pair.shape[1], width_here), jnp.float32)
    window_grads = window_grads.at[:, window_rows.reshape(-1)].add(
        jnp.stack([window_dk, window_dv])
    )
    spread_grads = window_grads.reshape(2, 2 * REACH + 1, tokens_here, width_here)
    slots = [spread_grads[:, slot_index] for slot_index in range(2 * REACH + 1)]
    carried = slots[2 * REACH]
    for hop_index in range(2 * REACH):
        carried = (
            passed_along(carried.astype(jnp.bfloat16), "ctx", 1).astype(carried.dtype)
            + slots[2 * REACH - 1 - hop_index]
        )
    home_grads = passed_along(carried.astype(jnp.bfloat16), "ctx", -REACH).astype(carried.dtype)
    global_part = lax.psum_scatter(
        jnp.stack([global_dk, global_dv]), "ctx", scatter_dimension=1, tiled=True
    )
    home_grads = home_grads.at[:, own_rows].add(global_part)
    scaled_query = grad_query * query_gain
    scaled_key = home_grads[0] * key_gain
    query_dot, key_dot = lax.psum(
        (jnp.sum(scaled_query * query_rows, axis=1), jnp.sum(scaled_key * key_rows, axis=1)), "head"
    )
    query_grad = norm_grad(query_rows, query_inv, scaled_query, query_dot)
    key_grad = norm_grad(key_rows, key_inv, scaled_key, key_dot)
    return (query_grad, key_grad, home_grads[1].astype(jnp.bfloat16))


def solution(mesh):
    sizes = dict(mesh.shape)
    planes = sizes["ctx"] == GROUP * GROUP and sizes["head"] == 2
    return jax.shard_map(
        plane_body if planes else body,
        mesh=mesh,
        in_specs=(
            P("ctx", "head"),
            P("ctx", "head"),
            P("ctx", "head"),
            P("ctx", "head"),
            P("head"),
            P("head"),
            P("ctx", None),
            P("ctx"),
            P("ctx", None),
        ),
        out_specs=(P("ctx", "head"), P("ctx", "head"), P("ctx", "head")),
        check_vma=False,
    )
```

```python
import functools

import jax
import jax.numpy as jnp
from jax import lax
from jax.experimental import pallas as pl
from jax.experimental.pallas import tpu as pltpu
from jax.sharding import PartitionSpec as P

HEAD_DIM = 128
D = 5120
TILE = 128
REACH = 1
G_DEV = 2
GROUP = 4
CHUNKS = (2, 2, 1)
ORDER = ("b0 i0 g0 b1", "i1 e0 b2 g1", "i2:z2 s0 e1 g2", "e2 s1",)


EPSILON = 1e-06
FACTOR = HEAD_DIM ** (-0.5)
LOG2_E = 1.4426950408889634
FACTS = 32
FINISH_STEPS = 4
F32 = jnp.float32
BF16 = jnp.bfloat16
ANY = pl.BlockSpec(memory_space=pl.ANY)
VMEM_LIMIT = 48 * 1024 * 1024


def swapped(shard, bit):
    count = lax.axis_size("ctx")
    return lax.ppermute(shard, "ctx", [(i, i ^ bit) for i in range(count)])


def swapped_edges(shard):
    count = lax.axis_size("ctx")
    pairs = [(i, i ^ 12) for i in range(count) if i // GROUP % GROUP in (1, 2)]
    return lax.ppermute(shard, "ctx", pairs)


def params():
    return pltpu.CompilerParams(vmem_limit_bytes=VMEM_LIMIT)


def cost(flops, read):
    return pl.CostEstimate(flops=1, bytes_accessed=1, transcendentals=0)


def behind(kernel, inputs, tokens):
    def run(*refs):
        kernel(*refs[:inputs], *refs[inputs + tokens :])

    return run


def heads_call(kernel, count, place, inputs, outputs, after=(), scratch=(), name=None):
    widths = [w for _, w in inputs] + [w for _, w in outputs]

    def run(place_ref, *refs):
        refs = refs[: len(inputs)] + refs[len(inputs) + len(after) :]
        for h in range(count):
            views = [
                ref.at[:, h * w : (h + 1) * w] if w else ref for ref, w in zip(refs, widths)
            ]
            kernel(h, place_ref, *views, *refs[len(widths) :])

    vmem = pl.BlockSpec(memory_space=pltpu.VMEM)
    return pl.pallas_call(
        run,
        out_shape=[shape for shape, _ in outputs],
        in_specs=[pl.BlockSpec(memory_space=pltpu.SMEM)]
        + [vmem] * len(inputs)
        + [ANY] * len(after),
        out_specs=[vmem] * len(outputs),
        scratch_shapes=scratch,
        compiler_params=params(),
        cost_estimate=cost(1, 1),
        name=name,
    )(place, *[x for x, _ in inputs], *after)


def contract(a, b, dims, precision=None):
    return lax.dot_general(
        a, b, (dims, ((), ())), precision=precision, preferred_element_type=F32
    )


def lane_pair(first, second, rows):
    lane = lax.broadcasted_iota(jnp.int32, (rows, HEAD_DIM), 1)
    return jnp.where(lane < HEAD_DIM // 2, first, second)


def squares_kernel(query_ref, key_ref, out_ref):
    rows, width = query_ref.shape
    step = rows // 4
    for at in range(0, rows, step):
        part = []
        for ref in (query_ref, key_ref):
            x = ref[at : at + step].astype(F32)
            part.append(jnp.sum(x * x, axis=1, keepdims=True))
        out_ref[at : at + step] = lane_pair(*part, step)


def squares(query_raw, key_raw):
    rows, width = query_raw.shape
    vmem = pl.BlockSpec(memory_space=pltpu.VMEM)
    return pl.pallas_call(
        squares_kernel,
        out_shape=jax.ShapeDtypeStruct((rows, HEAD_DIM), F32),
        in_specs=[vmem] * 2,
        out_specs=vmem,
        compiler_params=params(),
        cost_estimate=cost(1, 1),
        name="squares",
    )(query_raw, key_raw)


def inverses(own, other):
    both = lax.rsqrt((own + other) / D + EPSILON)
    return both[:, :1], both[:, HEAD_DIM // 2 : HEAD_DIM // 2 + 1]


def rows_kernel(place_ref, ids_ref, own_ref, other_ref, key_ref, value_ref, gain_ref, out, raw):
    rows, width = key_ref.shape
    block = width // GROUP
    device = place_ref[1] * GROUP + place_ref[0]
    row = lax.broadcasted_iota(jnp.int32, (16, width), 0)
    keys, found, vals = [], [], []
    for r in range(G_DEV):
        at = ids_ref[r] - device * rows
        base = pl.multiple_of(at // 16 * 16, 16)
        here = pl.ds(base, 16)
        _, inv = inverses(own_ref[here], other_ref[here])
        hot = row == at - base

        def only(x):
            return jnp.sum(jnp.where(hot, x, 0.0), axis=0, keepdims=True)

        key = key_ref[here].astype(F32)
        keys.append(only(key))
        found.append(only((key * inv * gain_ref[...]).astype(BF16).astype(F32)))
        vals.append(only(value_ref[here].astype(F32)))
    raw[...] = jnp.where(row == 0, keys[0], keys[1]).astype(BF16)
    total = jnp.zeros((16, block), F32)
    row = lax.broadcasted_iota(jnp.int32, (16, block), 0)
    for g in range(GROUP):
        for i, x in enumerate(found + vals):
            total = jnp.where(row == 4 * g + i, x[:, g * block : (g + 1) * block], total)
    out[...] = total.astype(BF16)


def global_rows(place, ids, own, other, key_raw, values, key_gain):
    rows, width = key_raw.shape
    smem = pl.BlockSpec(memory_space=pltpu.SMEM)
    vmem = pl.BlockSpec(memory_space=pltpu.VMEM)
    return pl.pallas_call(
        rows_kernel,
        out_shape=[
            jax.ShapeDtypeStruct((16, width // GROUP), BF16),
            jax.ShapeDtypeStruct((16, width), BF16),
        ],
        in_specs=[smem, smem] + [vmem] * 5,
        out_specs=[vmem] * 2,
        compiler_params=params(),
        cost_estimate=cost(1, 1),
        name="global_rows",
    )(place, ids, own, other, key_raw, values, key_gain)


def pack_kernel(first, whole, place_ref, tiles_ref, readers_ref, own_ref, other_ref, *refs):
    me, plane = place_ref[0], place_ref[1]
    query_inv, key_inv = inverses(own_ref[...], other_ref[...])
    rows = own_ref.shape[0]
    row = lax.broadcasted_iota(jnp.int32, (16, HEAD_DIM), 0)
    lane = lax.broadcasted_iota(jnp.int32, (16, HEAD_DIM), 1)
    facts = jnp.zeros((16, HEAD_DIM), jnp.int32)
    for tile in range(rows // TILE):
        start = tiles_ref[tile, 0] - (plane * GROUP - 1) * (rows // TILE)
        facts = jnp.where(row == 1 + tile, start, facts)
    for e in range(GROUP):
        for j in range(GROUP):
            live = readers_ref[0, (plane ^ e) * GROUP + j]
            chosen = (row == 0) & (lane // G_DEV == GROUP * j + e)
            facts = jnp.where(chosen, live, facts)
    facts = facts.astype(F32).astype(BF16)
    key_ref, value_ref, query_ref, grad_ref, key_gain, query_gain = refs[:6]
    *outs, token = refs[6 + GROUP :]
    token[...] = jnp.zeros((8, HEAD_DIM), F32)
    parts = jnp.concatenate([ref[...] for ref in refs[6 : 6 + GROUP]], axis=0)
    row = lax.broadcasted_iota(jnp.int32, (16, 16 * GROUP), 0)
    col = lax.broadcasted_iota(jnp.int32, (16, 16 * GROUP), 1)
    each = key_ref.shape[1] // HEAD_DIM // GROUP
    for d, out in enumerate(outs):
        spot = col % 16 - 4 * (me ^ d)
        hot = (spot >= 0) & (spot < 4)
        hot = hot & (row == 2 * (col // 16) + spot % 2 + 8 * (spot // 2))
        hot = hot.astype(F32).astype(BF16)
        chosen = parts[:, first * HEAD_DIM : first * HEAD_DIM + out.shape[1]]
        top = 2 * rows if whole else 0
        out[top + 2 * rows + 16 :] = contract(hot, chosen, ((1,), (0,))).astype(BF16)
        for h in range(out.shape[1] // HEAD_DIM):
            at = pl.multiple_of(((me ^ d) * each + first + h) * HEAD_DIM, HEAD_DIM)
            here = pl.ds(at, HEAD_DIM)
            lanes = slice(h * HEAD_DIM, (h + 1) * HEAD_DIM)
            key = key_ref[:, here].astype(F32)
            query = query_ref[:, here].astype(F32)
            if whole:
                out[0:rows, lanes] = value_ref[:, here]
                out[rows : 2 * rows, lanes] = grad_ref[:, here]
            out[top : top + rows, lanes] = (key * key_inv * key_gain[:, here]).astype(BF16)
            out[top + rows : top + 2 * rows, lanes] = (
                query * query_inv * query_gain[:, here]
            ).astype(BF16)
            out[top + 2 * rows : top + 2 * rows + 16, lanes] = facts


def pack(place, tiles, readers, own, other, arrays, gains, parts, first, count, whole, after):
    query_raw, key_raw, values, out_grad = arrays
    query_gain, key_gain = gains
    rows, width = query_raw.shape
    smem = pl.BlockSpec(memory_space=pltpu.SMEM)
    vmem = pl.BlockSpec(memory_space=pltpu.VMEM)
    out_rows = (4 if whole else 2) * rows + FACTS
    kernel = functools.partial(pack_kernel, first, whole)
    return pl.pallas_call(
        behind(kernel, 11 + GROUP, len(after)),
        out_shape=[jax.ShapeDtypeStruct((out_rows, count * HEAD_DIM), BF16)] * GROUP
        + [jax.ShapeDtypeStruct((8, HEAD_DIM), F32)],
        in_specs=[smem] * 3 + [vmem] * (8 + GROUP) + [ANY] * len(after),
        out_specs=[vmem] * (GROUP + 1),
        compiler_params=params(),
        cost_estimate=cost(1, 1),
        name="pack",
    )(
        place, tiles, readers, own, other, key_raw, values, query_raw, out_grad,
        key_gain, query_gain, *parts, *after,
    )


def raw_kernel(first, head, place_ref, value_ref, grad_ref, *outs):
    rows, width = value_ref.shape
    for d, out in enumerate(outs):
        wide = out.shape[1]
        at = (place_ref[0] ^ d) * (width // GROUP) + first * HEAD_DIM
        here = pl.ds(pl.multiple_of(at, HEAD_DIM), wide)
        out[:rows] = value_ref[:, here]
        out[rows:] = grad_ref[:, here]


def pack_raw(place, values, out_grad, first, count):
    shape = jax.ShapeDtypeStruct((2 * values.shape[0], count * HEAD_DIM), BF16)
    return heads_call(
        functools.partial(raw_kernel, first),
        1,
        place,
        [(values, 0), (out_grad, 0)],
        [(shape, 0)] * GROUP,
        name="pack_raw",
    )


def halves(refs, rows):
    if len(refs) == 2 * GROUP:
        return list(zip(refs[:GROUP], refs[GROUP:]))
    return [(ref.at[0 : 2 * rows], ref.at[2 * rows : ref.shape[0]]) for ref in refs]


def edges_kernel(head, place_ref, *refs):
    *blocks, near_ref, far_ref, token = refs
    rows = near_ref.shape[0] // 2
    me, plane = place_ref[0], place_ref[1]
    token[...] = jnp.zeros((8, HEAD_DIM), F32)
    even = plane % 2 == 0
    last, first = me ^ (GROUP - 1), me
    for d, block in enumerate(halves(blocks, rows)):

        @pl.when(jnp.where(even, last, first) == d)
        def _(block=block):
            near_ref[:rows] = block[1][:rows]
            near_ref[rows:] = block[0][:rows]

        @pl.when(jnp.where(even, first, last) == d)
        def _(block=block):
            far_ref[:rows] = block[1][:rows]
            far_ref[rows:] = block[0][:rows]


def block_rows(blocks):
    return (sum(x.shape[0] for x in blocks) // GROUP - FACTS) // 4


def edges(place, blocks, after):
    width = blocks[0].shape[1]
    rows = block_rows(blocks)
    half = jax.ShapeDtypeStruct((2 * rows, width), BF16)
    return heads_call(
        edges_kernel,
        1,
        place,
        [(block, 0) for block in blocks],
        [(half, 0), (half, 0), (jax.ShapeDtypeStruct((8, HEAD_DIM), F32), 0)],
        after,
        name="edges",
    )


def attend_kernel(outer, inputs, head, place_ref, *refs):
    blocks, refs = refs[:inputs], refs[inputs:]
    if outer:
        near, far, g_in, dq_out, acc_out, g_out, near_out, far_out, mid_out, end_out = refs[:10]
    else:
        dq_out, acc_out, g_out = refs[:3]
    pair, weights, sums, raw_g, pair_g, sums_g, facts_at = refs[-7:]
    me, plane = place_ref[0], place_ref[1]
    rows = block_rows(blocks)
    tiles = rows // TILE
    keys = slice(0, HEAD_DIM)
    vals = slice(HEAD_DIM, 2 * HEAD_DIM)

    if head == 0:
        weights[...] = jnp.zeros_like(weights)

    for d, (raw, normed) in enumerate(halves(blocks, rows)):
        j = me ^ d
        at = pl.multiple_of((j + 1) * rows, TILE)
        pair[pl.ds(at, rows), keys] = normed[0:rows]
        pair[pl.ds(at, rows), vals] = raw[0:rows]
        for tile in range(tiles):
            here = rows + tile * TILE
            weights[j * tiles + tile, :TILE, keys] = normed[here : here + TILE]
            weights[j * tiles + tile, TILE:, vals] = raw[here : here + TILE]
        facts_at[j] = normed[2 * rows : 2 * rows + 16].astype(F32)
        extra = normed[2 * rows + 16 : 2 * rows + 32].astype(F32)
        eight = pl.ds(pl.multiple_of(8 * j, 8), 8)
        raw_g[eight, keys] = extra[:8]
        raw_g[eight, vals] = extra[8:]
    pair_g[...] = raw_g[...].astype(BF16)
    if outer:
        even = plane % 2 == 0
        top = (GROUP + 1) * rows
        near_at = pl.multiple_of(jnp.where(even, top, 0), TILE)
        far_at = pl.multiple_of(jnp.where(even, 0, top), TILE)
        for ref, at in ((near, near_at), (far, far_at)):
            pair[pl.ds(at, rows), keys] = ref[0:rows]
            pair[pl.ds(at, rows), vals] = ref[rows : 2 * rows]
    sums[...] = jnp.zeros_like(sums)
    sums_g[...] = jnp.zeros_like(sums_g)
    count_g = pair_g.shape[0]
    row = lax.broadcasted_iota(jnp.int32, (count_g, HEAD_DIM), 0)
    lane = lax.broadcasted_iota(jnp.int32, (count_g, HEAD_DIM), 1)
    span = 4 * TILE
    units = []
    for j in (0, GROUP - 1) if outer else range(1, GROUP - 1):
        facts = facts_at[j]
        live = jnp.sum(jnp.where(row == lane, facts[0:1], 0.0), axis=1, keepdims=True) > 0.0
        for tile in range(tiles):
            start = jnp.max(facts[1 + tile : 2 + tile]).astype(jnp.int32)
            units.append((j * tiles + tile, pl.multiple_of(start * TILE, TILE), live))

    def products(unit):
        weight, at, _ = units[unit]
        both = jnp.concatenate([pair[pl.ds(at, span)], pair_g[...]], axis=0)
        return contract(both, weights[weight], ((1,), (1,)))

    ahead = products(0)
    for unit, (weight, at, live) in enumerate(units):
        product = ahead
        if unit + 1 < len(units):
            ahead = products(unit + 1)
        score = product[:, :TILE] * (FACTOR * LOG2_E)
        dprob = product[:, TILE:]
        score_g = jnp.where(live, score[span:], -jnp.inf)
        score = jnp.concatenate([score[:span], score_g], axis=0)
        largest = jnp.max(score, axis=0, keepdims=True)
        probs = jnp.exp2(score - largest)
        probs = probs * (1.0 / jnp.sum(probs, axis=0, keepdims=True))
        delta = jnp.sum(probs * dprob, axis=0, keepdims=True)
        dscore = (probs * ((dprob - delta) * FACTOR)).astype(BF16)
        grads = contract(
            jnp.concatenate([dscore, probs.astype(BF16)], axis=1), weights[weight], ((1,), (0,))
        )
        sums[pl.ds(at, span)] += grads[:span]
        sums_g[...] += grads[span:]
        both = jnp.concatenate([pair[pl.ds(at, span), keys], pair_g[:, keys]], axis=0)
        grad_query = contract(dscore, both, ((0,), (0,)))
        dq_out[unit * TILE : (unit + 1) * TILE] = grad_query.astype(BF16)
    acc_out[...] = sums[rows : (GROUP + 1) * rows].astype(BF16)
    if not outer:
        g_out[...] = sums_g[...]
    else:
        total_g = (g_in[...] + sums_g[...]).astype(BF16)
        row = lax.broadcasted_iota(jnp.int32, (8, 8 * GROUP), 0)
        col = lax.broadcasted_iota(jnp.int32, (8, 8 * GROUP), 1)
        for e, out in enumerate((g_out, near_out, mid_out, end_out)):
            hot = (col // 8 == row // G_DEV) & (col % 8 == G_DEV * e + row % G_DEV)
            part = contract(hot.astype(F32).astype(BF16), total_g, ((1,), (0,)))
            out[out.shape[0] - 16 :] = jnp.concatenate([part[:, keys], part[:, vals]], axis=0).astype(
                BF16
            )
        for out, at in ((near_out, near_at), (far_out, far_at)):
            out[:rows] = sums[pl.ds(at, rows), keys].astype(BF16)
            out[rows : 2 * rows] = sums[pl.ds(at, rows), vals].astype(BF16)


def attend(place, blocks, halo, inner_g, after):
    width = blocks[0].shape[1]
    rows = block_rows(blocks)
    wide = 2 * HEAD_DIM
    half = jax.ShapeDtypeStruct((2 * rows, width), BF16)
    few = jax.ShapeDtypeStruct((16, width), BF16)
    near = jax.ShapeDtypeStruct((2 * rows + 16, width), BF16)
    outs = [(half, HEAD_DIM), (jax.ShapeDtypeStruct((GROUP * rows, 2 * width), BF16), wide)]
    if halo:
        outs += [(x, HEAD_DIM) for x in (few, near, half, few, few)]
    else:
        outs += [(jax.ShapeDtypeStruct((8 * GROUP, 2 * width), F32), wide)]
    return heads_call(
        functools.partial(attend_kernel, len(halo) > 0, len(blocks)),
        width // HEAD_DIM,
        place,
        [(x, HEAD_DIM) for x in (*blocks, *halo)] + [(x, wide) for x in inner_g],
        outs,
        after,
        [
            pltpu.VMEM(((GROUP + 2) * rows, wide), BF16),
            pltpu.VMEM((GROUP * rows // TILE, 2 * TILE, wide), BF16),
            pltpu.VMEM(((GROUP + 2) * rows, wide), F32),
            pltpu.VMEM((8 * GROUP, wide), F32),
            pltpu.VMEM((8 * GROUP, wide), BF16),
            pltpu.VMEM((8 * GROUP, wide), F32),
            pltpu.VMEM((GROUP, 16, HEAD_DIM), F32),
        ],
        name="outer" if halo else "inner",
    )


def settle_kernel(
    head, place_ref, dq_in, acc_in, dq_out, acc_out, own_g, near, far, *refs
):
    *more, o0, o1, o2, o3, token = refs
    me, plane = place_ref[0], place_ref[1]
    token[...] = jnp.zeros((8, HEAD_DIM), F32)
    rows = dq_in.shape[0] // 2
    even = plane % 2 == 0
    inner = (plane == 1) | (plane == 2)
    part = (own_g[...].astype(F32) + near[2 * rows :].astype(F32)).astype(BF16)
    if more and head == 0:
        rest_g = (more[0][...].astype(F32) + more[1][...].astype(F32)).astype(BF16)
    for d, out in enumerate((o0, o1, o2, o3)):
        j = me ^ d
        near_here = j == jnp.where(even, GROUP - 1, 0)
        far_here = (j == jnp.where(even, 0, GROUP - 1)) & inner
        outside = (j == 0) | (j == GROUP - 1)

        @pl.when(outside)
        def _(out=out, j=j):
            out[:rows] = dq_out[pl.ds(pl.multiple_of(jnp.where(j == 0, 0, rows), TILE), rows)]

        @pl.when(~outside)
        def _(out=out, j=j):
            out[:rows] = dq_in[pl.ds(pl.multiple_of(jnp.where(j == 1, 0, rows), TILE), rows)]

        here = pl.ds(pl.multiple_of(j * rows, TILE), rows)
        for i in range(2):
            lanes = slice(i * HEAD_DIM, (i + 1) * HEAD_DIM)
            rest = slice(i * rows, (i + 1) * rows)
            total = acc_in[here, lanes].astype(F32) + acc_out[here, lanes].astype(F32)
            total = total + jnp.where(near_here, near[rest].astype(F32), 0.0)
            total = total + jnp.where(far_here, far[rest].astype(F32), 0.0)
            out[(i + 1) * rows : (i + 2) * rows] = total.astype(BF16)
        out[3 * rows : 3 * rows + 16] = part
        if more and head == 0:
            for h in range(rest_g.shape[1] // HEAD_DIM):
                at = 3 * rows + 16 * (h + 1)
                out[at : at + 16] = rest_g[:, h * HEAD_DIM : (h + 1) * HEAD_DIM]


def settle(place, inner, outer, own_g, near, far, more, after):
    rows, width = inner[0].shape
    rows = rows // 2
    part = (HEAD_DIM, 2 * HEAD_DIM)
    extra = 16 + 16 * (more[0].shape[1] // HEAD_DIM if more else 0)
    home = jax.ShapeDtypeStruct((3 * rows + extra, width), BF16)
    return heads_call(
        settle_kernel,
        width // HEAD_DIM,
        place,
        [*zip(inner, part), *zip(outer, part)]
        + [(x, HEAD_DIM) for x in (own_g, near, far)]
        + [(x, 0) for x in more],
        [(home, HEAD_DIM)] * GROUP + [(jax.ShapeDtypeStruct((8, HEAD_DIM), F32), 0)],
        after,
        name="settle",
    )


def join_kernel(head, place_ref, *refs):
    *parts, mid, end = refs
    half = len(parts) // 2
    for out, some in ((mid, parts[:half]), (end, parts[half:])):
        first = 0
        for part in some:
            out[:, first : first + part.shape[1]] = part[...]
            first += part.shape[1]


def join(place, mids, ends):
    shape = jax.ShapeDtypeStruct((16, sum(x.shape[1] for x in mids)), BF16)
    return heads_call(
        join_kernel,
        1,
        place,
        [(x, 0) for x in (*mids, *ends)],
        [(shape, 0), (shape, 0)],
        name="join",
    )


def total_kernel(chunks, place_ref, ids_ref, raw_ref, query, key, query_gain, gain_ref, *refs):
    *refs, out, sums = refs
    homes, dot_refs = refs[: GROUP * len(chunks)], refs[GROUP * len(chunks) :]
    rows, width = out.shape[0], sums.shape[1]
    me = place_ref[0]
    device = place_ref[1] * GROUP + me
    total = part_dots(
        sum(chunks[:-1]), me, homes[-GROUP:], query, key, query_gain, gain_ref
    )
    for ref in dot_refs:
        total = total + ref[...]
    few = lax.broadcasted_iota(jnp.int32, (16, HEAD_DIM), 0)
    eight = lax.broadcasted_iota(jnp.int32, (8, HEAD_DIM), 0)
    hot = [few == 8 * i + G_DEV * me + r for i in range(2) for r in range(G_DEV)]
    dot = [jnp.zeros((1, HEAD_DIM), F32) for _ in range(G_DEV)]
    for d in range(GROUP):
        first = 0
        for c, count in enumerate(chunks):
            for h in range(count):
                home = homes[c * GROUP + d]
                last = homes[(len(chunks) - 1) * GROUP + d]
                at = 3 * rows + 16 * (first + h + 1)
                part = home[3 * rows : 3 * rows + 16, h * HEAD_DIM : (h + 1) * HEAD_DIM].astype(F32)
                part = part + last[at : at + 16, :HEAD_DIM].astype(F32)
                found = [jnp.sum(jnp.where(x, part, 0.0), axis=0, keepdims=True) for x in hot]
                at = pl.multiple_of(
                    (me ^ d) * (width // GROUP) + (first + h) * HEAD_DIM, HEAD_DIM
                )
                here = pl.ds(at, HEAD_DIM)
                block = jnp.zeros((8, HEAD_DIM), F32)
                for i, x in enumerate(found):
                    block = jnp.where(eight == i, x, block)
                sums[:, here] = block
                raw = raw_ref[:, here].astype(F32)
                for r in range(G_DEV):
                    dot[r] = dot[r] + found[r] * gain_ref[:, here] * raw[r : r + 1]
            first += count
    row = lax.broadcasted_iota(jnp.int32, (rows, HEAD_DIM), 0)
    lane = lax.broadcasted_iota(jnp.int32, (rows, HEAD_DIM), 1)
    for r in range(G_DEV):
        here = (row == ids_ref[r] - device * rows) & (lane >= HEAD_DIM // 2)
        total = total + jnp.where(here, jnp.sum(dot[r], axis=1, keepdims=True), 0.0)
    out[...] = total


def total_dots(place, ids, raw, query_raw, key_raw, gains, homes, dots, chunks):
    smem = pl.BlockSpec(memory_space=pltpu.SMEM)
    vmem = pl.BlockSpec(memory_space=pltpu.VMEM)
    flat = [x for home in homes for x in home]
    raw_rows = query_raw.shape[0]
    return pl.pallas_call(
        functools.partial(total_kernel, chunks),
        out_shape=[
            jax.ShapeDtypeStruct((raw_rows, HEAD_DIM), F32),
            jax.ShapeDtypeStruct((8, raw.shape[1]), F32),
        ],
        in_specs=[smem, smem] + [vmem] * (5 + len(flat) + len(dots)),
        out_specs=[vmem, vmem],
        compiler_params=params(),
        cost_estimate=cost(1, 1),
        name="total_dots",
    )(place, ids, raw, query_raw, key_raw, *gains, *flat, *dots)


def part_dots(first, me, homes, query, key, query_gain, key_gain):
    rows, width = query.shape
    each = width // HEAD_DIM // GROUP
    totals = [jnp.zeros((rows, HEAD_DIM), F32), jnp.zeros((rows, HEAD_DIM), F32)]
    for d, grads in enumerate(homes):
        for h in range(grads.shape[1] // HEAD_DIM):
            at = ((me ^ d) * each + first + h) * HEAD_DIM
            here = pl.ds(pl.multiple_of(at, HEAD_DIM), HEAD_DIM)
            lanes = slice(h * HEAD_DIM, (h + 1) * HEAD_DIM)
            for i, (raw, gain) in enumerate(((query, query_gain), (key, key_gain))):
                grad = grads[i * rows : (i + 1) * rows, lanes].astype(F32)
                totals[i] += grad * gain[:, here] * raw[:, here].astype(F32)
    sums = [jnp.sum(x, axis=1, keepdims=True) for x in totals]
    return lane_pair(*sums, rows)


def dots_kernel(first, head, place_ref, *refs):
    refs[-1][...] = part_dots(first, place_ref[0], refs[:GROUP], *refs[GROUP:-1])


def dots(place, grads, query_raw, key_raw, gains, first, after):
    return heads_call(
        functools.partial(dots_kernel, first),
        1,
        place,
        [(x, 0) for x in (*grads, query_raw, key_raw, *gains)],
        [(jax.ShapeDtypeStruct((query_raw.shape[0], HEAD_DIM), F32), 0)],
        after,
        name="dots",
    )[0]


def finish_kernel(chunks, place_ref, ids_ref, own_ref, other_ref, dot_ref, dot_other_ref, *refs):
    me = place_ref[0]
    device = place_ref[1] * GROUP + me
    grads = refs[: GROUP * len(chunks)]
    sum_ref, query_ref, key_ref, query_gain, key_gain = refs[GROUP * len(chunks) : -3]
    query_out, key_out, value_out = refs[-3:]
    rows, width = query_ref.shape
    block = query_out.shape[0]
    each = width // GROUP
    start = pl.program_id(0) * block
    now = pl.ds(pl.multiple_of(start, block), block)
    inv = inverses(own_ref[now], other_ref[now])
    total = dot_ref[now] + dot_other_ref[now]
    dot = (total[:, :1], total[:, HEAD_DIM // 2 : HEAD_DIM // 2 + 1])
    coeff = [inv[i] * inv[i] * inv[i] * (dot[i] / D) for i in range(2)]
    row = lax.broadcasted_iota(jnp.int32, (block, HEAD_DIM), 0) + start
    hot = [row == ids_ref[r] - device * rows for r in range(G_DEV)]
    for d in range(GROUP):
        first = 0
        for c, count in enumerate(chunks):
            ref = grads[c * GROUP + d]
            for h in range(count):
                at = pl.multiple_of((me ^ d) * each + (first + h) * HEAD_DIM, HEAD_DIM)
                here = pl.ds(at, HEAD_DIM)
                col = slice(h * HEAD_DIM, (h + 1) * HEAD_DIM)
                grad = [
                    ref[pl.ds(pl.multiple_of(start + i * rows, block), block), col].astype(F32)
                    for i in range(3)
                ]
                for i in (1, 2):
                    for r in range(G_DEV):
                        more = sum_ref[2 * (i - 1) + r : 2 * (i - 1) + r + 1, here]
                        grad[i] = grad[i] + jnp.where(hot[r], more, 0.0)
                for i, (raw, gain, out) in enumerate(
                    ((query_ref, query_gain, query_out), (key_ref, key_gain, key_out))
                ):
                    out[:, here] = (
                        inv[i] * (grad[i] * gain[:, here]) - raw[now, here].astype(F32) * coeff[i]
                    ).astype(BF16)
                value_out[:, here] = grad[2].astype(BF16)
            first += count


def finish(place, ids, own, other, dot, dot_other, sums, grads, query_raw, key_raw, gains, chunks):
    rows, width = query_raw.shape
    smem = pl.BlockSpec(memory_space=pltpu.SMEM)
    vmem = pl.BlockSpec(memory_space=pltpu.VMEM)
    flat = [x for chunk in grads for x in chunk]
    block = pl.BlockSpec((rows // FINISH_STEPS, width), lambda i: (i, 0))
    return pl.pallas_call(
        functools.partial(finish_kernel, chunks),
        out_shape=[jax.ShapeDtypeStruct(query_raw.shape, BF16)] * 3,
        grid=(FINISH_STEPS,),
        in_specs=[smem, smem] + [vmem] * (4 + len(flat) + 5),
        out_specs=[block] * 3,
        compiler_params=params(),
        cost_estimate=cost(1, 1),
        name="finish",
    )(place, ids, own, other, dot, dot_other, *flat, sums, query_raw, key_raw, *gains)


def swap_heads(x):
    return lax.ppermute(x, "head", [(0, 1), (1, 0)])


def plane_body(
    query_raw, key_raw, values, out_grad, query_gain, key_gain, key_tiles, global_ids, readers
):
    device = lax.axis_index("ctx")
    place = jnp.stack([device % GROUP, device // GROUP]).astype(jnp.int32)
    gains = (query_gain[None, :], key_gain[None, :])
    own = squares(query_raw, key_raw)
    other = swap_heads(own)
    arrays = (query_raw, key_raw, values, out_grad)
    mine, raw_rows = global_rows(place, global_ids, own, other, key_raw, values, gains[1])
    parts = [mine] + [swapped(mine, 4 * e) for e in range(1, GROUP)]
    chunks = len(CHUNKS)
    firsts = [sum(CHUNKS[:c]) for c in range(chunks)]
    packed, token = [], ()

    def spread(sent):
        return [sent[0]] + [swapped(sent[d], d) for d in range(1, GROUP)]

    raw = spread(pack_raw(place, values, out_grad, 0, CHUNKS[0]))
    token = tuple(raw[1:])
    for first, count in zip(firsts, CHUNKS):
        *sent, last = pack(
            place, key_tiles, readers, own, other, arrays, gains, parts, first, count, first > 0,
            token,
        )
        token = (last,)
        packed.append((raw if first == 0 else []) + spread(sent))
    edge, inner, outer, back, home, dot = ({} for _ in range(6))
    fars = []

    def begin(c, token):
        near, far, last = edges(place, packed[c], token)
        edge[c] = (swapped(near, 4), swapped_edges(far))
        return (last,)

    def inside(c, token):
        inner[c] = attend(place, packed[c], (), (), token)
        return (inner[c][2],)

    def outside(c, token):
        results = attend(place, packed[c], edge[c], (inner[c][2],), token)
        outer[c], own_g, near, far, mid, last = results[:2], *results[2:]
        fars.append((mid, last))
        more = ()
        if c == chunks - 1:
            mids, lasts = zip(*fars)
            mid, last = join(place, mids, lasts)
            more = (swapped(mid, 8), swapped(last, 12))
        back[c] = (own_g, swapped(near, 4), swapped_edges(far), more)
        return (own_g,)

    def end(c, token):
        *sent, last = settle(place, inner[c][:2], outer[c], *back[c], token)
        home[c] = [sent[0]] + [swapped(sent[d], d) for d in range(1, GROUP)]
        return (last,)

    def score(c, token):
        dot[c] = dots(place, home[c], query_raw, key_raw, gains, firsts[c], token)
        return (dot[c],)

    stages = {"b": begin, "i": inside, "g": outside, "e": end, "s": score}
    for step in " ".join(ORDER).split():
        name, *extra = step.split(":")
        held = tuple(x for e in extra for x in edge[int(e[1])])
        token = stages[name[0]](int(name[1]), token + held)
    homes = [home[c] for c in range(chunks)]
    total, sums = total_dots(
        place, global_ids, raw_rows, query_raw, key_raw, gains, homes, list(dot.values()), CHUNKS
    )
    return tuple(
        finish(
            place, global_ids, own, other, total, swap_heads(total), sums, homes,
            query_raw, key_raw, gains, CHUNKS,
        )
    )


def passed_along(shard, axis, by):
    count = lax.axis_size(axis)
    return lax.ppermute(shard, axis, [(i, (i + by) % count) for i in range(count)])


def normalize(as_float, gain, squares):
    inverse = lax.rsqrt(squares[:, None] / D + EPSILON)
    return (inverse, (as_float * inverse * gain).astype(jnp.bfloat16))


def norm_grad(as_float, inverse, scaled, coeffs):
    return (inverse * scaled - as_float * inverse**3 * (coeffs[:, None] / D)).astype(jnp.bfloat16)


def body(
    query_raw, key_raw, values, out_grad, query_gain, key_gain, key_tiles, global_ids, readers
):
    tokens_here, width_here = query_raw.shape
    heads_here = width_here // HEAD_DIM
    tiles_here = tokens_here // TILE
    factor = HEAD_DIM ** (-0.5)
    device = lax.axis_index("ctx")
    query_rows = query_raw.astype(jnp.float32)
    key_rows = key_raw.astype(jnp.float32)
    query_sq, key_sq = lax.psum(
        (jnp.sum(query_rows * query_rows, axis=1), jnp.sum(key_rows * key_rows, axis=1)), "head"
    )
    query_inv, query_norm = normalize(query_rows, query_gain, query_sq)
    key_inv, key_norm = normalize(key_rows, key_gain, key_sq)
    own_rows = global_ids - device * tokens_here
    own_pair = jnp.stack([key_norm[own_rows], values[own_rows]])
    global_pair = lax.all_gather(own_pair, "ctx", axis=1, tiled=True)
    global_keys = global_pair[0].reshape(-1, heads_here, HEAD_DIM)
    global_vals = global_pair[1].reshape(-1, heads_here, HEAD_DIM)
    live_mask = jnp.repeat(readers[0] > 0, G_DEV)
    key_value = jnp.stack([key_norm, values])
    current = passed_along(key_value, "ctx", -REACH)
    pieces = [current]
    for hop_index in range(2 * REACH):
        current = passed_along(current, "ctx", 1)
        pieces.append(current)
    pieces = pieces[::-1]
    window_pair = jnp.concatenate(pieces, axis=1)
    first_tile = (device - REACH) * tiles_here
    local_tiles = key_tiles - first_tile
    window_rows = (
        local_tiles[:, :, None] * TILE + jnp.arange(TILE, dtype=jnp.int32)[None, None, :]
    ).reshape(tiles_here, -1)
    window_count = window_rows.shape[1]
    window_keys = window_pair[0][window_rows].reshape(
        tiles_here, window_count, heads_here, HEAD_DIM
    )
    window_vals = window_pair[1][window_rows].reshape(
        tiles_here, window_count, heads_here, HEAD_DIM
    )
    query_four = query_norm.reshape(tiles_here, TILE, heads_here, HEAD_DIM)
    grad_four = out_grad.reshape(tiles_here, TILE, heads_here, HEAD_DIM)

    def head_block(head_number):
        query_head = lax.dynamic_index_in_dim(query_four, head_number, 2, keepdims=False)
        grad_head = lax.dynamic_index_in_dim(grad_four, head_number, 2, keepdims=False)
        wkeys = lax.dynamic_index_in_dim(window_keys, head_number, 2, keepdims=False)
        wvals = lax.dynamic_index_in_dim(window_vals, head_number, 2, keepdims=False)
        gkeys = lax.dynamic_index_in_dim(global_keys, head_number, 1, keepdims=False)
        gvals = lax.dynamic_index_in_dim(global_vals, head_number, 1, keepdims=False)
        score_window = (
            jnp.einsum("tqd,tkd->tqk", query_head, wkeys, preferred_element_type=jnp.float32)
            * factor
        )
        score_global = (
            jnp.einsum("tqd,kd->tqk", query_head, gkeys, preferred_element_type=jnp.float32)
            * factor
        )
        score_global = jnp.where(live_mask, score_global, -jnp.inf)
        scores = jnp.concatenate([score_window, score_global], axis=2)
        largest = jnp.max(scores, axis=2, keepdims=True)
        log_total = largest + jnp.log(jnp.sum(jnp.exp(scores - largest), axis=2, keepdims=True))
        probs = jnp.exp(scores - log_total)
        probs_low = probs.astype(jnp.bfloat16)
        attended = jnp.einsum(
            "tqk,tkd->tqd", probs_low[..., :window_count], wvals, preferred_element_type=jnp.float32
        )
        attended = attended + jnp.einsum(
            "tqk,kd->tqd", probs_low[..., window_count:], gvals, preferred_element_type=jnp.float32
        )
        attended = lax.optimization_barrier(attended.astype(jnp.bfloat16))
        delta_rows = jnp.sum(grad_head.astype(jnp.float32) * attended.astype(jnp.float32), axis=2)
        dprob = jnp.concatenate(
            [
                jnp.einsum("tqd,tkd->tqk", grad_head, wvals, preferred_element_type=jnp.float32),
                jnp.einsum("tqd,kd->tqk", grad_head, gvals, preferred_element_type=jnp.float32),
            ],
            axis=2,
        )
        dscore = (probs * (dprob - delta_rows[..., None]) * factor).astype(jnp.bfloat16)
        grad_query = jnp.einsum(
            "tqk,tkd->tqd", dscore[..., :window_count], wkeys, preferred_element_type=jnp.float32
        )
        grad_query = grad_query + jnp.einsum(
            "tqk,kd->tqd", dscore[..., window_count:], gkeys, preferred_element_type=jnp.float32
        )
        window_dk = jnp.einsum(
            "tqk,tqd->tkd",
            dscore[..., :window_count],
            query_head,
            preferred_element_type=jnp.float32,
        )
        window_dv = jnp.einsum(
            "tqk,tqd->tkd",
            probs_low[..., :window_count],
            grad_head,
            preferred_element_type=jnp.float32,
        )
        global_dk = jnp.einsum(
            "tqk,tqd->kd",
            dscore[..., window_count:],
            query_head,
            preferred_element_type=jnp.float32,
        )
        global_dv = jnp.einsum(
            "tqk,tqd->kd",
            probs_low[..., window_count:],
            grad_head,
            preferred_element_type=jnp.float32,
        )
        return (grad_query, window_dk, window_dv, global_dk, global_dv)

    head_results = lax.map(head_block, jnp.arange(heads_here, dtype=jnp.int32))
    grad_query = jnp.moveaxis(head_results[0], 0, 2).reshape(tokens_here, width_here)
    window_dk = jnp.moveaxis(head_results[1], 0, 2).reshape(-1, width_here)
    window_dv = jnp.moveaxis(head_results[2], 0, 2).reshape(-1, width_here)
    global_dk = jnp.moveaxis(head_results[3], 0, 1).reshape(-1, width_here)
    global_dv = jnp.moveaxis(head_results[4], 0, 1).reshape(-1, width_here)
    window_grads = jnp.zeros((2, window_pair.shape[1], width_here), jnp.float32)
    window_grads = window_grads.at[:, window_rows.reshape(-1)].add(
        jnp.stack([window_dk, window_dv])
    )
    spread_grads = window_grads.reshape(2, 2 * REACH + 1, tokens_here, width_here)
    slots = [spread_grads[:, slot_index] for slot_index in range(2 * REACH + 1)]
    carried = slots[2 * REACH]
    for hop_index in range(2 * REACH):
        carried = (
            passed_along(carried.astype(jnp.bfloat16), "ctx", 1).astype(carried.dtype)
            + slots[2 * REACH - 1 - hop_index]
        )
    home_grads = passed_along(carried.astype(jnp.bfloat16), "ctx", -REACH).astype(carried.dtype)
    global_part = lax.psum_scatter(
        jnp.stack([global_dk, global_dv]), "ctx", scatter_dimension=1, tiled=True
    )
    home_grads = home_grads.at[:, own_rows].add(global_part)
    scaled_query = grad_query * query_gain
    scaled_key = home_grads[0] * key_gain
    query_dot, key_dot = lax.psum(
        (jnp.sum(scaled_query * query_rows, axis=1), jnp.sum(scaled_key * key_rows, axis=1)), "head"
    )
    query_grad = norm_grad(query_rows, query_inv, scaled_query, query_dot)
    key_grad = norm_grad(key_rows, key_inv, scaled_key, key_dot)
    return (query_grad, key_grad, home_grads[1].astype(jnp.bfloat16))


def solution(mesh):
    sizes = dict(mesh.shape)
    planes = sizes["ctx"] == GROUP * GROUP and sizes["head"] == 2
    return jax.shard_map(
        plane_body if planes else body,
        mesh=mesh,
        in_specs=(
            P("ctx", "head"),
            P("ctx", "head"),
            P("ctx", "head"),
            P("ctx", "head"),
            P("head"),
            P("head"),
            P("ctx", None),
            P("ctx"),
            P("ctx", None),
        ),
        out_specs=(P("ctx", "head"), P("ctx", "head"), P("ctx", "head")),
        check_vma=False,
    )
```

```python
import functools

import jax
import jax.numpy as jnp
from jax import lax
from jax.experimental import pallas as pl
from jax.experimental.pallas import tpu as pltpu
from jax.sharding import PartitionSpec as P

HEAD_DIM = 128
D = 5120
TILE = 128
REACH = 1
G_DEV = 2
GROUP = 4
CHUNKS = (2, 2, 1)
ORDER = ("b0 i0 g0 b1", "i1 e0 b2 g1", "i2:z2 s0 e1 g2", "e2 s1",)


EPSILON = 1e-06
FACTOR = HEAD_DIM ** (-0.5)
LOG2_E = 1.4426950408889634
FACTS = 32
FINISH_STEPS = 4
F32 = jnp.float32
BF16 = jnp.bfloat16
ANY = pl.BlockSpec(memory_space=pl.ANY)
VMEM_LIMIT = 48 * 1024 * 1024


def swapped(shard, bit):
    count = lax.axis_size("ctx")
    return lax.ppermute(shard, "ctx", [(i, i ^ bit) for i in range(count)])


def swapped_edges(shard):
    count = lax.axis_size("ctx")
    pairs = [(i, i ^ 12) for i in range(count) if i // GROUP % GROUP in (1, 2)]
    return lax.ppermute(shard, "ctx", pairs)


def params():
    return pltpu.CompilerParams(vmem_limit_bytes=VMEM_LIMIT)


def cost(flops, read):
    return pl.CostEstimate(flops=1, bytes_accessed=1, transcendentals=0)


def behind(kernel, inputs, tokens):
    def run(*refs):
        kernel(*refs[:inputs], *refs[inputs + tokens :])

    return run


def heads_call(
    kernel, count, place, inputs, outputs, after=(), scratch=(), aliases={}, name=None
):
    lanes = [(entry[1], entry[2] if len(entry) > 2 else 0) for entry in (*inputs, *outputs)]

    def run(place_ref, *refs):
        refs = refs[: len(inputs)] + refs[len(inputs) + len(after) :]
        for h in range(count):
            views = [
                ref.at[:, at + h * w : at + (h + 1) * w] if w else ref
                for ref, (w, at) in zip(refs, lanes)
            ]
            kernel(h, place_ref, *views, *refs[len(lanes) :])

    vmem = pl.BlockSpec(memory_space=pltpu.VMEM)
    return pl.pallas_call(
        run,
        out_shape=[entry[0] for entry in outputs],
        in_specs=[pl.BlockSpec(memory_space=pltpu.SMEM)]
        + [vmem] * len(inputs)
        + [ANY] * len(after),
        out_specs=[vmem] * len(outputs),
        scratch_shapes=scratch,
        input_output_aliases={1 + i: o for i, o in aliases.items()},
        compiler_params=params(),
        cost_estimate=cost(1, 1),
        name=name,
    )(place, *[x for x, _ in inputs], *after)


def contract(a, b, dims, precision=None):
    return lax.dot_general(
        a, b, (dims, ((), ())), precision=precision, preferred_element_type=F32
    )


def lane_pair(first, second, rows):
    lane = lax.broadcasted_iota(jnp.int32, (rows, HEAD_DIM), 1)
    return jnp.where(lane < HEAD_DIM // 2, first, second)


def squares_kernel(query_ref, key_ref, out_ref):
    rows, width = query_ref.shape
    step = rows // 4
    for at in range(0, rows, step):
        part = []
        for ref in (query_ref, key_ref):
            x = ref[at : at + step].astype(F32)
            part.append(jnp.sum(x * x, axis=1, keepdims=True))
        out_ref[at : at + step] = lane_pair(*part, step)


def squares(query_raw, key_raw):
    rows, width = query_raw.shape
    vmem = pl.BlockSpec(memory_space=pltpu.VMEM)
    return pl.pallas_call(
        squares_kernel,
        out_shape=jax.ShapeDtypeStruct((rows, HEAD_DIM), F32),
        in_specs=[vmem] * 2,
        out_specs=vmem,
        compiler_params=params(),
        cost_estimate=cost(1, 1),
        name="squares",
    )(query_raw, key_raw)


def inverses(own, other):
    both = lax.rsqrt((own + other) / D + EPSILON)
    return both[:, :1], both[:, HEAD_DIM // 2 : HEAD_DIM // 2 + 1]


def rows_kernel(place_ref, ids_ref, own_ref, other_ref, key_ref, value_ref, gain_ref, out, raw):
    rows, width = key_ref.shape
    block = width // GROUP
    device = place_ref[1] * GROUP + place_ref[0]
    row = lax.broadcasted_iota(jnp.int32, (16, width), 0)
    keys, found, vals = [], [], []
    for r in range(G_DEV):
        at = ids_ref[r] - device * rows
        base = pl.multiple_of(at // 16 * 16, 16)
        here = pl.ds(base, 16)
        _, inv = inverses(own_ref[here], other_ref[here])
        hot = row == at - base

        def only(x):
            return jnp.sum(jnp.where(hot, x, 0.0), axis=0, keepdims=True)

        key = key_ref[here].astype(F32)
        keys.append(only(key))
        found.append(only((key * inv * gain_ref[...]).astype(BF16).astype(F32)))
        vals.append(only(value_ref[here].astype(F32)))
    raw[...] = jnp.where(row == 0, keys[0], keys[1]).astype(BF16)
    total = jnp.zeros((16, block), F32)
    row = lax.broadcasted_iota(jnp.int32, (16, block), 0)
    for g in range(GROUP):
        for i, x in enumerate(found + vals):
            total = jnp.where(row == 4 * g + i, x[:, g * block : (g + 1) * block], total)
    out[...] = total.astype(BF16)


def global_rows(place, ids, own, other, key_raw, values, key_gain):
    rows, width = key_raw.shape
    smem = pl.BlockSpec(memory_space=pltpu.SMEM)
    vmem = pl.BlockSpec(memory_space=pltpu.VMEM)
    return pl.pallas_call(
        rows_kernel,
        out_shape=[
            jax.ShapeDtypeStruct((16, width // GROUP), BF16),
            jax.ShapeDtypeStruct((16, width), BF16),
        ],
        in_specs=[smem, smem] + [vmem] * 5,
        out_specs=[vmem] * 2,
        compiler_params=params(),
        cost_estimate=cost(1, 1),
        name="global_rows",
    )(place, ids, own, other, key_raw, values, key_gain)


def add_globals(me, d, first, parts, out):
    parts = jnp.concatenate([ref[...] for ref in parts], axis=0)
    row = lax.broadcasted_iota(jnp.int32, (16, 16 * GROUP), 0)
    col = lax.broadcasted_iota(jnp.int32, (16, 16 * GROUP), 1)
    spot = col % 16 - 4 * (me ^ d)
    hot = (spot >= 0) & (spot < 4)
    hot = hot & (row == 2 * (col // 16) + spot % 2 + 8 * (spot // 2))
    hot = hot.astype(F32).astype(BF16)
    chosen = parts[:, first * HEAD_DIM : first * HEAD_DIM + out.shape[1]]
    out[out.shape[0] - 16 :] = contract(hot, chosen, ((1,), (0,))).astype(BF16)


def append_kernel(first, head, place_ref, *refs):
    for d, out in enumerate(refs[2 * GROUP :]):
        add_globals(place_ref[0], d, first, refs[GROUP : 2 * GROUP], out)


def append(place, sent, parts, first, after):
    return heads_call(
        functools.partial(append_kernel, first),
        1,
        place,
        [(x, 0) for x in (*sent, *parts)],
        [(jax.ShapeDtypeStruct(x.shape, BF16), 0) for x in sent],
        after,
        aliases={d: d for d in range(GROUP)},
        name="append",
    )


def pack_kernel(first, whole, place_ref, tiles_ref, readers_ref, own_ref, other_ref, *refs):
    me, plane = place_ref[0], place_ref[1]
    query_inv, key_inv = inverses(own_ref[...], other_ref[...])
    rows = own_ref.shape[0]
    row = lax.broadcasted_iota(jnp.int32, (16, HEAD_DIM), 0)
    lane = lax.broadcasted_iota(jnp.int32, (16, HEAD_DIM), 1)
    facts = jnp.zeros((16, HEAD_DIM), jnp.int32)
    for tile in range(rows // TILE):
        start = tiles_ref[tile, 0] - (plane * GROUP - 1) * (rows // TILE)
        facts = jnp.where(row == 1 + tile, start, facts)
    for e in range(GROUP):
        for j in range(GROUP):
            live = readers_ref[0, (plane ^ e) * GROUP + j]
            chosen = (row == 0) & (lane // G_DEV == GROUP * j + e)
            facts = jnp.where(chosen, live, facts)
    facts = facts.astype(F32).astype(BF16)
    key_ref, value_ref, query_ref, grad_ref, key_gain, query_gain = refs[:6]
    *outs, token = refs[-GROUP - 1 :]
    token[...] = jnp.zeros((8, HEAD_DIM), F32)
    each = key_ref.shape[1] // HEAD_DIM // GROUP
    for d, out in enumerate(outs):
        top = 2 * rows if whole else 0
        if whole:
            add_globals(me, d, first, refs[6 : 6 + GROUP], out)
        for h in range(out.shape[1] // HEAD_DIM):
            at = pl.multiple_of(((me ^ d) * each + first + h) * HEAD_DIM, HEAD_DIM)
            here = pl.ds(at, HEAD_DIM)
            lanes = slice(h * HEAD_DIM, (h + 1) * HEAD_DIM)
            key = key_ref[:, here].astype(F32)
            query = query_ref[:, here].astype(F32)
            if whole:
                out[0:rows, lanes] = value_ref[:, here]
                out[rows : 2 * rows, lanes] = grad_ref[:, here]
            out[top : top + rows, lanes] = (key * key_inv * key_gain[:, here]).astype(BF16)
            out[top + rows : top + 2 * rows, lanes] = (
                query * query_inv * query_gain[:, here]
            ).astype(BF16)
            out[top + 2 * rows : top + 2 * rows + 16, lanes] = facts


def pack(place, tiles, readers, own, other, arrays, gains, parts, first, count, whole, after):
    query_raw, key_raw, values, out_grad = arrays
    query_gain, key_gain = gains
    rows, width = query_raw.shape
    smem = pl.BlockSpec(memory_space=pltpu.SMEM)
    vmem = pl.BlockSpec(memory_space=pltpu.VMEM)
    out_rows = (4 if whole else 2) * rows + FACTS
    kernel = functools.partial(pack_kernel, first, whole)
    return pl.pallas_call(
        behind(kernel, 11 + len(parts), len(after)),
        out_shape=[jax.ShapeDtypeStruct((out_rows, count * HEAD_DIM), BF16)] * GROUP
        + [jax.ShapeDtypeStruct((8, HEAD_DIM), F32)],
        in_specs=[smem] * 3 + [vmem] * (8 + len(parts)) + [ANY] * len(after),
        out_specs=[vmem] * (GROUP + 1),
        compiler_params=params(),
        cost_estimate=cost(1, 1),
        name="pack",
    )(
        place, tiles, readers, own, other, key_raw, values, query_raw, out_grad,
        key_gain, query_gain, *parts, *after,
    )


def raw_kernel(first, head, place_ref, value_ref, grad_ref, *outs):
    rows, width = value_ref.shape
    for d, out in enumerate(outs):
        wide = out.shape[1]
        at = (place_ref[0] ^ d) * (width // GROUP) + first * HEAD_DIM
        here = pl.ds(pl.multiple_of(at, HEAD_DIM), wide)
        out[:rows] = value_ref[:, here]
        out[rows:] = grad_ref[:, here]


def pack_raw(place, values, out_grad, first, count):
    shape = jax.ShapeDtypeStruct((2 * values.shape[0], count * HEAD_DIM), BF16)
    return heads_call(
        functools.partial(raw_kernel, first),
        1,
        place,
        [(values, 0), (out_grad, 0)],
        [(shape, 0)] * GROUP,
        name="pack_raw",
    )


def halves(refs, rows):
    if len(refs) == 2 * GROUP:
        return list(zip(refs[:GROUP], refs[GROUP:]))
    return [(ref.at[0 : 2 * rows], ref.at[2 * rows : ref.shape[0]]) for ref in refs]


def edges_kernel(head, place_ref, *refs):
    *blocks, near_ref, far_ref, token = refs
    rows = near_ref.shape[0] // 2
    me, plane = place_ref[0], place_ref[1]
    token[...] = jnp.zeros((8, HEAD_DIM), F32)
    even = plane % 2 == 0
    last, first = me ^ (GROUP - 1), me
    for d, block in enumerate(halves(blocks, rows)):

        @pl.when(jnp.where(even, last, first) == d)
        def _(block=block):
            near_ref[:rows] = block[1][:rows]
            near_ref[rows:] = block[0][:rows]

        @pl.when(jnp.where(even, first, last) == d)
        def _(block=block):
            far_ref[:rows] = block[1][:rows]
            far_ref[rows:] = block[0][:rows]


def block_rows(blocks):
    return (sum(x.shape[0] for x in blocks) // GROUP - FACTS) // 4


def edges(place, blocks, after):
    width = blocks[0].shape[1]
    rows = block_rows(blocks)
    half = jax.ShapeDtypeStruct((2 * rows, width), BF16)
    return heads_call(
        edges_kernel,
        1,
        place,
        [(block, 0) for block in blocks],
        [(half, 0), (half, 0), (jax.ShapeDtypeStruct((8, HEAD_DIM), F32), 0)],
        after,
        name="edges",
    )


def attend_kernel(outer, inputs, head, place_ref, *refs):
    blocks, refs = refs[:inputs], refs[inputs:]
    if outer:
        near, far, g_in = refs[:3]
        dq_out, acc_out, g_out, near_out, far_out, mid_out, end_out = refs[-14:-7]
    else:
        dq_out, acc_out, g_out = refs[:3]
    pair, weights, sums, raw_g, pair_g, sums_g, facts_at = refs[-7:]
    me, plane = place_ref[0], place_ref[1]
    rows = block_rows(blocks)
    tiles = rows // TILE
    keys = slice(0, HEAD_DIM)
    vals = slice(HEAD_DIM, 2 * HEAD_DIM)

    if head == 0:
        weights[...] = jnp.zeros_like(weights)

    for d, (raw, normed) in enumerate(halves(blocks, rows)):
        j = me ^ d
        at = pl.multiple_of((j + 1) * rows, TILE)
        pair[pl.ds(at, rows), keys] = normed[0:rows]
        pair[pl.ds(at, rows), vals] = raw[0:rows]
        for tile in range(tiles):
            here = rows + tile * TILE
            weights[j * tiles + tile, :TILE, keys] = normed[here : here + TILE]
            weights[j * tiles + tile, TILE:, vals] = raw[here : here + TILE]
        facts_at[j] = normed[2 * rows : 2 * rows + 16].astype(F32)
        extra = normed[2 * rows + 16 : 2 * rows + 32].astype(F32)
        eight = pl.ds(pl.multiple_of(8 * j, 8), 8)
        raw_g[eight, keys] = extra[:8]
        raw_g[eight, vals] = extra[8:]
    pair_g[...] = raw_g[...].astype(BF16)
    if outer:
        even = plane % 2 == 0
        top = (GROUP + 1) * rows
        near_at = pl.multiple_of(jnp.where(even, top, 0), TILE)
        far_at = pl.multiple_of(jnp.where(even, 0, top), TILE)
        for ref, at in ((near, near_at), (far, far_at)):
            pair[pl.ds(at, rows), keys] = ref[0:rows]
            pair[pl.ds(at, rows), vals] = ref[rows : 2 * rows]
    sums[...] = jnp.zeros_like(sums)
    sums_g[...] = jnp.zeros_like(sums_g)
    count_g = pair_g.shape[0]
    row = lax.broadcasted_iota(jnp.int32, (count_g, HEAD_DIM), 0)
    lane = lax.broadcasted_iota(jnp.int32, (count_g, HEAD_DIM), 1)
    span = 4 * TILE
    units = []
    for j in (0, GROUP - 1) if outer else range(1, GROUP - 1):
        facts = facts_at[j]
        live = jnp.sum(jnp.where(row == lane, facts[0:1], 0.0), axis=1, keepdims=True) > 0.0
        for tile in range(tiles):
            start = jnp.max(facts[1 + tile : 2 + tile]).astype(jnp.int32)
            units.append((j * tiles + tile, pl.multiple_of(start * TILE, TILE), live))

    def products(unit):
        weight, at, _ = units[unit]
        both = jnp.concatenate([pair[pl.ds(at, span)], pair_g[...]], axis=0)
        return contract(both, weights[weight], ((1,), (1,)))

    ahead = products(0)
    for unit, (weight, at, live) in enumerate(units):
        product = ahead
        if unit + 1 < len(units):
            ahead = products(unit + 1)
        score = product[:, :TILE] * (FACTOR * LOG2_E)
        dprob = product[:, TILE:]
        score_g = jnp.where(live, score[span:], -jnp.inf)
        score = jnp.concatenate([score[:span], score_g], axis=0)
        largest = jnp.max(score, axis=0, keepdims=True)
        probs = jnp.exp2(score - largest)
        probs = probs * (1.0 / jnp.sum(probs, axis=0, keepdims=True))
        delta = jnp.sum(probs * dprob, axis=0, keepdims=True)
        dscore = (probs * ((dprob - delta) * FACTOR)).astype(BF16)
        grads = contract(
            jnp.concatenate([dscore, probs.astype(BF16)], axis=1), weights[weight], ((1,), (0,))
        )
        sums[pl.ds(at, span)] += grads[:span]
        sums_g[...] += grads[span:]
        both = jnp.concatenate([pair[pl.ds(at, span), keys], pair_g[:, keys]], axis=0)
        grad_query = contract(dscore, both, ((0,), (0,)))
        dq_out[unit * TILE : (unit + 1) * TILE] = grad_query.astype(BF16)
    acc_out[...] = sums[rows : (GROUP + 1) * rows].astype(BF16)
    if not outer:
        g_out[...] = sums_g[...]
    else:
        total_g = (g_in[...] + sums_g[...]).astype(BF16)
        row = lax.broadcasted_iota(jnp.int32, (8, 8 * GROUP), 0)
        col = lax.broadcasted_iota(jnp.int32, (8, 8 * GROUP), 1)
        for e, out in enumerate((g_out, near_out, mid_out, end_out)):
            hot = (col // 8 == row // G_DEV) & (col % 8 == G_DEV * e + row % G_DEV)
            part = contract(hot.astype(F32).astype(BF16), total_g, ((1,), (0,)))
            out[out.shape[0] - 16 :] = jnp.concatenate([part[:, keys], part[:, vals]], axis=0).astype(
                BF16
            )
        for out, at in ((near_out, near_at), (far_out, far_at)):
            out[:rows] = sums[pl.ds(at, rows), keys].astype(BF16)
            out[rows : 2 * rows] = sums[pl.ds(at, rows), vals].astype(BF16)


def attend(place, blocks, halo, inner_g, fars, first, each, after):
    width = blocks[0].shape[1]
    rows = block_rows(blocks)
    wide = 2 * HEAD_DIM
    half = jax.ShapeDtypeStruct((2 * rows, width), BF16)
    few = jax.ShapeDtypeStruct((16, width), BF16)
    near = jax.ShapeDtypeStruct((2 * rows + 16, width), BF16)
    outs = [(half, HEAD_DIM), (jax.ShapeDtypeStruct((GROUP * rows, 2 * width), BF16), wide)]
    if halo:
        outs += [(x, HEAD_DIM) for x in (few, near, half)]
        outs += [(jax.ShapeDtypeStruct((16, each * HEAD_DIM), BF16), HEAD_DIM, first * HEAD_DIM)] * 2
    else:
        outs += [(jax.ShapeDtypeStruct((8 * GROUP, 2 * width), F32), wide)]
    return heads_call(
        functools.partial(attend_kernel, len(halo) > 0, len(blocks)),
        width // HEAD_DIM,
        place,
        [(x, HEAD_DIM) for x in (*blocks, *halo)]
        + [(x, wide) for x in inner_g]
        + [(x, 0) for x in fars],
        outs,
        after,
        [
            pltpu.VMEM(((GROUP + 2) * rows, wide), BF16),
            pltpu.VMEM((GROUP * rows // TILE, 2 * TILE, wide), BF16),
            pltpu.VMEM(((GROUP + 2) * rows, wide), F32),
            pltpu.VMEM((8 * GROUP, wide), F32),
            pltpu.VMEM((8 * GROUP, wide), BF16),
            pltpu.VMEM((8 * GROUP, wide), F32),
            pltpu.VMEM((GROUP, 16, HEAD_DIM), F32),
        ],
        {len(blocks) + 3 + i: 5 + i for i in range(len(fars))},
        name="outer" if halo else "inner",
    )


def settle_kernel(
    head, place_ref, dq_in, acc_in, dq_out, acc_out, own_g, near, far, *refs
):
    *more, o0, o1, o2, o3, token = refs
    me, plane = place_ref[0], place_ref[1]
    token[...] = jnp.zeros((8, HEAD_DIM), F32)
    rows = dq_in.shape[0] // 2
    even = plane % 2 == 0
    inner = (plane == 1) | (plane == 2)
    part = (own_g[...].astype(F32) + near[2 * rows :].astype(F32)).astype(BF16)
    if more and head == 0:
        rest_g = (more[0][...].astype(F32) + more[1][...].astype(F32)).astype(BF16)
    for d, out in enumerate((o0, o1, o2, o3)):
        j = me ^ d
        near_here = j == jnp.where(even, GROUP - 1, 0)
        far_here = (j == jnp.where(even, 0, GROUP - 1)) & inner
        outside = (j == 0) | (j == GROUP - 1)

        @pl.when(outside)
        def _(out=out, j=j):
            out[:rows] = dq_out[pl.ds(pl.multiple_of(jnp.where(j == 0, 0, rows), TILE), rows)]

        @pl.when(~outside)
        def _(out=out, j=j):
            out[:rows] = dq_in[pl.ds(pl.multiple_of(jnp.where(j == 1, 0, rows), TILE), rows)]

        here = pl.ds(pl.multiple_of(j * rows, TILE), rows)
        for i in range(2):
            lanes = slice(i * HEAD_DIM, (i + 1) * HEAD_DIM)
            rest = slice(i * rows, (i + 1) * rows)
            total = acc_in[here, lanes].astype(F32) + acc_out[here, lanes].astype(F32)
            total = total + jnp.where(near_here, near[rest].astype(F32), 0.0)
            total = total + jnp.where(far_here, far[rest].astype(F32), 0.0)
            out[(i + 1) * rows : (i + 2) * rows] = total.astype(BF16)
        out[3 * rows : 3 * rows + 16] = part
        if more and head == 0:
            for h in range(rest_g.shape[1] // HEAD_DIM):
                at = 3 * rows + 16 * (h + 1)
                out[at : at + 16] = rest_g[:, h * HEAD_DIM : (h + 1) * HEAD_DIM]


def settle(place, inner, outer, own_g, near, far, more, after):
    rows, width = inner[0].shape
    rows = rows // 2
    part = (HEAD_DIM, 2 * HEAD_DIM)
    extra = 16 + 16 * (more[0].shape[1] // HEAD_DIM if more else 0)
    home = jax.ShapeDtypeStruct((3 * rows + extra, width), BF16)
    return heads_call(
        settle_kernel,
        width // HEAD_DIM,
        place,
        [*zip(inner, part), *zip(outer, part)]
        + [(x, HEAD_DIM) for x in (own_g, near, far)]
        + [(x, 0) for x in more],
        [(home, HEAD_DIM)] * GROUP + [(jax.ShapeDtypeStruct((8, HEAD_DIM), F32), 0)],
        after,
        name="settle",
    )


def total_kernel(chunks, place_ref, ids_ref, raw_ref, query, key, query_gain, gain_ref, *refs):
    *refs, out, sums = refs
    homes, dot_refs = refs[: GROUP * len(chunks)], refs[GROUP * len(chunks) :]
    rows, width = out.shape[0], sums.shape[1]
    me = place_ref[0]
    device = place_ref[1] * GROUP + me
    total = part_dots(
        sum(chunks[:-1]), me, homes[-GROUP:], query, key, query_gain, gain_ref
    )
    for ref in dot_refs:
        total = total + ref[...]
    few = lax.broadcasted_iota(jnp.int32, (16, HEAD_DIM), 0)
    eight = lax.broadcasted_iota(jnp.int32, (8, HEAD_DIM), 0)
    hot = [few == 8 * i + G_DEV * me + r for i in range(2) for r in range(G_DEV)]
    dot = [jnp.zeros((1, HEAD_DIM), F32) for _ in range(G_DEV)]
    for d in range(GROUP):
        first = 0
        for c, count in enumerate(chunks):
            for h in range(count):
                home = homes[c * GROUP + d]
                last = homes[(len(chunks) - 1) * GROUP + d]
                at = 3 * rows + 16 * (first + h + 1)
                part = home[3 * rows : 3 * rows + 16, h * HEAD_DIM : (h + 1) * HEAD_DIM].astype(F32)
                part = part + last[at : at + 16, :HEAD_DIM].astype(F32)
                found = [jnp.sum(jnp.where(x, part, 0.0), axis=0, keepdims=True) for x in hot]
                at = pl.multiple_of(
                    (me ^ d) * (width // GROUP) + (first + h) * HEAD_DIM, HEAD_DIM
                )
                here = pl.ds(at, HEAD_DIM)
                block = jnp.zeros((8, HEAD_DIM), F32)
                for i, x in enumerate(found):
                    block = jnp.where(eight == i, x, block)
                sums[:, here] = block
                raw = raw_ref[:, here].astype(F32)
                for r in range(G_DEV):
                    dot[r] = dot[r] + found[r] * gain_ref[:, here] * raw[r : r + 1]
            first += count
    row = lax.broadcasted_iota(jnp.int32, (rows, HEAD_DIM), 0)
    lane = lax.broadcasted_iota(jnp.int32, (rows, HEAD_DIM), 1)
    for r in range(G_DEV):
        here = (row == ids_ref[r] - device * rows) & (lane >= HEAD_DIM // 2)
        total = total + jnp.where(here, jnp.sum(dot[r], axis=1, keepdims=True), 0.0)
    out[...] = total


def total_dots(place, ids, raw, query_raw, key_raw, gains, homes, dots, chunks):
    smem = pl.BlockSpec(memory_space=pltpu.SMEM)
    vmem = pl.BlockSpec(memory_space=pltpu.VMEM)
    flat = [x for home in homes for x in home]
    raw_rows = query_raw.shape[0]
    return pl.pallas_call(
        functools.partial(total_kernel, chunks),
        out_shape=[
            jax.ShapeDtypeStruct((raw_rows, HEAD_DIM), F32),
            jax.ShapeDtypeStruct((8, raw.shape[1]), F32),
        ],
        in_specs=[smem, smem] + [vmem] * (5 + len(flat) + len(dots)),
        out_specs=[vmem, vmem],
        compiler_params=params(),
        cost_estimate=cost(1, 1),
        name="total_dots",
    )(place, ids, raw, query_raw, key_raw, *gains, *flat, *dots)


def part_dots(first, me, homes, query, key, query_gain, key_gain):
    rows, width = query.shape
    each = width // HEAD_DIM // GROUP
    totals = [jnp.zeros((rows, HEAD_DIM), F32), jnp.zeros((rows, HEAD_DIM), F32)]
    for d, grads in enumerate(homes):
        for h in range(grads.shape[1] // HEAD_DIM):
            at = ((me ^ d) * each + first + h) * HEAD_DIM
            here = pl.ds(pl.multiple_of(at, HEAD_DIM), HEAD_DIM)
            lanes = slice(h * HEAD_DIM, (h + 1) * HEAD_DIM)
            for i, (raw, gain) in enumerate(((query, query_gain), (key, key_gain))):
                grad = grads[i * rows : (i + 1) * rows, lanes].astype(F32)
                totals[i] += grad * gain[:, here] * raw[:, here].astype(F32)
    sums = [jnp.sum(x, axis=1, keepdims=True) for x in totals]
    return lane_pair(*sums, rows)


def dots_kernel(first, head, place_ref, *refs):
    refs[-1][...] = part_dots(first, place_ref[0], refs[:GROUP], *refs[GROUP:-1])


def dots(place, grads, query_raw, key_raw, gains, first, after):
    return heads_call(
        functools.partial(dots_kernel, first),
        1,
        place,
        [(x, 0) for x in (*grads, query_raw, key_raw, *gains)],
        [(jax.ShapeDtypeStruct((query_raw.shape[0], HEAD_DIM), F32), 0)],
        after,
        name="dots",
    )[0]


def finish_kernel(chunks, place_ref, ids_ref, own_ref, other_ref, dot_ref, dot_other_ref, *refs):
    me = place_ref[0]
    device = place_ref[1] * GROUP + me
    grads = refs[: GROUP * len(chunks)]
    sum_ref, query_ref, key_ref, query_gain, key_gain = refs[GROUP * len(chunks) : -3]
    query_out, key_out, value_out = refs[-3:]
    rows, width = query_ref.shape
    block = query_out.shape[0]
    each = width // GROUP
    start = pl.program_id(0) * block
    now = pl.ds(pl.multiple_of(start, block), block)
    inv = inverses(own_ref[now], other_ref[now])
    total = dot_ref[now] + dot_other_ref[now]
    dot = (total[:, :1], total[:, HEAD_DIM // 2 : HEAD_DIM // 2 + 1])
    coeff = [inv[i] * inv[i] * inv[i] * (dot[i] / D) for i in range(2)]
    row = lax.broadcasted_iota(jnp.int32, (block, HEAD_DIM), 0) + start
    hot = [row == ids_ref[r] - device * rows for r in range(G_DEV)]
    for d in range(GROUP):
        first = 0
        for c, count in enumerate(chunks):
            ref = grads[c * GROUP + d]
            for h in range(count):
                at = pl.multiple_of((me ^ d) * each + (first + h) * HEAD_DIM, HEAD_DIM)
                here = pl.ds(at, HEAD_DIM)
                col = slice(h * HEAD_DIM, (h + 1) * HEAD_DIM)
                grad = [
                    ref[pl.ds(pl.multiple_of(start + i * rows, block), block), col].astype(F32)
                    for i in range(3)
                ]
                for i in (1, 2):
                    for r in range(G_DEV):
                        more = sum_ref[2 * (i - 1) + r : 2 * (i - 1) + r + 1, here]
                        grad[i] = grad[i] + jnp.where(hot[r], more, 0.0)
                for i, (raw, gain, out) in enumerate(
                    ((query_ref, query_gain, query_out), (key_ref, key_gain, key_out))
                ):
                    out[:, here] = (
                        inv[i] * (grad[i] * gain[:, here]) - raw[now, here].astype(F32) * coeff[i]
                    ).astype(BF16)
                value_out[:, here] = grad[2].astype(BF16)
            first += count


def finish(place, ids, own, other, dot, dot_other, sums, grads, query_raw, key_raw, gains, chunks):
    rows, width = query_raw.shape
    smem = pl.BlockSpec(memory_space=pltpu.SMEM)
    vmem = pl.BlockSpec(memory_space=pltpu.VMEM)
    flat = [x for chunk in grads for x in chunk]
    block = pl.BlockSpec((rows // FINISH_STEPS, width), lambda i: (i, 0))
    return pl.pallas_call(
        functools.partial(finish_kernel, chunks),
        out_shape=[jax.ShapeDtypeStruct(query_raw.shape, BF16)] * 3,
        grid=(FINISH_STEPS,),
        in_specs=[smem, smem] + [vmem] * (4 + len(flat) + 5),
        out_specs=[block] * 3,
        compiler_params=params(),
        cost_estimate=cost(1, 1),
        name="finish",
    )(place, ids, own, other, dot, dot_other, *flat, sums, query_raw, key_raw, *gains)


def swap_heads(x):
    return lax.ppermute(x, "head", [(0, 1), (1, 0)])


def plane_body(
    query_raw, key_raw, values, out_grad, query_gain, key_gain, key_tiles, global_ids, readers
):
    device = lax.axis_index("ctx")
    place = jnp.stack([device % GROUP, device // GROUP]).astype(jnp.int32)
    gains = (query_gain[None, :], key_gain[None, :])
    own = squares(query_raw, key_raw)
    other = swap_heads(own)
    arrays = (query_raw, key_raw, values, out_grad)
    mine, raw_rows = global_rows(place, global_ids, own, other, key_raw, values, gains[1])
    parts = [mine] + [swapped(mine, 4 * e) for e in range(1, GROUP)]
    chunks = len(CHUNKS)
    firsts = [sum(CHUNKS[:c]) for c in range(chunks)]
    packed, token = [], ()

    def spread(sent):
        return [sent[0]] + [swapped(sent[d], d) for d in range(1, GROUP)]

    raw = spread(pack_raw(place, values, out_grad, 0, CHUNKS[0]))
    token = (raw_rows,)
    for first, count in zip(firsts, CHUNKS):
        *sent, last = pack(
            place, key_tiles, readers, own, other, arrays, gains, parts if first else (), first,
            count, first > 0, token,
        )
        if first == 0:
            sent = append(place, sent, parts, first, tuple(raw[1:]))
            last = sent[0]
        token = (last,)
        packed.append((raw if first == 0 else []) + spread(sent))
    edge, inner, outer, back, home, dot = ({} for _ in range(6))
    fars = []
    each = query_raw.shape[1] // HEAD_DIM // GROUP

    def begin(c, token):
        near, far, last = edges(place, packed[c], token)
        edge[c] = (swapped(near, 4), swapped_edges(far))
        return (last,)

    def inside(c, token):
        inner[c] = attend(place, packed[c], (), (), (), firsts[c], each, token)
        return (inner[c][2],)

    def outside(c, token):
        results = attend(
            place, packed[c], edge[c], (inner[c][2],), tuple(fars), firsts[c], each, token
        )
        outer[c], own_g, near, far = results[:2], *results[2:5]
        fars[:] = results[5:]
        more = ()
        if c == chunks - 1:
            more = (swapped(fars[0], 8), swapped(fars[1], 12))
        back[c] = (own_g, swapped(near, 4), swapped_edges(far), more)
        return (own_g,)

    def end(c, token):
        *sent, last = settle(place, inner[c][:2], outer[c], *back[c], token)
        home[c] = [sent[0]] + [swapped(sent[d], d) for d in range(1, GROUP)]
        return (last,)

    def score(c, token):
        dot[c] = dots(place, home[c], query_raw, key_raw, gains, firsts[c], token)
        return (dot[c],)

    stages = {"b": begin, "i": inside, "g": outside, "e": end, "s": score}
    for step in " ".join(ORDER).split():
        name, *extra = step.split(":")
        held = tuple(x for e in extra for x in edge[int(e[1])])
        token = stages[name[0]](int(name[1]), token + held)
    homes = [home[c] for c in range(chunks)]
    total, sums = total_dots(
        place, global_ids, raw_rows, query_raw, key_raw, gains, homes, list(dot.values()), CHUNKS
    )
    return tuple(
        finish(
            place, global_ids, own, other, total, swap_heads(total), sums, homes,
            query_raw, key_raw, gains, CHUNKS,
        )
    )


def passed_along(shard, axis, by):
    count = lax.axis_size(axis)
    return lax.ppermute(shard, axis, [(i, (i + by) % count) for i in range(count)])


def normalize(as_float, gain, squares):
    inverse = lax.rsqrt(squares[:, None] / D + EPSILON)
    return (inverse, (as_float * inverse * gain).astype(jnp.bfloat16))


def norm_grad(as_float, inverse, scaled, coeffs):
    return (inverse * scaled - as_float * inverse**3 * (coeffs[:, None] / D)).astype(jnp.bfloat16)


def body(
    query_raw, key_raw, values, out_grad, query_gain, key_gain, key_tiles, global_ids, readers
):
    tokens_here, width_here = query_raw.shape
    heads_here = width_here // HEAD_DIM
    tiles_here = tokens_here // TILE
    factor = HEAD_DIM ** (-0.5)
    device = lax.axis_index("ctx")
    query_rows = query_raw.astype(jnp.float32)
    key_rows = key_raw.astype(jnp.float32)
    query_sq, key_sq = lax.psum(
        (jnp.sum(query_rows * query_rows, axis=1), jnp.sum(key_rows * key_rows, axis=1)), "head"
    )
    query_inv, query_norm = normalize(query_rows, query_gain, query_sq)
    key_inv, key_norm = normalize(key_rows, key_gain, key_sq)
    own_rows = global_ids - device * tokens_here
    own_pair = jnp.stack([key_norm[own_rows], values[own_rows]])
    global_pair = lax.all_gather(own_pair, "ctx", axis=1, tiled=True)
    global_keys = global_pair[0].reshape(-1, heads_here, HEAD_DIM)
    global_vals = global_pair[1].reshape(-1, heads_here, HEAD_DIM)
    live_mask = jnp.repeat(readers[0] > 0, G_DEV)
    key_value = jnp.stack([key_norm, values])
    current = passed_along(key_value, "ctx", -REACH)
    pieces = [current]
    for hop_index in range(2 * REACH):
        current = passed_along(current, "ctx", 1)
        pieces.append(current)
    pieces = pieces[::-1]
    window_pair = jnp.concatenate(pieces, axis=1)
    first_tile = (device - REACH) * tiles_here
    local_tiles = key_tiles - first_tile
    window_rows = (
        local_tiles[:, :, None] * TILE + jnp.arange(TILE, dtype=jnp.int32)[None, None, :]
    ).reshape(tiles_here, -1)
    window_count = window_rows.shape[1]
    window_keys = window_pair[0][window_rows].reshape(
        tiles_here, window_count, heads_here, HEAD_DIM
    )
    window_vals = window_pair[1][window_rows].reshape(
        tiles_here, window_count, heads_here, HEAD_DIM
    )
    query_four = query_norm.reshape(tiles_here, TILE, heads_here, HEAD_DIM)
    grad_four = out_grad.reshape(tiles_here, TILE, heads_here, HEAD_DIM)

    def head_block(head_number):
        query_head = lax.dynamic_index_in_dim(query_four, head_number, 2, keepdims=False)
        grad_head = lax.dynamic_index_in_dim(grad_four, head_number, 2, keepdims=False)
        wkeys = lax.dynamic_index_in_dim(window_keys, head_number, 2, keepdims=False)
        wvals = lax.dynamic_index_in_dim(window_vals, head_number, 2, keepdims=False)
        gkeys = lax.dynamic_index_in_dim(global_keys, head_number, 1, keepdims=False)
        gvals = lax.dynamic_index_in_dim(global_vals, head_number, 1, keepdims=False)
        score_window = (
            jnp.einsum("tqd,tkd->tqk", query_head, wkeys, preferred_element_type=jnp.float32)
            * factor
        )
        score_global = (
            jnp.einsum("tqd,kd->tqk", query_head, gkeys, preferred_element_type=jnp.float32)
            * factor
        )
        score_global = jnp.where(live_mask, score_global, -jnp.inf)
        scores = jnp.concatenate([score_window, score_global], axis=2)
        largest = jnp.max(scores, axis=2, keepdims=True)
        log_total = largest + jnp.log(jnp.sum(jnp.exp(scores - largest), axis=2, keepdims=True))
        probs = jnp.exp(scores - log_total)
        probs_low = probs.astype(jnp.bfloat16)
        attended = jnp.einsum(
            "tqk,tkd->tqd", probs_low[..., :window_count], wvals, preferred_element_type=jnp.float32
        )
        attended = attended + jnp.einsum(
            "tqk,kd->tqd", probs_low[..., window_count:], gvals, preferred_element_type=jnp.float32
        )
        attended = lax.optimization_barrier(attended.astype(jnp.bfloat16))
        delta_rows = jnp.sum(grad_head.astype(jnp.float32) * attended.astype(jnp.float32), axis=2)
        dprob = jnp.concatenate(
            [
                jnp.einsum("tqd,tkd->tqk", grad_head, wvals, preferred_element_type=jnp.float32),
                jnp.einsum("tqd,kd->tqk", grad_head, gvals, preferred_element_type=jnp.float32),
            ],
            axis=2,
        )
        dscore = (probs * (dprob - delta_rows[..., None]) * factor).astype(jnp.bfloat16)
        grad_query = jnp.einsum(
            "tqk,tkd->tqd", dscore[..., :window_count], wkeys, preferred_element_type=jnp.float32
        )
        grad_query = grad_query + jnp.einsum(
            "tqk,kd->tqd", dscore[..., window_count:], gkeys, preferred_element_type=jnp.float32
        )
        window_dk = jnp.einsum(
            "tqk,tqd->tkd",
            dscore[..., :window_count],
            query_head,
            preferred_element_type=jnp.float32,
        )
        window_dv = jnp.einsum(
            "tqk,tqd->tkd",
            probs_low[..., :window_count],
            grad_head,
            preferred_element_type=jnp.float32,
        )
        global_dk = jnp.einsum(
            "tqk,tqd->kd",
            dscore[..., window_count:],
            query_head,
            preferred_element_type=jnp.float32,
        )
        global_dv = jnp.einsum(
            "tqk,tqd->kd",
            probs_low[..., window_count:],
            grad_head,
            preferred_element_type=jnp.float32,
        )
        return (grad_query, window_dk, window_dv, global_dk, global_dv)

    head_results = lax.map(head_block, jnp.arange(heads_here, dtype=jnp.int32))
    grad_query = jnp.moveaxis(head_results[0], 0, 2).reshape(tokens_here, width_here)
    window_dk = jnp.moveaxis(head_results[1], 0, 2).reshape(-1, width_here)
    window_dv = jnp.moveaxis(head_results[2], 0, 2).reshape(-1, width_here)
    global_dk = jnp.moveaxis(head_results[3], 0, 1).reshape(-1, width_here)
    global_dv = jnp.moveaxis(head_results[4], 0, 1).reshape(-1, width_here)
    window_grads = jnp.zeros((2, window_pair.shape[1], width_here), jnp.float32)
    window_grads = window_grads.at[:, window_rows.reshape(-1)].add(
        jnp.stack([window_dk, window_dv])
    )
    spread_grads = window_grads.reshape(2, 2 * REACH + 1, tokens_here, width_here)
    slots = [spread_grads[:, slot_index] for slot_index in range(2 * REACH + 1)]
    carried = slots[2 * REACH]
    for hop_index in range(2 * REACH):
        carried = (
            passed_along(carried.astype(jnp.bfloat16), "ctx", 1).astype(carried.dtype)
            + slots[2 * REACH - 1 - hop_index]
        )
    home_grads = passed_along(carried.astype(jnp.bfloat16), "ctx", -REACH).astype(carried.dtype)
    global_part = lax.psum_scatter(
        jnp.stack([global_dk, global_dv]), "ctx", scatter_dimension=1, tiled=True
    )
    home_grads = home_grads.at[:, own_rows].add(global_part)
    scaled_query = grad_query * query_gain
    scaled_key = home_grads[0] * key_gain
    query_dot, key_dot = lax.psum(
        (jnp.sum(scaled_query * query_rows, axis=1), jnp.sum(scaled_key * key_rows, axis=1)), "head"
    )
    query_grad = norm_grad(query_rows, query_inv, scaled_query, query_dot)
    key_grad = norm_grad(key_rows, key_inv, scaled_key, key_dot)
    return (query_grad, key_grad, home_grads[1].astype(jnp.bfloat16))


def solution(mesh):
    sizes = dict(mesh.shape)
    planes = sizes["ctx"] == GROUP * GROUP and sizes["head"] == 2
    return jax.shard_map(
        plane_body if planes else body,
        mesh=mesh,
        in_specs=(
            P("ctx", "head"),
            P("ctx", "head"),
            P("ctx", "head"),
            P("ctx", "head"),
            P("head"),
            P("head"),
            P("ctx", None),
            P("ctx"),
            P("ctx", None),
        ),
        out_specs=(P("ctx", "head"), P("ctx", "head"), P("ctx", "head")),
        check_vma=False,
    )
```

```python
import functools

import jax
import jax.numpy as jnp
from jax import lax
from jax.experimental import pallas as pl
from jax.experimental.pallas import tpu as pltpu
from jax.sharding import PartitionSpec as P

HEAD_DIM = 128
D = 5120
TILE = 128
REACH = 1
G_DEV = 2
GROUP = 4
CHUNKS = (2, 2, 1)
ORDER = ("b0 i0 g0 b1", "i1 e0 b2 g1", "i2:z2 s0 e1 g2", "e2 s1",)


EPSILON = 1e-06
FACTOR = HEAD_DIM ** (-0.5)
LOG2_E = 1.4426950408889634
FACTS = 32
FINISH_STEPS = 4
F32 = jnp.float32
BF16 = jnp.bfloat16
ANY = pl.BlockSpec(memory_space=pl.ANY)
VMEM_LIMIT = 48 * 1024 * 1024


def swapped(shard, bit):
    count = lax.axis_size("ctx")
    return lax.ppermute(shard, "ctx", [(i, i ^ bit) for i in range(count)])


def swapped_edges(shard):
    count = lax.axis_size("ctx")
    pairs = [(i, i ^ 12) for i in range(count) if i // GROUP % GROUP in (1, 2)]
    return lax.ppermute(shard, "ctx", pairs)


def params():
    return pltpu.CompilerParams(vmem_limit_bytes=VMEM_LIMIT)


def cost(flops, read):
    return pl.CostEstimate(flops=1, bytes_accessed=1, transcendentals=0)


def behind(kernel, inputs, tokens):
    def run(*refs):
        kernel(*refs[:inputs], *refs[inputs + tokens :])

    return run


def heads_call(
    kernel, count, place, inputs, outputs, after=(), scratch=(), aliases={}, name=None
):
    lanes = [(entry[1], entry[2] if len(entry) > 2 else 0) for entry in (*inputs, *outputs)]

    def run(place_ref, *refs):
        refs = refs[: len(inputs)] + refs[len(inputs) + len(after) :]
        for h in range(count):
            views = [
                ref.at[:, at + h * w : at + (h + 1) * w] if w else ref
                for ref, (w, at) in zip(refs, lanes)
            ]
            kernel(h, place_ref, *views, *refs[len(lanes) :])

    vmem = pl.BlockSpec(memory_space=pltpu.VMEM)
    return pl.pallas_call(
        run,
        out_shape=[entry[0] for entry in outputs],
        in_specs=[pl.BlockSpec(memory_space=pltpu.SMEM)]
        + [vmem] * len(inputs)
        + [ANY] * len(after),
        out_specs=[vmem] * len(outputs),
        scratch_shapes=scratch,
        input_output_aliases={1 + i: o for i, o in aliases.items()},
        compiler_params=params(),
        cost_estimate=cost(1, 1),
        name=name,
    )(place, *[x for x, _ in inputs], *after)


def contract(a, b, dims, precision=None):
    return lax.dot_general(
        a, b, (dims, ((), ())), precision=precision, preferred_element_type=F32
    )


def lane_pair(first, second, rows):
    lane = lax.broadcasted_iota(jnp.int32, (rows, HEAD_DIM), 1)
    return jnp.where(lane < HEAD_DIM // 2, first, second)


def squares_kernel(query_ref, key_ref, out_ref):
    rows, width = query_ref.shape
    step = rows // 4
    for at in range(0, rows, step):
        part = []
        for ref in (query_ref, key_ref):
            x = ref[at : at + step].astype(F32)
            part.append(jnp.sum(x * x, axis=1, keepdims=True))
        out_ref[at : at + step] = lane_pair(*part, step)


def squares(query_raw, key_raw):
    rows, width = query_raw.shape
    vmem = pl.BlockSpec(memory_space=pltpu.VMEM)
    return pl.pallas_call(
        squares_kernel,
        out_shape=jax.ShapeDtypeStruct((rows, HEAD_DIM), F32),
        in_specs=[vmem] * 2,
        out_specs=vmem,
        compiler_params=params(),
        cost_estimate=cost(1, 1),
        name="squares",
    )(query_raw, key_raw)


def inverses(own, other):
    both = lax.rsqrt((own + other) / D + EPSILON)
    return both[:, :1], both[:, HEAD_DIM // 2 : HEAD_DIM // 2 + 1]


def rows_kernel(place_ref, ids_ref, own_ref, other_ref, key_ref, value_ref, gain_ref, out, raw):
    rows, width = key_ref.shape
    block = width // GROUP
    device = place_ref[1] * GROUP + place_ref[0]
    row = lax.broadcasted_iota(jnp.int32, (16, width), 0)
    keys, found, vals = [], [], []
    for r in range(G_DEV):
        at = ids_ref[r] - device * rows
        base = pl.multiple_of(at // 16 * 16, 16)
        here = pl.ds(base, 16)
        _, inv = inverses(own_ref[here], other_ref[here])
        hot = row == at - base

        def only(x):
            return jnp.sum(jnp.where(hot, x, 0.0), axis=0, keepdims=True)

        key = key_ref[here].astype(F32)
        keys.append(only(key))
        found.append(only((key * inv * gain_ref[...]).astype(BF16).astype(F32)))
        vals.append(only(value_ref[here].astype(F32)))
    raw[...] = jnp.where(row == 0, keys[0], keys[1]).astype(BF16)
    total = jnp.zeros((16, block), F32)
    row = lax.broadcasted_iota(jnp.int32, (16, block), 0)
    for g in range(GROUP):
        for i, x in enumerate(found + vals):
            total = jnp.where(row == 4 * g + i, x[:, g * block : (g + 1) * block], total)
    out[...] = total.astype(BF16)


def global_rows(place, ids, own, other, key_raw, values, key_gain):
    rows, width = key_raw.shape
    smem = pl.BlockSpec(memory_space=pltpu.SMEM)
    vmem = pl.BlockSpec(memory_space=pltpu.VMEM)
    return pl.pallas_call(
        rows_kernel,
        out_shape=[
            jax.ShapeDtypeStruct((16, width // GROUP), BF16),
            jax.ShapeDtypeStruct((16, width), BF16),
        ],
        in_specs=[smem, smem] + [vmem] * 5,
        out_specs=[vmem] * 2,
        compiler_params=params(),
        cost_estimate=cost(1, 1),
        name="global_rows",
    )(place, ids, own, other, key_raw, values, key_gain)


def add_globals(me, d, first, parts, out):
    parts = jnp.concatenate([ref[...] for ref in parts], axis=0)
    row = lax.broadcasted_iota(jnp.int32, (16, 16 * GROUP), 0)
    col = lax.broadcasted_iota(jnp.int32, (16, 16 * GROUP), 1)
    spot = col % 16 - 4 * (me ^ d)
    hot = (spot >= 0) & (spot < 4)
    hot = hot & (row == 2 * (col // 16) + spot % 2 + 8 * (spot // 2))
    hot = hot.astype(F32).astype(BF16)
    chosen = parts[:, first * HEAD_DIM : first * HEAD_DIM + out.shape[1]]
    out[out.shape[0] - 16 :] = contract(hot, chosen, ((1,), (0,))).astype(BF16)


def append_kernel(first, head, place_ref, *refs):
    for d, out in enumerate(refs[2 * GROUP :]):
        add_globals(place_ref[0], d, first, refs[GROUP : 2 * GROUP], out)


def append(place, sent, parts, first, after):
    return heads_call(
        functools.partial(append_kernel, first),
        1,
        place,
        [(x, 0) for x in (*sent, *parts)],
        [(jax.ShapeDtypeStruct(x.shape, BF16), 0) for x in sent],
        after,
        aliases={d: d for d in range(GROUP)},
        name="append",
    )


def pack_kernel(first, whole, place_ref, tiles_ref, readers_ref, own_ref, other_ref, *refs):
    me, plane = place_ref[0], place_ref[1]
    query_inv, key_inv = inverses(own_ref[...], other_ref[...])
    rows = own_ref.shape[0]
    row = lax.broadcasted_iota(jnp.int32, (16, HEAD_DIM), 0)
    lane = lax.broadcasted_iota(jnp.int32, (16, HEAD_DIM), 1)
    facts = jnp.zeros((16, HEAD_DIM), jnp.int32)
    for tile in range(rows // TILE):
        start = tiles_ref[tile, 0] - (plane * GROUP - 1) * (rows // TILE)
        facts = jnp.where(row == 1 + tile, start, facts)
    for e in range(GROUP):
        for j in range(GROUP):
            live = readers_ref[0, (plane ^ e) * GROUP + j]
            chosen = (row == 0) & (lane // G_DEV == GROUP * j + e)
            facts = jnp.where(chosen, live, facts)
    facts = facts.astype(F32).astype(BF16)
    key_ref, value_ref, query_ref, grad_ref, key_gain, query_gain = refs[:6]
    *outs, token = refs[-GROUP - 1 :]
    token[...] = jnp.zeros((8, HEAD_DIM), F32)
    each = key_ref.shape[1] // HEAD_DIM // GROUP
    for d, out in enumerate(outs):
        top = 2 * rows if whole else 0
        if whole:
            add_globals(me, d, first, refs[6 : 6 + GROUP], out)
        for h in range(out.shape[1] // HEAD_DIM):
            at = pl.multiple_of(((me ^ d) * each + first + h) * HEAD_DIM, HEAD_DIM)
            here = pl.ds(at, HEAD_DIM)
            lanes = slice(h * HEAD_DIM, (h + 1) * HEAD_DIM)
            key = key_ref[:, here].astype(F32)
            query = query_ref[:, here].astype(F32)
            if whole:
                out[0:rows, lanes] = value_ref[:, here]
                out[rows : 2 * rows, lanes] = grad_ref[:, here]
            out[top : top + rows, lanes] = (key * key_inv * key_gain[:, here]).astype(BF16)
            out[top + rows : top + 2 * rows, lanes] = (
                query * query_inv * query_gain[:, here]
            ).astype(BF16)
            out[top + 2 * rows : top + 2 * rows + 16, lanes] = facts


def pack(place, tiles, readers, own, other, arrays, gains, parts, first, count, whole, after):
    query_raw, key_raw, values, out_grad = arrays
    query_gain, key_gain = gains
    rows, width = query_raw.shape
    smem = pl.BlockSpec(memory_space=pltpu.SMEM)
    vmem = pl.BlockSpec(memory_space=pltpu.VMEM)
    out_rows = (4 if whole else 2) * rows + FACTS
    kernel = functools.partial(pack_kernel, first, whole)
    return pl.pallas_call(
        behind(kernel, 11 + len(parts), len(after)),
        out_shape=[jax.ShapeDtypeStruct((out_rows, count * HEAD_DIM), BF16)] * GROUP
        + [jax.ShapeDtypeStruct((8, HEAD_DIM), F32)],
        in_specs=[smem] * 3 + [vmem] * (8 + len(parts)) + [ANY] * len(after),
        out_specs=[vmem] * (GROUP + 1),
        compiler_params=params(),
        cost_estimate=cost(1, 1),
        name="pack",
    )(
        place, tiles, readers, own, other, key_raw, values, query_raw, out_grad,
        key_gain, query_gain, *parts, *after,
    )


def raw_kernel(first, head, place_ref, value_ref, grad_ref, *outs):
    rows, width = value_ref.shape
    for d, out in enumerate(outs):
        wide = out.shape[1]
        at = (place_ref[0] ^ d) * (width // GROUP) + first * HEAD_DIM
        here = pl.ds(pl.multiple_of(at, HEAD_DIM), wide)
        out[:rows] = value_ref[:, here]
        out[rows:] = grad_ref[:, here]


def pack_raw(place, values, out_grad, first, count):
    shape = jax.ShapeDtypeStruct((2 * values.shape[0], count * HEAD_DIM), BF16)
    return heads_call(
        functools.partial(raw_kernel, first),
        1,
        place,
        [(values, 0), (out_grad, 0)],
        [(shape, 0)] * GROUP,
        name="pack_raw",
    )


def halves(refs, rows):
    if len(refs) == 2 * GROUP:
        return list(zip(refs[:GROUP], refs[GROUP:]))
    return [(ref.at[0 : 2 * rows], ref.at[2 * rows : ref.shape[0]]) for ref in refs]


def edges_kernel(head, place_ref, *refs):
    *blocks, near_ref, far_ref, token = refs
    rows = near_ref.shape[0] // 2
    me, plane = place_ref[0], place_ref[1]
    token[...] = jnp.zeros((8, HEAD_DIM), F32)
    even = plane % 2 == 0
    last, first = me ^ (GROUP - 1), me
    for d, block in enumerate(halves(blocks, rows)):

        @pl.when(jnp.where(even, last, first) == d)
        def _(block=block):
            near_ref[:rows] = block[1][:rows]
            near_ref[rows:] = block[0][:rows]

        @pl.when(jnp.where(even, first, last) == d)
        def _(block=block):
            far_ref[:rows] = block[1][:rows]
            far_ref[rows:] = block[0][:rows]


def block_rows(blocks):
    return (sum(x.shape[0] for x in blocks) // GROUP - FACTS) // 4


def edges(place, blocks, after):
    width = blocks[0].shape[1]
    rows = block_rows(blocks)
    half = jax.ShapeDtypeStruct((2 * rows, width), BF16)
    return heads_call(
        edges_kernel,
        1,
        place,
        [(block, 0) for block in blocks],
        [(half, 0), (half, 0), (jax.ShapeDtypeStruct((8, HEAD_DIM), F32), 0)],
        after,
        name="edges",
    )


def attend_kernel(outer, inputs, head, place_ref, *refs):
    blocks, refs = refs[:inputs], refs[inputs:]
    if outer:
        near, far, g_in = refs[:3]
        dq_out, acc_out, g_out, near_out, far_out, mid_out, end_out = refs[-14:-7]
    else:
        dq_out, acc_out, g_out = refs[:3]
    pair, weights, sums, raw_g, pair_g, sums_g, facts_at = refs[-7:]
    me, plane = place_ref[0], place_ref[1]
    rows = block_rows(blocks)
    tiles = rows // TILE
    keys = slice(0, HEAD_DIM)
    vals = slice(HEAD_DIM, 2 * HEAD_DIM)

    if head == 0:
        weights[...] = jnp.zeros_like(weights)

    for d, (raw, normed) in enumerate(halves(blocks, rows)):
        j = me ^ d
        at = pl.multiple_of((j + 1) * rows, TILE)
        pair[pl.ds(at, rows), keys] = normed[0:rows]
        pair[pl.ds(at, rows), vals] = raw[0:rows]
        for tile in range(tiles):
            here = rows + tile * TILE
            weights[j * tiles + tile, :TILE, keys] = normed[here : here + TILE]
            weights[j * tiles + tile, TILE:, vals] = raw[here : here + TILE]
        facts_at[j] = normed[2 * rows : 2 * rows + 16].astype(F32)
        extra = normed[2 * rows + 16 : 2 * rows + 32].astype(F32)
        eight = pl.ds(pl.multiple_of(8 * j, 8), 8)
        raw_g[eight, keys] = extra[:8]
        raw_g[eight, vals] = extra[8:]
    pair_g[...] = raw_g[...].astype(BF16)
    if outer:
        even = plane % 2 == 0
        top = (GROUP + 1) * rows
        near_at = pl.multiple_of(jnp.where(even, top, 0), TILE)
        far_at = pl.multiple_of(jnp.where(even, 0, top), TILE)
        for ref, at in ((near, near_at), (far, far_at)):
            pair[pl.ds(at, rows), keys] = ref[0:rows]
            pair[pl.ds(at, rows), vals] = ref[rows : 2 * rows]
    sums[...] = jnp.zeros_like(sums)
    sums_g[...] = jnp.zeros_like(sums_g)
    count_g = pair_g.shape[0]
    row = lax.broadcasted_iota(jnp.int32, (count_g, HEAD_DIM), 0)
    lane = lax.broadcasted_iota(jnp.int32, (count_g, HEAD_DIM), 1)
    span = 4 * TILE
    units = []
    for j in (0, GROUP - 1) if outer else range(1, GROUP - 1):
        facts = facts_at[j]
        live = jnp.sum(jnp.where(row == lane, facts[0:1], 0.0), axis=1, keepdims=True) > 0.0
        for tile in range(tiles):
            start = jnp.max(facts[1 + tile : 2 + tile]).astype(jnp.int32)
            units.append((j * tiles + tile, pl.multiple_of(start * TILE, TILE), live))

    def products(unit):
        weight, at, _ = units[unit]
        both = jnp.concatenate([pair[pl.ds(at, span)], pair_g[...]], axis=0)
        return contract(both, weights[weight], ((1,), (1,)))

    ahead = products(0)
    for unit, (weight, at, live) in enumerate(units):
        product = ahead
        if unit + 1 < len(units):
            ahead = products(unit + 1)
        score = product[:, :TILE] * (FACTOR * LOG2_E)
        dprob = product[:, TILE:]
        score_g = jnp.where(live, score[span:], -jnp.inf)
        score = jnp.concatenate([score[:span], score_g], axis=0)
        largest = jnp.max(score, axis=0, keepdims=True)
        probs = jnp.exp2(score - largest)
        probs = probs * (1.0 / jnp.sum(probs, axis=0, keepdims=True))
        delta = jnp.sum(probs * dprob, axis=0, keepdims=True)
        dscore = (probs * ((dprob - delta) * FACTOR)).astype(BF16)
        grads = contract(
            jnp.concatenate([dscore, probs.astype(BF16)], axis=1), weights[weight], ((1,), (0,))
        )
        sums[pl.ds(at, span)] += grads[:span]
        sums_g[...] += grads[span:]
        both = jnp.concatenate([pair[pl.ds(at, span), keys], pair_g[:, keys]], axis=0)
        grad_query = contract(dscore, both, ((0,), (0,)))
        dq_out[unit * TILE : (unit + 1) * TILE] = grad_query.astype(BF16)
    acc_out[...] = sums[rows : (GROUP + 1) * rows].astype(BF16)
    if not outer:
        g_out[...] = sums_g[...]
    else:
        total_g = (g_in[...] + sums_g[...]).astype(BF16)
        row = lax.broadcasted_iota(jnp.int32, (8, 8 * GROUP), 0)
        col = lax.broadcasted_iota(jnp.int32, (8, 8 * GROUP), 1)
        for e, out in enumerate((g_out, near_out, mid_out, end_out)):
            hot = (col // 8 == row // G_DEV) & (col % 8 == G_DEV * e + row % G_DEV)
            part = contract(hot.astype(F32).astype(BF16), total_g, ((1,), (0,)))
            out[out.shape[0] - 16 :] = jnp.concatenate([part[:, keys], part[:, vals]], axis=0).astype(
                BF16
            )
        for out, at in ((near_out, near_at), (far_out, far_at)):
            out[:rows] = sums[pl.ds(at, rows), keys].astype(BF16)
            out[rows : 2 * rows] = sums[pl.ds(at, rows), vals].astype(BF16)


def attend(place, blocks, halo, inner_g, fars, first, each, after):
    width = blocks[0].shape[1]
    rows = block_rows(blocks)
    wide = 2 * HEAD_DIM
    half = jax.ShapeDtypeStruct((2 * rows, width), BF16)
    few = jax.ShapeDtypeStruct((16, width), BF16)
    near = jax.ShapeDtypeStruct((2 * rows + 16, width), BF16)
    outs = [(half, HEAD_DIM), (jax.ShapeDtypeStruct((GROUP * rows, 2 * width), BF16), wide)]
    if halo:
        outs += [(x, HEAD_DIM) for x in (few, near, half)]
        outs += [(jax.ShapeDtypeStruct((16, each * HEAD_DIM), BF16), HEAD_DIM, first * HEAD_DIM)] * 2
    else:
        outs += [(jax.ShapeDtypeStruct((8 * GROUP, 2 * width), F32), wide)]
    return heads_call(
        functools.partial(attend_kernel, len(halo) > 0, len(blocks)),
        width // HEAD_DIM,
        place,
        [(x, HEAD_DIM) for x in (*blocks, *halo)]
        + [(x, wide) for x in inner_g]
        + [(x, 0) for x in fars],
        outs,
        after,
        [
            pltpu.VMEM(((GROUP + 2) * rows, wide), BF16),
            pltpu.VMEM((GROUP * rows // TILE, 2 * TILE, wide), BF16),
            pltpu.VMEM(((GROUP + 2) * rows, wide), F32),
            pltpu.VMEM((8 * GROUP, wide), F32),
            pltpu.VMEM((8 * GROUP, wide), BF16),
            pltpu.VMEM((8 * GROUP, wide), F32),
            pltpu.VMEM((GROUP, 16, HEAD_DIM), F32),
        ],
        {len(blocks) + 3 + i: 5 + i for i in range(len(fars))},
        name="outer" if halo else "inner",
    )


def settle_kernel(
    head, place_ref, dq_in, acc_in, dq_out, acc_out, own_g, near, far, *refs
):
    *more, o0, o1, o2, o3, token = refs
    me, plane = place_ref[0], place_ref[1]
    token[...] = jnp.zeros((8, HEAD_DIM), F32)
    rows = dq_in.shape[0] // 2
    even = plane % 2 == 0
    inner = (plane == 1) | (plane == 2)
    part = (own_g[...].astype(F32) + near[2 * rows :].astype(F32)).astype(BF16)
    if more and head == 0:
        rest_g = (more[0][...].astype(F32) + more[1][...].astype(F32)).astype(BF16)
    for d, out in enumerate((o0, o1, o2, o3)):
        j = me ^ d
        near_here = j == jnp.where(even, GROUP - 1, 0)
        far_here = (j == jnp.where(even, 0, GROUP - 1)) & inner
        outside = (j == 0) | (j == GROUP - 1)

        @pl.when(outside)
        def _(out=out, j=j):
            out[:rows] = dq_out[pl.ds(pl.multiple_of(jnp.where(j == 0, 0, rows), TILE), rows)]

        @pl.when(~outside)
        def _(out=out, j=j):
            out[:rows] = dq_in[pl.ds(pl.multiple_of(jnp.where(j == 1, 0, rows), TILE), rows)]

        here = pl.ds(pl.multiple_of(j * rows, TILE), rows)
        for i in range(2):
            lanes = slice(i * HEAD_DIM, (i + 1) * HEAD_DIM)
            rest = slice(i * rows, (i + 1) * rows)
            total = acc_in[here, lanes].astype(F32) + acc_out[here, lanes].astype(F32)
            total = total + jnp.where(near_here, near[rest].astype(F32), 0.0)
            total = total + jnp.where(far_here, far[rest].astype(F32), 0.0)
            out[(i + 1) * rows : (i + 2) * rows] = total.astype(BF16)
        out[3 * rows : 3 * rows + 16] = part
        if more and head == 0:
            row = lax.broadcasted_iota(jnp.int32, (32, 16), 0)
            spot = lax.broadcasted_iota(jnp.int32, (32, 16), 1) - G_DEV * j
            few = jnp.zeros((32, HEAD_DIM), F32)
            for h in range(rest_g.shape[1] // HEAD_DIM):
                hot = (spot >= 0) & (spot % 8 < G_DEV) & (row == 4 * h + spot % 8 + spot // 8 * 2)
                hot = hot.astype(F32).astype(BF16)
                some = rest_g[:, h * HEAD_DIM : (h + 1) * HEAD_DIM]
                few = few + contract(hot, some, ((1,), (0,)))
            out[3 * rows + 16 : 3 * rows + 48] = few.astype(BF16)


def settle(place, inner, outer, own_g, near, far, more, after):
    rows, width = inner[0].shape
    rows = rows // 2
    part = (HEAD_DIM, 2 * HEAD_DIM)
    extra = 48 if more else 16
    home = jax.ShapeDtypeStruct((3 * rows + extra, width), BF16)
    return heads_call(
        settle_kernel,
        width // HEAD_DIM,
        place,
        [*zip(inner, part), *zip(outer, part)]
        + [(x, HEAD_DIM) for x in (own_g, near, far)]
        + [(x, 0) for x in more],
        [(home, HEAD_DIM)] * GROUP + [(jax.ShapeDtypeStruct((8, HEAD_DIM), F32), 0)],
        after,
        name="settle",
    )


def total_kernel(chunks, place_ref, ids_ref, raw_ref, query, key, query_gain, gain_ref, *refs):
    *refs, out, sums = refs
    homes, dot_refs = refs[: GROUP * len(chunks)], refs[GROUP * len(chunks) :]
    rows, width = out.shape[0], sums.shape[1]
    me = place_ref[0]
    device = place_ref[1] * GROUP + me
    total = part_dots(
        sum(chunks[:-1]), me, homes[-GROUP:], query, key, query_gain, gain_ref
    )
    for ref in dot_refs:
        total = total + ref[...]
    few = lax.broadcasted_iota(jnp.int32, (16, HEAD_DIM), 0)
    eight = lax.broadcasted_iota(jnp.int32, (8, HEAD_DIM), 0)
    hot = [few == 8 * i + G_DEV * me + r for i in range(2) for r in range(G_DEV)]
    dot = [jnp.zeros((1, HEAD_DIM), F32) for _ in range(G_DEV)]
    for d in range(GROUP):
        first = 0
        for c, count in enumerate(chunks):
            for h in range(count):
                home = homes[c * GROUP + d]
                last = homes[(len(chunks) - 1) * GROUP + d]
                at = 4 * (first + h)
                part = home[3 * rows : 3 * rows + 16, h * HEAD_DIM : (h + 1) * HEAD_DIM].astype(F32)
                rest = last[3 * rows + 16 : 3 * rows + 48, :HEAD_DIM].astype(F32)
                found = [
                    jnp.sum(jnp.where(x, part, 0.0), axis=0, keepdims=True)
                    + rest[at + i : at + i + 1]
                    for i, x in enumerate(hot)
                ]
                at = pl.multiple_of(
                    (me ^ d) * (width // GROUP) + (first + h) * HEAD_DIM, HEAD_DIM
                )
                here = pl.ds(at, HEAD_DIM)
                block = jnp.zeros((8, HEAD_DIM), F32)
                for i, x in enumerate(found):
                    block = jnp.where(eight == i, x, block)
                sums[:, here] = block
                raw = raw_ref[:, here].astype(F32)
                for r in range(G_DEV):
                    dot[r] = dot[r] + found[r] * gain_ref[:, here] * raw[r : r + 1]
            first += count
    row = lax.broadcasted_iota(jnp.int32, (rows, HEAD_DIM), 0)
    lane = lax.broadcasted_iota(jnp.int32, (rows, HEAD_DIM), 1)
    for r in range(G_DEV):
        here = (row == ids_ref[r] - device * rows) & (lane >= HEAD_DIM // 2)
        total = total + jnp.where(here, jnp.sum(dot[r], axis=1, keepdims=True), 0.0)
    out[...] = total


def total_dots(place, ids, raw, query_raw, key_raw, gains, homes, dots, chunks):
    smem = pl.BlockSpec(memory_space=pltpu.SMEM)
    vmem = pl.BlockSpec(memory_space=pltpu.VMEM)
    flat = [x for home in homes for x in home]
    raw_rows = query_raw.shape[0]
    return pl.pallas_call(
        functools.partial(total_kernel, chunks),
        out_shape=[
            jax.ShapeDtypeStruct((raw_rows, HEAD_DIM), F32),
            jax.ShapeDtypeStruct((8, raw.shape[1]), F32),
        ],
        in_specs=[smem, smem] + [vmem] * (5 + len(flat) + len(dots)),
        out_specs=[vmem, vmem],
        compiler_params=params(),
        cost_estimate=cost(1, 1),
        name="total_dots",
    )(place, ids, raw, query_raw, key_raw, *gains, *flat, *dots)


def part_dots(first, me, homes, query, key, query_gain, key_gain):
    rows, width = query.shape
    each = width // HEAD_DIM // GROUP
    totals = [jnp.zeros((rows, HEAD_DIM), F32), jnp.zeros((rows, HEAD_DIM), F32)]
    for d, grads in enumerate(homes):
        for h in range(grads.shape[1] // HEAD_DIM):
            at = ((me ^ d) * each + first + h) * HEAD_DIM
            here = pl.ds(pl.multiple_of(at, HEAD_DIM), HEAD_DIM)
            lanes = slice(h * HEAD_DIM, (h + 1) * HEAD_DIM)
            for i, (raw, gain) in enumerate(((query, query_gain), (key, key_gain))):
                grad = grads[i * rows : (i + 1) * rows, lanes].astype(F32)
                totals[i] += grad * gain[:, here] * raw[:, here].astype(F32)
    sums = [jnp.sum(x, axis=1, keepdims=True) for x in totals]
    return lane_pair(*sums, rows)


def dots_kernel(first, head, place_ref, *refs):
    refs[-1][...] = part_dots(first, place_ref[0], refs[:GROUP], *refs[GROUP:-1])


def dots(place, grads, query_raw, key_raw, gains, first, after):
    return heads_call(
        functools.partial(dots_kernel, first),
        1,
        place,
        [(x, 0) for x in (*grads, query_raw, key_raw, *gains)],
        [(jax.ShapeDtypeStruct((query_raw.shape[0], HEAD_DIM), F32), 0)],
        after,
        name="dots",
    )[0]


def finish_kernel(chunks, place_ref, ids_ref, own_ref, other_ref, dot_ref, dot_other_ref, *refs):
    me = place_ref[0]
    device = place_ref[1] * GROUP + me
    grads = refs[: GROUP * len(chunks)]
    sum_ref, query_ref, key_ref, query_gain, key_gain = refs[GROUP * len(chunks) : -3]
    query_out, key_out, value_out = refs[-3:]
    rows, width = query_ref.shape
    block = query_out.shape[0]
    each = width // GROUP
    start = pl.program_id(0) * block
    now = pl.ds(pl.multiple_of(start, block), block)
    inv = inverses(own_ref[now], other_ref[now])
    total = dot_ref[now] + dot_other_ref[now]
    dot = (total[:, :1], total[:, HEAD_DIM // 2 : HEAD_DIM // 2 + 1])
    coeff = [inv[i] * inv[i] * inv[i] * (dot[i] / D) for i in range(2)]
    row = lax.broadcasted_iota(jnp.int32, (block, HEAD_DIM), 0) + start
    hot = [row == ids_ref[r] - device * rows for r in range(G_DEV)]
    for d in range(GROUP):
        first = 0
        for c, count in enumerate(chunks):
            ref = grads[c * GROUP + d]
            for h in range(count):
                at = pl.multiple_of((me ^ d) * each + (first + h) * HEAD_DIM, HEAD_DIM)
                here = pl.ds(at, HEAD_DIM)
                col = slice(h * HEAD_DIM, (h + 1) * HEAD_DIM)
                grad = [
                    ref[pl.ds(pl.multiple_of(start + i * rows, block), block), col].astype(F32)
                    for i in range(3)
                ]
                for i in (1, 2):
                    for r in range(G_DEV):
                        more = sum_ref[2 * (i - 1) + r : 2 * (i - 1) + r + 1, here]
                        grad[i] = grad[i] + jnp.where(hot[r], more, 0.0)
                for i, (raw, gain, out) in enumerate(
                    ((query_ref, query_gain, query_out), (key_ref, key_gain, key_out))
                ):
                    out[:, here] = (
                        inv[i] * (grad[i] * gain[:, here]) - raw[now, here].astype(F32) * coeff[i]
                    ).astype(BF16)
                value_out[:, here] = grad[2].astype(BF16)
            first += count


def finish(place, ids, own, other, dot, dot_other, sums, grads, query_raw, key_raw, gains, chunks):
    rows, width = query_raw.shape
    smem = pl.BlockSpec(memory_space=pltpu.SMEM)
    vmem = pl.BlockSpec(memory_space=pltpu.VMEM)
    flat = [x for chunk in grads for x in chunk]
    block = pl.BlockSpec((rows // FINISH_STEPS, width), lambda i: (i, 0))
    return pl.pallas_call(
        functools.partial(finish_kernel, chunks),
        out_shape=[jax.ShapeDtypeStruct(query_raw.shape, BF16)] * 3,
        grid=(FINISH_STEPS,),
        in_specs=[smem, smem] + [vmem] * (4 + len(flat) + 5),
        out_specs=[block] * 3,
        compiler_params=params(),
        cost_estimate=cost(1, 1),
        name="finish",
    )(place, ids, own, other, dot, dot_other, *flat, sums, query_raw, key_raw, *gains)


def swap_heads(x):
    return lax.ppermute(x, "head", [(0, 1), (1, 0)])


def plane_body(
    query_raw, key_raw, values, out_grad, query_gain, key_gain, key_tiles, global_ids, readers
):
    device = lax.axis_index("ctx")
    place = jnp.stack([device % GROUP, device // GROUP]).astype(jnp.int32)
    gains = (query_gain[None, :], key_gain[None, :])
    own = squares(query_raw, key_raw)
    other = swap_heads(own)
    arrays = (query_raw, key_raw, values, out_grad)
    mine, raw_rows = global_rows(place, global_ids, own, other, key_raw, values, gains[1])
    parts = [mine] + [swapped(mine, 4 * e) for e in range(1, GROUP)]
    chunks = len(CHUNKS)
    firsts = [sum(CHUNKS[:c]) for c in range(chunks)]
    packed, token = [], ()

    def spread(sent):
        return [sent[0]] + [swapped(sent[d], d) for d in range(1, GROUP)]

    raw = spread(pack_raw(place, values, out_grad, 0, CHUNKS[0]))
    token = (raw_rows,)
    for first, count in zip(firsts, CHUNKS):
        *sent, last = pack(
            place, key_tiles, readers, own, other, arrays, gains, parts if first else (), first,
            count, first > 0, token,
        )
        if first == 0:
            sent = append(place, sent, parts, first, tuple(raw[1:]))
            last = sent[0]
        token = (last,)
        packed.append((raw if first == 0 else []) + spread(sent))
    edge, inner, outer, back, home, dot = ({} for _ in range(6))
    fars = []
    each = query_raw.shape[1] // HEAD_DIM // GROUP

    def begin(c, token):
        near, far, last = edges(place, packed[c], token)
        edge[c] = (swapped(near, 4), swapped_edges(far))
        return (last,)

    def inside(c, token):
        inner[c] = attend(place, packed[c], (), (), (), firsts[c], each, token)
        return (inner[c][2],)

    def outside(c, token):
        results = attend(
            place, packed[c], edge[c], (inner[c][2],), tuple(fars), firsts[c], each, token
        )
        outer[c], own_g, near, far = results[:2], *results[2:5]
        fars[:] = results[5:]
        more = ()
        if c == chunks - 1:
            more = (swapped(fars[0], 8), swapped(fars[1], 12))
        back[c] = (own_g, swapped(near, 4), swapped_edges(far), more)
        return (own_g,)

    def end(c, token):
        *sent, last = settle(place, inner[c][:2], outer[c], *back[c], token)
        home[c] = [sent[0]] + [swapped(sent[d], d) for d in range(1, GROUP)]
        return (last,)

    def score(c, token):
        dot[c] = dots(place, home[c], query_raw, key_raw, gains, firsts[c], token)
        return (dot[c],)

    stages = {"b": begin, "i": inside, "g": outside, "e": end, "s": score}
    for step in " ".join(ORDER).split():
        name, *extra = step.split(":")
        held = tuple(x for e in extra for x in edge[int(e[1])])
        token = stages[name[0]](int(name[1]), token + held)
    homes = [home[c] for c in range(chunks)]
    total, sums = total_dots(
        place, global_ids, raw_rows, query_raw, key_raw, gains, homes, list(dot.values()), CHUNKS
    )
    return tuple(
        finish(
            place, global_ids, own, other, total, swap_heads(total), sums, homes,
            query_raw, key_raw, gains, CHUNKS,
        )
    )


def passed_along(shard, axis, by):
    count = lax.axis_size(axis)
    return lax.ppermute(shard, axis, [(i, (i + by) % count) for i in range(count)])


def normalize(as_float, gain, squares):
    inverse = lax.rsqrt(squares[:, None] / D + EPSILON)
    return (inverse, (as_float * inverse * gain).astype(jnp.bfloat16))


def norm_grad(as_float, inverse, scaled, coeffs):
    return (inverse * scaled - as_float * inverse**3 * (coeffs[:, None] / D)).astype(jnp.bfloat16)


def body(
    query_raw, key_raw, values, out_grad, query_gain, key_gain, key_tiles, global_ids, readers
):
    tokens_here, width_here = query_raw.shape
    heads_here = width_here // HEAD_DIM
    tiles_here = tokens_here // TILE
    factor = HEAD_DIM ** (-0.5)
    device = lax.axis_index("ctx")
    query_rows = query_raw.astype(jnp.float32)
    key_rows = key_raw.astype(jnp.float32)
    query_sq, key_sq = lax.psum(
        (jnp.sum(query_rows * query_rows, axis=1), jnp.sum(key_rows * key_rows, axis=1)), "head"
    )
    query_inv, query_norm = normalize(query_rows, query_gain, query_sq)
    key_inv, key_norm = normalize(key_rows, key_gain, key_sq)
    own_rows = global_ids - device * tokens_here
    own_pair = jnp.stack([key_norm[own_rows], values[own_rows]])
    global_pair = lax.all_gather(own_pair, "ctx", axis=1, tiled=True)
    global_keys = global_pair[0].reshape(-1, heads_here, HEAD_DIM)
    global_vals = global_pair[1].reshape(-1, heads_here, HEAD_DIM)
    live_mask = jnp.repeat(readers[0] > 0, G_DEV)
    key_value = jnp.stack([key_norm, values])
    current = passed_along(key_value, "ctx", -REACH)
    pieces = [current]
    for hop_index in range(2 * REACH):
        current = passed_along(current, "ctx", 1)
        pieces.append(current)
    pieces = pieces[::-1]
    window_pair = jnp.concatenate(pieces, axis=1)
    first_tile = (device - REACH) * tiles_here
    local_tiles = key_tiles - first_tile
    window_rows = (
        local_tiles[:, :, None] * TILE + jnp.arange(TILE, dtype=jnp.int32)[None, None, :]
    ).reshape(tiles_here, -1)
    window_count = window_rows.shape[1]
    window_keys = window_pair[0][window_rows].reshape(
        tiles_here, window_count, heads_here, HEAD_DIM
    )
    window_vals = window_pair[1][window_rows].reshape(
        tiles_here, window_count, heads_here, HEAD_DIM
    )
    query_four = query_norm.reshape(tiles_here, TILE, heads_here, HEAD_DIM)
    grad_four = out_grad.reshape(tiles_here, TILE, heads_here, HEAD_DIM)

    def head_block(head_number):
        query_head = lax.dynamic_index_in_dim(query_four, head_number, 2, keepdims=False)
        grad_head = lax.dynamic_index_in_dim(grad_four, head_number, 2, keepdims=False)
        wkeys = lax.dynamic_index_in_dim(window_keys, head_number, 2, keepdims=False)
        wvals = lax.dynamic_index_in_dim(window_vals, head_number, 2, keepdims=False)
        gkeys = lax.dynamic_index_in_dim(global_keys, head_number, 1, keepdims=False)
        gvals = lax.dynamic_index_in_dim(global_vals, head_number, 1, keepdims=False)
        score_window = (
            jnp.einsum("tqd,tkd->tqk", query_head, wkeys, preferred_element_type=jnp.float32)
            * factor
        )
        score_global = (
            jnp.einsum("tqd,kd->tqk", query_head, gkeys, preferred_element_type=jnp.float32)
            * factor
        )
        score_global = jnp.where(live_mask, score_global, -jnp.inf)
        scores = jnp.concatenate([score_window, score_global], axis=2)
        largest = jnp.max(scores, axis=2, keepdims=True)
        log_total = largest + jnp.log(jnp.sum(jnp.exp(scores - largest), axis=2, keepdims=True))
        probs = jnp.exp(scores - log_total)
        probs_low = probs.astype(jnp.bfloat16)
        attended = jnp.einsum(
            "tqk,tkd->tqd", probs_low[..., :window_count], wvals, preferred_element_type=jnp.float32
        )
        attended = attended + jnp.einsum(
            "tqk,kd->tqd", probs_low[..., window_count:], gvals, preferred_element_type=jnp.float32
        )
        attended = lax.optimization_barrier(attended.astype(jnp.bfloat16))
        delta_rows = jnp.sum(grad_head.astype(jnp.float32) * attended.astype(jnp.float32), axis=2)
        dprob = jnp.concatenate(
            [
                jnp.einsum("tqd,tkd->tqk", grad_head, wvals, preferred_element_type=jnp.float32),
                jnp.einsum("tqd,kd->tqk", grad_head, gvals, preferred_element_type=jnp.float32),
            ],
            axis=2,
        )
        dscore = (probs * (dprob - delta_rows[..., None]) * factor).astype(jnp.bfloat16)
        grad_query = jnp.einsum(
            "tqk,tkd->tqd", dscore[..., :window_count], wkeys, preferred_element_type=jnp.float32
        )
        grad_query = grad_query + jnp.einsum(
            "tqk,kd->tqd", dscore[..., window_count:], gkeys, preferred_element_type=jnp.float32
        )
        window_dk = jnp.einsum(
            "tqk,tqd->tkd",
            dscore[..., :window_count],
            query_head,
            preferred_element_type=jnp.float32,
        )
        window_dv = jnp.einsum(
            "tqk,tqd->tkd",
            probs_low[..., :window_count],
            grad_head,
            preferred_element_type=jnp.float32,
        )
        global_dk = jnp.einsum(
            "tqk,tqd->kd",
            dscore[..., window_count:],
            query_head,
            preferred_element_type=jnp.float32,
        )
        global_dv = jnp.einsum(
            "tqk,tqd->kd",
            probs_low[..., window_count:],
            grad_head,
            preferred_element_type=jnp.float32,
        )
        return (grad_query, window_dk, window_dv, global_dk, global_dv)

    head_results = lax.map(head_block, jnp.arange(heads_here, dtype=jnp.int32))
    grad_query = jnp.moveaxis(head_results[0], 0, 2).reshape(tokens_here, width_here)
    window_dk = jnp.moveaxis(head_results[1], 0, 2).reshape(-1, width_here)
    window_dv = jnp.moveaxis(head_results[2], 0, 2).reshape(-1, width_here)
    global_dk = jnp.moveaxis(head_results[3], 0, 1).reshape(-1, width_here)
    global_dv = jnp.moveaxis(head_results[4], 0, 1).reshape(-1, width_here)
    window_grads = jnp.zeros((2, window_pair.shape[1], width_here), jnp.float32)
    window_grads = window_grads.at[:, window_rows.reshape(-1)].add(
        jnp.stack([window_dk, window_dv])
    )
    spread_grads = window_grads.reshape(2, 2 * REACH + 1, tokens_here, width_here)
    slots = [spread_grads[:, slot_index] for slot_index in range(2 * REACH + 1)]
    carried = slots[2 * REACH]
    for hop_index in range(2 * REACH):
        carried = (
            passed_along(carried.astype(jnp.bfloat16), "ctx", 1).astype(carried.dtype)
            + slots[2 * REACH - 1 - hop_index]
        )
    home_grads = passed_along(carried.astype(jnp.bfloat16), "ctx", -REACH).astype(carried.dtype)
    global_part = lax.psum_scatter(
        jnp.stack([global_dk, global_dv]), "ctx", scatter_dimension=1, tiled=True
    )
    home_grads = home_grads.at[:, own_rows].add(global_part)
    scaled_query = grad_query * query_gain
    scaled_key = home_grads[0] * key_gain
    query_dot, key_dot = lax.psum(
        (jnp.sum(scaled_query * query_rows, axis=1), jnp.sum(scaled_key * key_rows, axis=1)), "head"
    )
    query_grad = norm_grad(query_rows, query_inv, scaled_query, query_dot)
    key_grad = norm_grad(key_rows, key_inv, scaled_key, key_dot)
    return (query_grad, key_grad, home_grads[1].astype(jnp.bfloat16))


def solution(mesh):
    sizes = dict(mesh.shape)
    planes = sizes["ctx"] == GROUP * GROUP and sizes["head"] == 2
    return jax.shard_map(
        plane_body if planes else body,
        mesh=mesh,
        in_specs=(
            P("ctx", "head"),
            P("ctx", "head"),
            P("ctx", "head"),
            P("ctx", "head"),
            P("head"),
            P("head"),
            P("ctx", None),
            P("ctx"),
            P("ctx", None),
        ),
        out_specs=(P("ctx", "head"), P("ctx", "head"), P("ctx", "head")),
        check_vma=False,
    )
```
